32 devices in a mesh: grp: 4 (over y, x), tile: 8 (over z, core).
Axes of the slice: x: 2, y: 2, z: 4, core: 2. Of those that a mesh axis runs over, the one named last changes fastest.
Arguments:
- tangents: float32 [2, 192, 64, 512], P(None, None, 'tile', 'grp'), may hold values from -60000 to 60000
- reaction_self: float32 [64, 512], P('tile', 'grp'), may hold values from -0.45 to -0.2
- reaction_cross: float32 [64, 512], P('tile', 'grp'), may hold values from -0.3 to -0.02
Outputs:
- corrections: float32 [6144, 192], P(('grp', 'tile'))
- growth: float32 [192], replicated
The draws below stay inside these ranges and needn't reach their ends.
All inputs are finite; a program needn't handle non-finite values.
Results may differ from the reference program's by a relative error of at most 0.0003.
Values sent between devices are 32-bit elements; how exact they have to be, the bound alone decides.
No kernel may reach another device: no remote copies, remote signals or barrier semaphores. Data moves between devices by JAX's collectives and lax.ppermute only.
A program may use at most 64 MiB of HBM per device.

```python
import math
import jax
import jax.numpy as jnp
from jax import lax

K = 192
NYD = 8
NXD = 128
STEPS = 4
TILES = 8
BLOCKS = 32
NY = 64
NX = 512


def draw_tangents(key, part):
    subkeys = jax.random.split(key, 8)
    full_shape = (2, K, NY, NX)
    column_shape = (2, K, 1, NX)
    row_index = jnp.arange(NY, dtype=jnp.float32)[None, None, :, None]
    row_position = jnp.arange(NY, dtype=jnp.float32)[:, None] / NY
    column_position = jnp.arange(NX, dtype=jnp.float32)[None, :] / NX
    wavelength = 32.0 * jnp.exp(jax.random.uniform(subkeys[0], (1, K, 1, 1), jnp.float32) * math.log(4.0))
    phase = jax.random.uniform(subkeys[1], column_shape, jnp.float32, -math.pi, math.pi)
    offset = jax.random.truncated_normal(subkeys[2], -4.0, 4.0, column_shape, jnp.float32)
    amplitude = jax.random.truncated_normal(subkeys[3], -4.0, 4.0, column_shape, jnp.float32)
    noise = 0.25 * jax.random.truncated_normal(subkeys[4], -4.0, 4.0, full_shape, jnp.float32)
    trend_factor = 3.0 ** (row_position + column_position)
    smooth = offset + amplitude * jnp.cos(2.0 * math.pi * row_index / wavelength + phase)
    values = smooth + noise
    field_scale = jnp.array([1.0, 0.03], jnp.float32).reshape(2, 1, 1, 1)
    column_scale = jnp.exp(jax.random.uniform(subkeys[6], (1, K, 1, 1), jnp.float32) * math.log(10.0))
    cell_scale = jnp.exp(jax.random.uniform(subkeys[7], (1, 1, 1, NX), jnp.float32) * math.log(4.0))
    result = values * field_scale * column_scale * cell_scale * trend_factor
    return jnp.clip(result, -60000.0, 60000.0)


def block_levels(rng, dims, cuts, smallest, top_value):
    factor_of, own = 1.0, jax.random.fold_in(rng, 6)
    for dim, shards_of in cuts:
        draws = jnp.exp(jax.random.uniform(jax.random.fold_in(own, dim), (shards_of,), jnp.float32, smallest / len(cuts), top_value / len(cuts)))
        factor_of = factor_of * jnp.repeat(draws, dims[dim] // shards_of).reshape([-1 if axis == dim else 1 for axis in range(len(dims))])
    return factor_of


def setup_inputs(seed: int = 0) -> dict:
    keys = jax.random.split(jax.random.key(seed), 4)
    tangents = draw_tangents(jax.random.fold_in(keys[3], 71), 0)
    reaction_self = jnp.clip(-0.45 + 0.24999999 * jax.random.uniform(keys[1], (NY, NX), jnp.float32) ** block_levels(keys[1], (NY, NX), ((0, 8), (1, 4)), -0.2, 0.2), -0.45, -0.2)
    reaction_cross = jnp.clip(-0.3 + 0.28 * jax.random.uniform(keys[2], (NY, NX), jnp.float32) ** block_levels(keys[2], (NY, NX), ((0, 8), (1, 4)), -0.2, 0.2), -0.3, -0.02)
    return dict(tangents=tangents, reaction_self=reaction_self, reaction_cross=reaction_cross)


diffusion = 0.2
slow_rate = 0.05

def laplace(field):
    padded = jnp.pad(field, ((0, 0), (1, 1), (1, 1)), mode='edge')
    return padded[:, :-2, 1:-1] + padded[:, 2:, 1:-1] + padded[:, 1:-1, :-2] + padded[:, 1:-1, 2:] - 4.0 * field

def reference(tangents, reaction_self, reaction_cross):
    block_width = math.gcd(K, 32)
    block_count = K // block_width

    def evolve_block(column_block):
        start = column_block * block_width
        fast_field = lax.dynamic_slice_in_dim(tangents[0], start, block_width, 0)
        slow_field = lax.dynamic_slice_in_dim(tangents[1], start, block_width, 0)
        for repeat in range(STEPS):
            laplacian = laplace(fast_field)
            new_fast = fast_field + diffusion * laplacian + reaction_self * fast_field + reaction_cross * slow_field
            slow_field = slow_field + slow_rate * (fast_field - slow_field)
            fast_field = new_fast
        return jnp.stack([fast_field, slow_field])
    evolved = lax.map(evolve_block, jnp.arange(block_count, dtype=jnp.int32))

    def local_gram(block_index):
        group_index = block_index // TILES
        tile_index = block_index % TILES
        anchor = jnp.zeros((), jnp.int32)
        piece = lax.dynamic_slice(evolved, (anchor, anchor, anchor, (tile_index * NYD).astype(jnp.int32), (group_index * NXD).astype(jnp.int32)), (block_count, 2, block_width, NYD, NXD))
        piece = jnp.transpose(piece, (1, 0, 2, 3, 4)).reshape(2, K, NYD, NXD)
        return jnp.einsum('fkyx,fjyx->kj', piece, piece, precision=lax.Precision.HIGHEST)
    grams = lax.map(local_gram, jnp.arange(BLOCKS, dtype=jnp.int32))
    gram = lax.optimization_barrier(jnp.sum(grams, axis=0))
    factor = jnp.linalg.cholesky(gram)
    local_factors = jnp.linalg.cholesky(grams)

    def solve_block(local_factor):
        return jax.scipy.linalg.solve_triangular(factor, local_factor, lower=True)
    solved = lax.map(solve_block, local_factors)
    corrections = math.sqrt(BLOCKS) * jnp.transpose(solved, (0, 2, 1)).reshape(BLOCKS * K, K)
    growth = jnp.log(jnp.diagonal(factor))
    return (corrections, growth)
```

```python
import functools
import math

import jax
import jax.numpy as jnp
from jax import lax
from jax.experimental import pallas as pl
from jax.experimental.pallas import tpu as pltpu
from jax.sharding import PartitionSpec as P


STEPS = 4


diffusion = 0.2
slow_rate = 0.05


def padded(cells, sides, width):
    for axis, dim in sides:
        count = lax.axis_size(axis)
        ends = count - 1
        head = lax.slice_in_dim(cells, 0, width, axis=dim)
        tail = lax.slice_in_dim(cells, cells.shape[dim] - width, cells.shape[dim], axis=dim)
        cells = jnp.concatenate(
            [
                lax.ppermute(tail, axis, [(i, (i + 1) % count) for i in range(ends)]),
                cells,
                lax.ppermute(head, axis, [((i + 1) % count, i) for i in range(ends)]),
            ],
            axis=dim,
        )
    return cells


def fix_ghosts(field, margin):
    row_count = field.shape[1]
    col_count = field.shape[2]
    rows = jnp.arange(row_count, dtype=jnp.int32)[:, None]
    cols = jnp.arange(col_count, dtype=jnp.int32)[None, :]
    top_edge = lax.axis_index("tile") == 0
    bottom_edge = lax.axis_index("tile") == lax.axis_size("tile") - 1
    left_edge = lax.axis_index("grp") == 0
    right_edge = lax.axis_index("grp") == lax.axis_size("grp") - 1
    field = jnp.where(top_edge & (rows < margin), field[:, margin : margin + 1, :], field)
    field = jnp.where(
        bottom_edge & (rows >= row_count - margin),
        field[:, row_count - margin - 1 : row_count - margin, :],
        field,
    )
    field = jnp.where(left_edge & (cols < margin), field[:, :, margin : margin + 1], field)
    field = jnp.where(
        right_edge & (cols >= col_count - margin),
        field[:, :, col_count - margin - 1 : col_count - margin],
        field,
    )
    return field


SIDE = 64
LANES = 128
SUB = 8
HI = lax.Precision.HIGHEST

def dot_nn(a, b):
    return lax.dot_general(a, b, (((1,), (0,)), ((), ())), precision=HI, preferred_element_type=jnp.float32)
def dot_tn(a, b):
    return lax.dot_general(a, b, (((0,), (0,)), ((), ())), precision=HI, preferred_element_type=jnp.float32)
def dot_nt(a, b):
    return lax.dot_general(a, b, (((1,), (1,)), ((), ())), precision=HI, preferred_element_type=jnp.float32)

def block_pairs(n):
    return [(i, j) for i in range(n) for j in range(i, n)]

def pack_blocks(gram):
    n = gram.shape[0] // SIDE
    blocks = [gram[i*SIDE:(i+1)*SIDE, j*SIDE:(j+1)*SIDE] for i, j in block_pairs(n)]
    if len(blocks) % 2: blocks.append(jnp.zeros_like(blocks[0]))
    return jnp.concatenate([jnp.concatenate(blocks[i:i+2], axis=1) for i in range(0, len(blocks), 2)], axis=0)

def unpack_blocks(ref, n):
    out = {}
    for index, key in enumerate(block_pairs(n)):
        row, half = divmod(index, 2)
        out[key] = ref[row*SIDE:(row+1)*SIDE, half*SIDE:(half+1)*SIDE]
    return out

def spread_lane(x, lane):
    return jnp.broadcast_to(x[:, lane:lane+1], (x.shape[0], LANES))
def spread_row(x, row):
    return jnp.broadcast_to(x[row:row+1, :], (SUB, x.shape[1]))

def factor_blocks(blocks):
    groups = SIDE // SUB
    eye = (lax.broadcasted_iota(jnp.int32, (SIDE, SIDE), 0) == lax.broadcasted_iota(jnp.int32, (SIDE, SIDE), 1)).astype(jnp.float32)
    sub = lax.broadcasted_iota(jnp.int32, (SUB, LANES), 0)
    states = []
    for d in blocks:
        whole = jnp.concatenate([d, eye], axis=1)
        states.append([whole[g*SUB:(g+1)*SUB] for g in range(groups)])
    done = [[] for _ in blocks]
    for p in range(groups):
        for s, v in enumerate(states):
            cols = {}
            for g in range(p, groups):
                for c in range(SUB):
                    cols[g, c] = spread_lane(v[g], p*SUB + c)
            rows = [spread_row(v[p], c) for c in range(SUB)]
            pivots = {(a, c): spread_row(cols[p, c], a) for c in range(SUB) for a in range(c, SUB)}
            mult = {}
            scale = []
            for c in range(SUB):
                inv = 1.0 / pivots[c, c]
                scale.append(lax.rsqrt(pivots[c, c]))
                for a in range(c + 1, SUB):
                    mult[a, c] = pivots[a, c] * inv
                    rows[a] = rows[a] - mult[a, c] * rows[c]
                    for b in range(c + 1, a + 1):
                        pivots[a, b] = pivots[a, b] - mult[a, c] * pivots[b, c]
            scaled = [rows[c] * scale[c] for c in range(SUB)]
            panel = scaled[0]
            for c in range(1, SUB):
                panel = jnp.where(sub == c, scaled[c], panel)
            done[s].append(panel)
            for g in range(p + 1, groups):
                for c in range(SUB):
                    for a in range(c + 1, SUB):
                        cols[g, a] = cols[g, a] - mult[a, c] * cols[g, c]
                    v[g] = v[g] - (cols[g, c] * scale[c]) * scaled[c]
    out = []
    for panels in done:
        whole = jnp.concatenate(panels, axis=0)
        out.append((whole[:, :SIDE], whole[:, SIDE:]))
    return out

def factor_kernel(n, weight, tot_ref, loc_ref, out_ref, growth_ref):
    total = unpack_blocks(tot_ref, n)
    local = unpack_blocks(loc_ref, n)
    keep = (lax.broadcasted_iota(jnp.int32, (SIDE, SIDE), 0) <= lax.broadcasted_iota(jnp.int32, (SIDE, SIDE), 1))
    diag = (lax.broadcasted_iota(jnp.int32, (SIDE, SIDE), 0) == lax.broadcasted_iota(jnp.int32, (SIDE, SIDE), 1))
    inverse = {}
    answer = {}
    for k in range(n):
        (r_t, i_t), (r_l, i_l) = factor_blocks([total[k, k], local[k, k]])
        inverse[k] = i_t
        local[k, k] = jnp.where(keep, r_l, 0.0)
        growth_ref[0, k*SIDE:(k+1)*SIDE] = jnp.log(jnp.sum(jnp.where(diag, r_t, 0.0), axis=0))
        for grams, inv in ((total, i_t), (local, i_l)):
            if k + 1 < n:
                row = dot_nn(inv, jnp.concatenate([grams[k, j] for j in range(k + 1, n)], axis=1))
                for j in range(k + 1, n):
                    grams[k, j] = row[:, (j-k-1)*SIDE:(j-k)*SIDE]
                for i in range(k + 1, n):
                    rest = dot_tn(grams[k, i], row[:, (i-k-1)*SIDE:])
                    for j in range(i, n):
                        grams[i, j] = grams[i, j] - rest[:, (j-i)*SIDE:(j-i+1)*SIDE]
    for j in range(n):
        for i in range(j + 1):
            rest = local[i, j]
            for m in range(i, j):
                rest = rest - dot_nn(answer[i, m], total[m, j])
            answer[i, j] = dot_nt(rest, inverse[j])
            out_ref[i*SIDE:(i+1)*SIDE, j*SIDE:(j+1)*SIDE] = weight * answer[i, j]
        for i in range(j + 1, n):
            out_ref[i*SIDE:(i+1)*SIDE, j*SIDE:(j+1)*SIDE] = jnp.zeros((SIDE, SIDE), jnp.float32)

def factor_call(total, local, k, weight):
    vm = pl.BlockSpec(memory_space=pltpu.VMEM)
    out, growth = pl.pallas_call(
        functools.partial(factor_kernel, k // SIDE, weight),
        out_shape=(jax.ShapeDtypeStruct((k, k), jnp.float32), jax.ShapeDtypeStruct((1, k), jnp.float32)),
        in_specs=[vm, vm], out_specs=(vm, vm), name="factor",
    )(total, local)
    return out, growth[0]


def exchange(cells, axis, bit):
    count = lax.axis_size(axis)
    return lax.ppermute(cells, axis, [(i, i ^ bit) for i in range(count)])


def sum_blocks(packed):
    half = packed.shape[0] // 2
    odd = lax.axis_index("tile") % 2 == 1
    low, high = packed[:half], packed[half:]
    part = jnp.where(odd, high, low) + exchange(jnp.where(odd, low, high), "tile", 1)
    for axis, first in (("grp", 1), ("tile", 2)):
        bit = first
        while bit < lax.axis_size(axis):
            part = part + exchange(part, axis, bit)
            bit *= 2
    other = exchange(part, "tile", 1)
    return jnp.concatenate([jnp.where(odd, other, part), jnp.where(odd, part, other)], axis=0)


def per_device(tangents, reaction_self, reaction_cross):
    fast_field = tangents[0]
    slow_field = tangents[1]
    coeffs = padded(jnp.stack([reaction_self, reaction_cross]), (("grp", 2), ("tile", 1)), 2)
    for pair in range(STEPS // 2):
        extended = padded(jnp.stack([fast_field, slow_field]), (("grp", 3), ("tile", 2)), 2)
        fast_ext = extended[0]
        slow_ext = extended[1]
        for substep in range(2):
            margin = 2 - substep
            fast_ext = fix_ghosts(fast_ext, margin)
            inner = fast_ext[:, 1:-1, 1:-1]
            slow_inner = slow_ext[:, 1:-1, 1:-1]
            laplacian = (
                fast_ext[:, :-2, 1:-1]
                + fast_ext[:, 2:, 1:-1]
                + fast_ext[:, 1:-1, :-2]
                + fast_ext[:, 1:-1, 2:]
                - 4.0 * inner
            )
            low = substep + 1
            high_rows = coeffs.shape[1] - substep - 1
            high_cols = coeffs.shape[2] - substep - 1
            self_inner = coeffs[0, low:high_rows, low:high_cols]
            cross_inner = coeffs[1, low:high_rows, low:high_cols]
            new_fast = inner + diffusion * laplacian + self_inner * inner + cross_inner * slow_inner
            slow_ext = slow_inner + slow_rate * (inner - slow_inner)
            fast_ext = new_fast
        fast_field = fast_ext
        slow_field = slow_ext
    evolved = jnp.stack([fast_field, slow_field])
    local_gram = jnp.einsum("fkyx,fjyx->kj", evolved, evolved, precision=lax.Precision.HIGHEST)
    packed = pack_blocks(local_gram)
    block_total = lax.axis_size("grp") * lax.axis_size("tile")
    corrections, growth = factor_call(sum_blocks(packed), packed, local_gram.shape[0], math.sqrt(block_total))
    return (corrections, growth)


def solution(mesh):
    in_specs = (P(None, None, "tile", "grp"), P("tile", "grp"), P("tile", "grp"))
    out_specs = (P(("grp", "tile"), None), P())
    return jax.shard_map(
        per_device, mesh=mesh, in_specs=in_specs, out_specs=out_specs, check_vma=False
    )
```

```python
import functools
import math

import jax
import jax.numpy as jnp
from jax import lax
from jax.experimental import pallas as pl
from jax.experimental.pallas import tpu as pltpu
from jax.sharding import PartitionSpec as P


STEPS = 4
diffusion = 0.2
slow_rate = 0.05
SIDE = 64
LANES = 128
SUB = 8
HI = lax.Precision.HIGHEST

def dot_nn(a, b):
    return lax.dot_general(a, b, (((1,), (0,)), ((), ())), precision=HI, preferred_element_type=jnp.float32)
def dot_tn(a, b):
    return lax.dot_general(a, b, (((0,), (0,)), ((), ())), precision=HI, preferred_element_type=jnp.float32)
def dot_nt(a, b):
    return lax.dot_general(a, b, (((1,), (1,)), ((), ())), precision=HI, preferred_element_type=jnp.float32)

def block_pairs(n):
    return [(i, j) for i in range(n) for j in range(i, n)]

def unpack_blocks(ref, n):
    out = {}
    for index, key in enumerate(block_pairs(n)):
        row, half = divmod(index, 2)
        out[key] = ref[row*SIDE:(row+1)*SIDE, half*SIDE:(half+1)*SIDE]
    return out

def spread_lane(x, lane):
    return jnp.broadcast_to(x[:, lane:lane+1], (x.shape[0], LANES))
def spread_row(x, row):
    return jnp.broadcast_to(x[row:row+1, :], (SUB, x.shape[1]))

def factor_blocks(blocks):
    groups = SIDE // SUB
    eye = (lax.broadcasted_iota(jnp.int32, (SIDE, SIDE), 0) == lax.broadcasted_iota(jnp.int32, (SIDE, SIDE), 1)).astype(jnp.float32)
    sub = lax.broadcasted_iota(jnp.int32, (SUB, LANES), 0)
    states = []
    for d in blocks:
        whole = jnp.concatenate([d, eye], axis=1)
        states.append([whole[g*SUB:(g+1)*SUB] for g in range(groups)])
    done = [[] for _ in blocks]
    for p in range(groups):
        for s, v in enumerate(states):
            cols = {}
            for g in range(p, groups):
                for c in range(SUB):
                    cols[g, c] = spread_lane(v[g], p*SUB + c)
            rows = [spread_row(v[p], c) for c in range(SUB)]
            pivots = {(a, c): spread_row(cols[p, c], a) for c in range(SUB) for a in range(c, SUB)}
            mult = {}
            scale = []
            for c in range(SUB):
                inv = 1.0 / pivots[c, c]
                scale.append(lax.rsqrt(pivots[c, c]))
                for a in range(c + 1, SUB):
                    mult[a, c] = pivots[a, c] * inv
                    rows[a] = rows[a] - mult[a, c] * rows[c]
                    for b in range(c + 1, a + 1):
                        pivots[a, b] = pivots[a, b] - mult[a, c] * pivots[b, c]
            scaled = [rows[c] * scale[c] for c in range(SUB)]
            panel = scaled[0]
            for c in range(1, SUB):
                panel = jnp.where(sub == c, scaled[c], panel)
            done[s].append(panel)
            for g in range(p + 1, groups):
                for c in range(SUB):
                    for a in range(c + 1, SUB):
                        cols[g, a] = cols[g, a] - mult[a, c] * cols[g, c]
                    v[g] = v[g] - (cols[g, c] * scale[c]) * scaled[c]
    out = []
    for panels in done:
        whole = jnp.concatenate(panels, axis=0)
        out.append((whole[:, :SIDE], whole[:, SIDE:]))
    return out

def factor_kernel(n, weight, tot_ref, loc_ref, out_ref, growth_ref):
    total = unpack_blocks(tot_ref, n)
    local = unpack_blocks(loc_ref, n)
    keep = (lax.broadcasted_iota(jnp.int32, (SIDE, SIDE), 0) <= lax.broadcasted_iota(jnp.int32, (SIDE, SIDE), 1))
    diag = (lax.broadcasted_iota(jnp.int32, (SIDE, SIDE), 0) == lax.broadcasted_iota(jnp.int32, (SIDE, SIDE), 1))
    inverse = {}
    answer = {}
    for k in range(n):
        (r_t, i_t), (r_l, i_l) = factor_blocks([total[k, k], local[k, k]])
        inverse[k] = i_t
        local[k, k] = jnp.where(keep, r_l, 0.0)
        growth_ref[0, k*SIDE:(k+1)*SIDE] = jnp.log(jnp.sum(jnp.where(diag, r_t, 0.0), axis=0))
        for grams, inv in ((total, i_t), (local, i_l)):
            if k + 1 < n:
                row = dot_nn(inv, jnp.concatenate([grams[k, j] for j in range(k + 1, n)], axis=1))
                for j in range(k + 1, n):
                    grams[k, j] = row[:, (j-k-1)*SIDE:(j-k)*SIDE]
                for i in range(k + 1, n):
                    rest = dot_tn(grams[k, i], row[:, (i-k-1)*SIDE:])
                    for j in range(i, n):
                        grams[i, j] = grams[i, j] - rest[:, (j-i)*SIDE:(j-i+1)*SIDE]
    for j in range(n):
        for i in range(j + 1):
            rest = local[i, j]
            for m in range(i, j):
                rest = rest - dot_nn(answer[i, m], total[m, j])
            answer[i, j] = dot_nt(rest, inverse[j])
            out_ref[i*SIDE:(i+1)*SIDE, j*SIDE:(j+1)*SIDE] = weight * answer[i, j]
        for i in range(j + 1, n):
            out_ref[i*SIDE:(i+1)*SIDE, j*SIDE:(j+1)*SIDE] = jnp.zeros((SIDE, SIDE), jnp.float32)

def factor_call(total, local, k, weight):
    vm = pl.BlockSpec(memory_space=pltpu.VMEM)
    out, growth = pl.pallas_call(
        functools.partial(factor_kernel, k // SIDE, weight),
        out_shape=(jax.ShapeDtypeStruct((k, k), jnp.float32), jax.ShapeDtypeStruct((1, k), jnp.float32)),
        in_specs=[vm, vm], out_specs=(vm, vm), name="factor",
    )(total, local)
    return out, growth[0]


def pick(flag, first, second):
    return jnp.where(flag, first, second)


def roll(x, shift):
    return pltpu.roll(x, shift % LANES, 1)


def lane_index():
    return lax.broadcasted_iota(jnp.int32, (SUB, LANES), 1)


def group(g):
    return pl.ds(pl.multiple_of(g * SUB, SUB), SUB)


def own_rows(tangents, g):
    return [[tangents[f, pl.ds(g * SUB * SUB + r, SUB, stride=SUB), :] for r in range(SUB)] for f in range(2)]


def own_coeffs(coeff_self, coeff_cross):
    return [[spread_row(ref[...], r) for r in range(SUB)] for ref in (coeff_self, coeff_cross)]


def edge_columns(slots):
    cell = lane_index() // SUB
    cells = LANES // SUB
    last, first = None, None
    for s, row in slots.items():
        turned = roll(row, (s + 1) * SUB)
        last = turned if last is None else jnp.where(cell == s, turned, last)
        first = turned if first is None else jnp.where(cell == (s + 1) % cells, turned, first)
    return last, roll(first, -SUB)


def pack_kernel(fields, tangents, coeff_self, coeff_cross, near, far, edges):
    odd = lax.axis_index("tile") % 2 == 1
    inner = lane_index() % SUB < STEPS

    def send(g, rows):
        for f in range(2):
            count = STEPS - f
            for j in range(count):
                top, bottom = rows[f][j], rows[f][SUB - count + j]
                near[f * STEPS + j, group(g), :] = pick(odd, top, bottom)
                far[f * STEPS + j, group(g), :] = pick(odd, bottom, top)
        last, first = edge_columns({f * SUB + r: rows[f][r] for f in range(2) for r in range(SUB)})
        edges[group(g), :] = jnp.where(inner, first, last)

    @pl.loop(0, fields // SUB)
    def _(g):
        send(g, own_rows(tangents, g))

    send(fields // SUB, own_coeffs(coeff_self, coeff_cross))


def column_kernel(edges, near, far, fast_edges, slow_edges, near_out, far_out):
    tile, tiles = lax.axis_index("tile"), lax.axis_size("tile")
    odd = tile % 2 == 1
    grp_odd = lax.axis_index("grp") % 2 == 1
    lane = lane_index()
    cell, low = lane // SUB, lane < LANES // 2
    inner = lane % SUB < STEPS

    @pl.loop(0, edges.shape[0] // SUB)
    def _(g):
        own, one, two = edges[group(g), :], near[group(g), :], far[group(g), :]
        flipped = roll(own, -7 * SUB)
        for s in range(1, SUB):
            flipped = jnp.where(cell % SUB == s, roll(own, (2 * s - 7) * SUB), flipped)
        above = pick(tile == 0, flipped, pick(odd, one, two))
        below = pick(tile == tiles - 1, flipped, pick(odd, two, one))
        outer = jnp.where(cell % SUB < STEPS, below, above)
        fast = jnp.where(low, own, roll(outer, LANES // 2))
        slow = jnp.where(low, roll(own, LANES // 2), outer)
        fast_edges[group(g), :] = fast
        slow_edges[group(g), :] = slow
        to_left = jnp.where(inner, fast, roll(slow, STEPS))
        to_right = jnp.where(inner, roll(fast, -STEPS), slow)
        near_out[group(g), :] = pick(grp_odd, to_left, to_right)
        far_out[group(g), :] = pick(grp_odd, to_right, to_left)


def extended_rows(own, near, far, g):
    tile, tiles = lax.axis_index("tile"), lax.axis_size("tile")
    odd, at_top, at_bottom = tile % 2 == 1, tile == 0, tile == tiles - 1
    out = []
    for f in range(2):
        count = STEPS - f
        rows = dict(enumerate(own[f]))
        for j in range(count):
            one, two = near[f * STEPS + j, group(g), :], far[f * STEPS + j, group(g), :]
            rows[j - count] = pick(at_top, own[f][count - 1 - j], pick(odd, one, two))
            rows[SUB + j] = pick(at_bottom, own[f][SUB - 1 - j], pick(odd, two, one))
        out.append(rows)
    return out


def strip_neighbours(last, first, halo):
    c = lane_index() % SUB
    end, begin = c == SUB - 1, c == 0
    out = []
    for x, after, before in (
        (last, roll(halo, 7), None),
        (first, None, roll(halo, -7)),
        (halo, roll(first, 7), roll(last, -7)),
    ):
        right, left = roll(x, -1), roll(x, 1)
        if after is not None:
            right = jnp.where(end, after, right)
        if before is not None:
            left = jnp.where(begin, before, left)
        out.append(roll(x, SUB) + roll(x, -SUB) + right + left)
    return out


def advance(fast, slow, around, gain, cross):
    return gain * fast + diffusion * around + cross * slow


def relax(fast, slow):
    return (1.0 - slow_rate) * slow + slow_rate * fast


def evolve_kernel(
    fields, tangents, coeff_self, coeff_cross, near, far, fast_edges, slow_edges, near_cols, far_cols,
    gram, halo, row_coeffs, strip_coeffs, cells,
):
    grp, grps = lax.axis_index("grp"), lax.axis_size("grp")
    grp_odd = grp % 2 == 1
    lane = lane_index()
    c = lane % SUB
    inner = c < STEPS
    groups = fields // SUB

    @pl.loop(0, groups + 1)
    def _(g):
        one, two = near_cols[group(g), :], far_cols[group(g), :]
        left, right = pick(grp_odd, one, two), pick(grp_odd, two, one)
        halo[0, group(g), :] = jnp.where(inner, right, roll(left, STEPS))
        halo[1, group(g), :] = jnp.where(inner, roll(right, -STEPS), left)

    @pl.when((grp == 0) | (grp == grps - 1))
    def _():
        outside = (inner & (grp == grps - 1)) | (~inner & (grp == 0))

        @pl.loop(0, groups + 1)
        def _(g):
            for f, ref in enumerate((fast_edges, slow_edges)):
                own = ref[group(g), :]
                mirrored = roll(own, -7)
                for s in range(1, SUB):
                    mirrored = jnp.where(c == s, roll(own, 2 * s - 7), mirrored)
                halo[f, group(g), :] = jnp.where(outside, mirrored, halo[f, group(g), :])

    def strips(rows, f, g):
        slots = {r % (2 * SUB): row for r, row in rows.items()}
        last, first = edge_columns(slots)
        return [last, first, halo[f, group(g), :]]

    coeff_rows = extended_rows(own_coeffs(coeff_self, coeff_cross), near, far, groups)
    for f in range(2):
        base = (1.0 - 4.0 * diffusion) * (1 - f)
        for r in range(1 - STEPS, SUB + STEPS - 1):
            row_coeffs[f, r + STEPS - 1, :, :] = coeff_rows[f][r] + base
        for part, strip in enumerate(strips(coeff_rows[f], f, groups)):
            strip_coeffs[f, part, :, :] = strip + base

    @pl.loop(0, groups)
    def _(g):
        fast, slow = extended_rows(own_rows(tangents, g), near, far, g)
        strip_fast, strip_slow = strips(fast, 0, g), strips(slow, 1, g)
        for step in range(1, STEPS + 1):
            margin = STEPS - step
            new_fast = {}
            for r in range(-margin, SUB + margin):
                around = fast[r - 1] + fast[r + 1] + roll(fast[r], 1) + roll(fast[r], -1)
                new_fast[r] = advance(fast[r], slow[r], around, row_coeffs[0, r + STEPS - 1], row_coeffs[1, r + STEPS - 1])
            keep = max(margin - 1, 0)
            slow = {r: relax(fast[r], slow[r]) for r in range(-keep, SUB + keep)}
            fast = new_fast
            around = strip_neighbours(*strip_fast)
            moved = [
                advance(strip_fast[p], strip_slow[p], around[p], strip_coeffs[0, p], strip_coeffs[1, p]) for p in range(3)
            ]
            strip_slow = [relax(a, b) for a, b in zip(strip_fast, strip_slow)]
            strip_fast = moved
        middle = (lane >= STEPS) & (lane < LANES - STEPS)
        for f, rows in enumerate((fast, slow)):
            for r in range(SUB):
                cells[group(g), (f * SUB + r) * LANES:(f * SUB + r + 1) * LANES] = jnp.where(middle, rows[r], 0.0)
        ends = [jnp.where(inner, s[1], s[0]) for s in (strip_fast, strip_slow)]
        cells[group(g), 2 * SUB * LANES:] = jnp.where(lane < LANES // 2, ends[0], roll(ends[1], LANES // 2))

    for index, (i, j) in enumerate(block_pairs(fields // SIDE)):
        row, half = divmod(index, 2)
        gram[row * SIDE:(row + 1) * SIDE, half * SIDE:(half + 1) * SIDE] = dot_nt(
            cells[i * SIDE:(i + 1) * SIDE, :], cells[j * SIDE:(j + 1) * SIDE, :]
        )


def local_call(body, name, out_shapes, scratch, *args):
    spec = pl.BlockSpec(memory_space=pltpu.VMEM)
    return pl.pallas_call(
        body,
        out_shape=[jax.ShapeDtypeStruct(s, jnp.float32) for s in out_shapes],
        in_specs=[spec] * len(args),
        out_specs=[spec] * len(out_shapes),
        scratch_shapes=[pltpu.VMEM(s, jnp.float32) for s in scratch],
        compiler_params=pltpu.CompilerParams(vmem_limit_bytes=40 * 1024 * 1024),
        name=name,
    )(*args)


def swap(cells, axis, first):
    count = lax.axis_size(axis)
    pairs = [(i, i + 1) for i in range(first, count - 1, 2)]
    return lax.ppermute(cells, axis, pairs + [(b, a) for a, b in pairs])


def exchange(cells, axis, bit):
    count = lax.axis_size(axis)
    return lax.ppermute(cells, axis, [(i, i ^ bit) for i in range(count)])


def sum_blocks(packed):
    half = packed.shape[0] // 2
    odd = lax.axis_index("tile") % 2 == 1
    low, high = packed[:half], packed[half:]
    part = jnp.where(odd, high, low) + exchange(jnp.where(odd, low, high), "tile", 1)
    for axis, first in (("grp", 1), ("tile", 2)):
        bit = first
        while bit < lax.axis_size(axis):
            part = part + exchange(part, axis, bit)
            bit *= 2
    other = exchange(part, "tile", 1)
    return jnp.concatenate([jnp.where(odd, other, part), jnp.where(odd, part, other)], axis=0)


def per_device(tangents, reaction_self, reaction_cross):
    fields = tangents.shape[1]
    padded = fields + SUB
    rows = tangents.reshape(2, fields * tangents.shape[2], tangents.shape[3])
    message, strip = (2 * STEPS - 1, padded, LANES), (padded, LANES)
    near, far, edges = local_call(
        functools.partial(pack_kernel, fields), "pack", [message, message, strip], [], rows, reaction_self, reaction_cross
    )
    near_edges, far_edges = swap(edges, "tile", 0), swap(edges, "tile", 1)
    near_rows, far_rows = swap(near, "tile", 0), swap(far, "tile", 1)
    fast_edges, slow_edges, near_cols, far_cols = local_call(
        column_kernel, "columns", [strip] * 4, [], edges, near_edges, far_edges
    )
    near_cols, far_cols = swap(near_cols, "grp", 0), swap(far_cols, "grp", 1)
    side_blocks = fields // SIDE
    blocks = side_blocks * (side_blocks + 1) // 2
    (packed,) = local_call(
        functools.partial(evolve_kernel, fields), "evolve", [((blocks + 1) // 2 * SIDE, 2 * SIDE)],
        [(2, padded, LANES), (2, SUB + 2 * STEPS - 2, SUB, LANES), (2, 3, SUB, LANES), (fields, (2 * SUB + 1) * LANES)],
        rows, reaction_self, reaction_cross, near_rows, far_rows, fast_edges, slow_edges, near_cols, far_cols,
    )
    block_total = lax.axis_size("grp") * lax.axis_size("tile")
    corrections, growth = factor_call(sum_blocks(packed), packed, fields, math.sqrt(block_total))
    return (corrections, growth)


def solution(mesh):
    in_specs = (P(None, None, "tile", "grp"), P("tile", "grp"), P("tile", "grp"))
    out_specs = (P(("grp", "tile"), None), P())
    return jax.shard_map(
        per_device, mesh=mesh, in_specs=in_specs, out_specs=out_specs, check_vma=False
    )
```

```python
import functools
import math

import jax
import jax.numpy as jnp
from jax import lax
from jax.experimental import pallas as pl
from jax.experimental.pallas import tpu as pltpu
from jax.sharding import PartitionSpec as P


STEPS = 4
diffusion = 0.2
slow_rate = 0.05
HEIGHT_EDGE = 24
HEIGHT_ROW = 24
HEIGHT_STRIP = 24
HEIGHT_EVOLVE = 16
SIDE = 64
LANES = 128
SUB = 8
HI = lax.Precision.HIGHEST

def dot_nn(a, b):
    return lax.dot_general(a, b, (((1,), (0,)), ((), ())), precision=HI, preferred_element_type=jnp.float32)
def dot_tn(a, b):
    return lax.dot_general(a, b, (((0,), (0,)), ((), ())), precision=HI, preferred_element_type=jnp.float32)
def dot_nt(a, b):
    return lax.dot_general(a, b, (((1,), (1,)), ((), ())), precision=HI, preferred_element_type=jnp.float32)

def block_pairs(n):
    return [(i, j) for i in range(n) for j in range(i, n)]

def unpack_blocks(ref, n):
    out = {}
    for index, key in enumerate(block_pairs(n)):
        row, half = divmod(index, 2)
        out[key] = ref[row*SIDE:(row+1)*SIDE, half*SIDE:(half+1)*SIDE]
    return out

def spread_lane(x, lane):
    return jnp.broadcast_to(x[:, lane:lane+1], (x.shape[0], LANES))
def spread_row(x, row):
    return jnp.broadcast_to(x[row:row+1, :], (SUB, x.shape[1]))

def factor_blocks(blocks):
    groups = SIDE // SUB
    eye = (lax.broadcasted_iota(jnp.int32, (SIDE, SIDE), 0) == lax.broadcasted_iota(jnp.int32, (SIDE, SIDE), 1)).astype(jnp.float32)
    sub = lax.broadcasted_iota(jnp.int32, (SUB, LANES), 0)
    states = []
    for d in blocks:
        whole = jnp.concatenate([d, eye], axis=1)
        states.append([whole[g*SUB:(g+1)*SUB] for g in range(groups)])
    done = [[] for _ in blocks]
    for p in range(groups):
        for s, v in enumerate(states):
            cols = {}
            for g in range(p, groups):
                for c in range(SUB):
                    cols[g, c] = spread_lane(v[g], p*SUB + c)
            rows = [spread_row(v[p], c) for c in range(SUB)]
            pivots = {(a, c): spread_row(cols[p, c], a) for c in range(SUB) for a in range(c, SUB)}
            mult = {}
            scale = []
            for c in range(SUB):
                inv = 1.0 / pivots[c, c]
                scale.append(lax.rsqrt(pivots[c, c]))
                for a in range(c + 1, SUB):
                    mult[a, c] = pivots[a, c] * inv
                    rows[a] = rows[a] - mult[a, c] * rows[c]
                    for b in range(c + 1, a + 1):
                        pivots[a, b] = pivots[a, b] - mult[a, c] * pivots[b, c]
            scaled = [rows[c] * scale[c] for c in range(SUB)]
            panel = scaled[0]
            for c in range(1, SUB):
                panel = jnp.where(sub == c, scaled[c], panel)
            done[s].append(panel)
            for g in range(p + 1, groups):
                for c in range(SUB):
                    for a in range(c + 1, SUB):
                        cols[g, a] = cols[g, a] - mult[a, c] * cols[g, c]
                    v[g] = v[g] - (cols[g, c] * scale[c]) * scaled[c]
    out = []
    for panels in done:
        whole = jnp.concatenate(panels, axis=0)
        out.append((whole[:, :SIDE], whole[:, SIDE:]))
    return out

def factor_kernel(n, weight, tot_ref, loc_ref, out_ref, growth_ref):
    total = unpack_blocks(tot_ref, n)
    local = unpack_blocks(loc_ref, n)
    keep = (lax.broadcasted_iota(jnp.int32, (SIDE, SIDE), 0) <= lax.broadcasted_iota(jnp.int32, (SIDE, SIDE), 1))
    diag = (lax.broadcasted_iota(jnp.int32, (SIDE, SIDE), 0) == lax.broadcasted_iota(jnp.int32, (SIDE, SIDE), 1))
    inverse = {}
    answer = {}
    for k in range(n):
        (r_t, i_t), (r_l, i_l) = factor_blocks([total[k, k], local[k, k]])
        inverse[k] = i_t
        local[k, k] = jnp.where(keep, r_l, 0.0)
        growth_ref[0, k*SIDE:(k+1)*SIDE] = jnp.log(jnp.sum(jnp.where(diag, r_t, 0.0), axis=0))
        for grams, inv in ((total, i_t), (local, i_l)):
            if k + 1 < n:
                row = dot_nn(inv, jnp.concatenate([grams[k, j] for j in range(k + 1, n)], axis=1))
                for j in range(k + 1, n):
                    grams[k, j] = row[:, (j-k-1)*SIDE:(j-k)*SIDE]
                for i in range(k + 1, n):
                    rest = dot_tn(grams[k, i], row[:, (i-k-1)*SIDE:])
                    for j in range(i, n):
                        grams[i, j] = grams[i, j] - rest[:, (j-i)*SIDE:(j-i+1)*SIDE]
    for j in range(n):
        for i in range(j + 1):
            rest = local[i, j]
            for m in range(i, j):
                rest = rest - dot_nn(answer[i, m], total[m, j])
            answer[i, j] = dot_nt(rest, inverse[j])
            out_ref[i*SIDE:(i+1)*SIDE, j*SIDE:(j+1)*SIDE] = weight * answer[i, j]
        for i in range(j + 1, n):
            out_ref[i*SIDE:(i+1)*SIDE, j*SIDE:(j+1)*SIDE] = jnp.zeros((SIDE, SIDE), jnp.float32)

def factor_call(total, local, k, weight):
    vm = pl.BlockSpec(memory_space=pltpu.VMEM)
    out, growth = pl.pallas_call(
        functools.partial(factor_kernel, k // SIDE, weight),
        out_shape=(jax.ShapeDtypeStruct((k, k), jnp.float32), jax.ShapeDtypeStruct((1, k), jnp.float32)),
        in_specs=[vm, vm], out_specs=(vm, vm), name="factor",
    )(total, local)
    return out, growth[0]


def pick(flag, first, second):
    return jnp.where(flag, first, second)


def roll(x, shift):
    return pltpu.roll(x, shift % LANES, 1)


def lane_index(like):
    return lax.broadcasted_iota(jnp.int32, like.shape, like.ndim - 1)


def chunk(g, height):
    return pl.ds(pl.multiple_of(g * height, height), height)


def own_rows(tangents, g, height):
    return [[tangents[f, pl.ds(g * height * SUB + r, height, stride=SUB), :] for r in range(SUB)] for f in range(2)]


def own_coeffs(coeff_self, coeff_cross):
    return [[spread_row(ref[...], r) for r in range(SUB)] for ref in (coeff_self, coeff_cross)]


def tall(x, height):
    return jnp.concatenate([x] * (height // SUB), axis=0)


def edge_kernel(fields, height, tangents_hbm, self_hbm, cross_hbm, last_out, first_out, near, far, tangents, coeff_self, coeff_cross, sems):
    loads = [
        pltpu.make_async_copy(src, dst, sems.at[i])
        for i, (src, dst) in enumerate(((tangents_hbm, tangents), (self_hbm, coeff_self), (cross_hbm, coeff_cross)))
    ]
    for load in loads:
        load.start()
    for load in loads:
        load.wait()
    odd = lax.axis_index("tile") % 2 == 1

    def send(at, rows):
        cell = lane_index(rows[0][0]) // SUB
        cells = LANES // SUB
        last, first = None, None
        for f in range(2):
            for r in range(SUB):
                s = f * SUB + r
                turned = roll(rows[f][r], (s + 1) * SUB)
                last = turned if last is None else jnp.where(cell == s, turned, last)
                first = turned if first is None else jnp.where(cell == (s + 1) % cells, turned, first)
        first = roll(first, -SUB)
        last_out[at, :] = last
        first_out[at, :] = first
        half = cell % SUB < STEPS
        to_above = jnp.where(half, last, roll(first, STEPS * SUB))
        to_below = jnp.where(half, roll(last, -STEPS * SUB), first)
        near[at, :] = pick(odd, to_above, to_below)
        far[at, :] = pick(odd, to_below, to_above)

    @pl.loop(0, fields // height)
    def _(g):
        send(chunk(g, height), own_rows(tangents, g, height))

    send(pl.ds(fields, SUB), own_coeffs(coeff_self, coeff_cross))


def row_kernel(fields, height, after, tangents, coeff_self, coeff_cross, near, far):
    odd = lax.axis_index("tile") % 2 == 1

    def send(at, rows):
        for f in range(2):
            count = STEPS - f
            for j in range(count):
                top, bottom = rows[f][j], rows[f][SUB - count + j]
                near[f * STEPS + j, at, :] = pick(odd, top, bottom)
                far[f * STEPS + j, at, :] = pick(odd, bottom, top)

    @pl.loop(0, fields // height)
    def _(g):
        send(chunk(g, height), own_rows(tangents, g, height))

    send(pl.ds(fields, SUB), own_coeffs(coeff_self, coeff_cross))


def column_kernel(last, first, near, far, strips, near_out, far_out, outer):
    tile, tiles = lax.axis_index("tile"), lax.axis_size("tile")
    odd, at_top, at_bottom = tile % 2 == 1, tile == 0, tile == tiles - 1
    grp_odd = lax.axis_index("grp") % 2 == 1
    one, two = near[...], far[...]
    lane = lane_index(one)
    cell, low, inner = lane // SUB % SUB, lane < LANES // 2, lane % SUB < STEPS
    half = cell < STEPS
    above, below = pick(odd, one, two), pick(odd, two, one)
    outer[0] = jnp.where(half, below, roll(above, STEPS * SUB))
    outer[1] = jnp.where(half, roll(below, -STEPS * SUB), above)

    @pl.when(at_top | at_bottom)
    def _():
        outside = (half & at_bottom) | (~half & at_top)
        for i, ref in enumerate((last, first)):
            own = ref[...]
            mirrored = roll(own, -7 * SUB)
            for s in range(1, SUB):
                mirrored = jnp.where(cell == s, roll(own, (2 * s - 7) * SUB), mirrored)
            outer[i] = jnp.where(outside, mirrored, outer[i])

    sides = []
    for i, ref in enumerate((last, first)):
        own, more = ref[...], outer[i]
        fast = jnp.where(low, own, roll(more, LANES // 2))
        slow = jnp.where(low, roll(own, LANES // 2), more)
        strips[2 * i] = fast
        strips[2 * i + 1] = slow
        sides.append((fast, slow))
    to_left = jnp.where(inner, sides[1][0], roll(sides[1][1], STEPS))
    to_right = jnp.where(inner, roll(sides[0][0], -STEPS), sides[0][1])
    near_out[...] = pick(grp_odd, to_left, to_right)
    far_out[...] = pick(grp_odd, to_right, to_left)


def strip_neighbours(last, first, halo):
    c = lane_index(last) % SUB
    end, begin = c == SUB - 1, c == 0
    out = []
    for x, after, before in (
        (last, roll(halo, 7), None),
        (first, None, roll(halo, -7)),
        (halo, roll(first, 7), roll(last, -7)),
    ):
        right, left = roll(x, -1), roll(x, 1)
        if after is not None:
            right = jnp.where(end, after, right)
        if before is not None:
            left = jnp.where(begin, before, left)
        out.append(roll(x, SUB) + roll(x, -SUB) + right + left)
    return out


def advance(fast, slow, around, gain, cross):
    return gain * fast + diffusion * around + cross * slow


def relax(fast, slow):
    return (1.0 - slow_rate) * slow + slow_rate * fast


def strip_kernel(fields, height, strips, near, far, ends, halo):
    grp, grps = lax.axis_index("grp"), lax.axis_size("grp")
    grp_odd = grp % 2 == 1
    one, two = near[...], far[...]
    lane = lane_index(one)
    c = lane % SUB
    inner = c < STEPS
    left, right = pick(grp_odd, one, two), pick(grp_odd, two, one)
    halo[0] = jnp.where(inner, right, roll(left, STEPS))
    halo[1] = jnp.where(inner, roll(right, -STEPS), left)

    @pl.when((grp == 0) | (grp == grps - 1))
    def _():
        after, before = inner & (grp == grps - 1), ~inner & (grp == 0)
        for f in range(2):
            tail, start = strips[f], strips[2 + f]
            mirrored = halo[f]
            for s in range(STEPS):
                mirrored = jnp.where(after & (c == s), roll(tail, 2 * s - 7), mirrored)
                mirrored = jnp.where(before & (c == 7 - s), roll(start, 7 - 2 * s), mirrored)
            halo[f] = mirrored

    def parts(f, at):
        return [strips[f, at, :], strips[2 + f, at, :], halo[f, at, :]]

    gains = [tall(x + (1.0 - 4.0 * diffusion), height) for x in parts(0, pl.ds(fields, SUB))]
    crosses = [tall(x, height) for x in parts(1, pl.ds(fields, SUB))]

    @pl.loop(0, fields // height)
    def _(g):
        fast, slow = parts(0, chunk(g, height)), parts(1, chunk(g, height))
        for step in range(STEPS):
            around = strip_neighbours(*fast)
            moved = [advance(fast[p], slow[p], around[p], gains[p], crosses[p]) for p in range(3)]
            slow = [relax(a, b) for a, b in zip(fast, slow)]
            fast = moved
        l = lane_index(fast[0])
        joined = [jnp.where(l % SUB < STEPS, s[1], s[0]) for s in (fast, slow)]
        ends[chunk(g, height), :] = jnp.where(l < LANES // 2, joined[0], roll(joined[1], LANES // 2))


def extended_rows(own, near, far, at):
    tile, tiles = lax.axis_index("tile"), lax.axis_size("tile")
    odd, at_top, at_bottom = tile % 2 == 1, tile == 0, tile == tiles - 1
    out = []
    for f in range(2):
        count = STEPS - f
        rows = dict(enumerate(own[f]))
        for j in range(count):
            one, two = near[f * STEPS + j, at, :], far[f * STEPS + j, at, :]
            rows[j - count] = pick(at_top, own[f][count - 1 - j], pick(odd, one, two))
            rows[SUB + j] = pick(at_bottom, own[f][SUB - 1 - j], pick(odd, two, one))
        out.append(rows)
    return out


def evolve_kernel(fields, height, tangents, coeff_self, coeff_cross, near, far, ends, gram, row_coeffs, cells):
    coeff_rows = extended_rows(own_coeffs(coeff_self, coeff_cross), near, far, pl.ds(fields, SUB))
    for f in range(2):
        for r in range(1 - STEPS, SUB + STEPS - 1):
            row_coeffs[f, r + STEPS - 1, :, :] = coeff_rows[f][r] + (1.0 - 4.0 * diffusion) * (1 - f)

    @pl.loop(0, fields // height)
    def _(g):
        at = chunk(g, height)
        fast, slow = extended_rows(own_rows(tangents, g, height), near, far, at)
        for step in range(1, STEPS + 1):
            margin = STEPS - step
            new_fast = {}
            for r in range(-margin, SUB + margin):
                around = fast[r - 1] + fast[r + 1] + roll(fast[r], 1) + roll(fast[r], -1)
                gain, cross = (tall(row_coeffs[f, r + STEPS - 1], height) for f in range(2))
                new_fast[r] = advance(fast[r], slow[r], around, gain, cross)
            keep = max(margin - 1, 0)
            slow = {r: relax(fast[r], slow[r]) for r in range(-keep, SUB + keep)}
            fast = new_fast
        lane = lane_index(fast[0])
        middle = (lane >= STEPS) & (lane < LANES - STEPS)
        for f, rows in enumerate((fast, slow)):
            for r in range(SUB):
                cells[at, (f * SUB + r) * LANES:(f * SUB + r + 1) * LANES] = jnp.where(middle, rows[r], 0.0)

    cells[:, 2 * SUB * LANES:] = ends[...]
    whole = dot_nt(cells[...], cells[...])
    for index, (i, j) in enumerate(block_pairs(fields // SIDE)):
        row, half = divmod(index, 2)
        gram[row * SIDE:(row + 1) * SIDE, half * SIDE:(half + 1) * SIDE] = whole[
            i * SIDE:(i + 1) * SIDE, j * SIDE:(j + 1) * SIDE
        ]


def local_call(body, name, out_shapes, scratch, *args, outside=0):
    spec = pl.BlockSpec(memory_space=pltpu.VMEM)
    own = [pltpu.VMEM(a.shape, a.dtype) for a in args[:outside]]
    if outside:
        own.append(pltpu.SemaphoreType.DMA((outside,)))
    return pl.pallas_call(
        body,
        out_shape=[jax.ShapeDtypeStruct(s, jnp.float32) for s in out_shapes],
        in_specs=[pl.BlockSpec(memory_space=pl.ANY)] * outside + [spec] * (len(args) - outside),
        out_specs=[spec] * len(out_shapes),
        scratch_shapes=[pltpu.VMEM(s, jnp.float32) for s in scratch] + own,
        compiler_params=pltpu.CompilerParams(vmem_limit_bytes=40 * 1024 * 1024),
        name=name,
    )(*args)


def swap(cells, axis, first):
    count = lax.axis_size(axis)
    pairs = [(i, i + 1) for i in range(first, count - 1, 2)]
    return lax.ppermute(cells, axis, pairs + [(b, a) for a, b in pairs])


def exchange(cells, axis, bit):
    count = lax.axis_size(axis)
    return lax.ppermute(cells, axis, [(i, i ^ bit) for i in range(count)])


def sum_blocks(packed):
    half = packed.shape[0] // 2
    odd = lax.axis_index("tile") % 2 == 1
    low, high = packed[:half], packed[half:]
    part = jnp.where(odd, high, low) + exchange(jnp.where(odd, low, high), "tile", 1)
    for axis, first in (("grp", 1), ("tile", 2)):
        bit = first
        while bit < lax.axis_size(axis):
            part = part + exchange(part, axis, bit)
            bit *= 2
    other = exchange(part, "tile", 1)
    return jnp.concatenate([jnp.where(odd, other, part), jnp.where(odd, part, other)], axis=0)


def per_device(tangents, reaction_self, reaction_cross):
    fields = tangents.shape[1]
    padded = fields + SUB
    rows = tangents.reshape(2, fields * tangents.shape[2], tangents.shape[3])
    message, strip = (2 * STEPS - 1, padded, LANES), (padded, LANES)
    inputs = (rows, reaction_self, reaction_cross)
    last, first, near_edges, far_edges = local_call(
        functools.partial(edge_kernel, fields, HEIGHT_EDGE), "edges", [strip] * 4, [], *inputs, outside=3
    )
    near_edges, far_edges = swap(near_edges, "tile", 0), swap(far_edges, "tile", 1)
    near_rows, far_rows = local_call(
        functools.partial(row_kernel, fields, HEIGHT_ROW), "rows", [message] * 2, [], last, *inputs
    )
    near_rows, far_rows = swap(near_rows, "tile", 0), swap(far_rows, "tile", 1)
    strips, near_cols, far_cols = local_call(
        column_kernel, "columns", [(4,) + strip, strip, strip], [(2,) + strip], last, first, near_edges, far_edges
    )
    near_cols, far_cols = swap(near_cols, "grp", 0), swap(far_cols, "grp", 1)
    (ends,) = local_call(
        functools.partial(strip_kernel, fields, HEIGHT_STRIP), "strips", [(fields, LANES)], [(2,) + strip], strips, near_cols, far_cols
    )
    side_blocks = fields // SIDE
    blocks = side_blocks * (side_blocks + 1) // 2
    (packed,) = local_call(
        functools.partial(evolve_kernel, fields, HEIGHT_EVOLVE), "evolve", [((blocks + 1) // 2 * SIDE, 2 * SIDE)],
        [(2, SUB + 2 * STEPS - 2, SUB, LANES), (fields, (2 * SUB + 1) * LANES)],
        *inputs, near_rows, far_rows, ends,
    )
    block_total = lax.axis_size("grp") * lax.axis_size("tile")
    corrections, growth = factor_call(sum_blocks(packed), packed, fields, math.sqrt(block_total))
    return (corrections, growth)


def solution(mesh):
    in_specs = (P(None, None, "tile", "grp"), P("tile", "grp"), P("tile", "grp"))
    out_specs = (P(("grp", "tile"), None), P())
    return jax.shard_map(
        per_device, mesh=mesh, in_specs=in_specs, out_specs=out_specs, check_vma=False
    )
```

```python
import functools
import math

import jax
import jax.numpy as jnp
from jax import lax
from jax.experimental import pallas as pl
from jax.experimental.pallas import tpu as pltpu
from jax.sharding import PartitionSpec as P


STEPS = 4
diffusion = 0.2
slow_rate = 0.05
HEIGHT_EDGE = 48
HEIGHT_ROW = 48
HEIGHT_STRIP = 96
HEIGHT_EVOLVE = 48
SIDE = 64
VMEM_BYTES = 24 * 1024 * 1024
LANES = 128
SUB = 8
HI = lax.Precision.HIGHEST

def dot_nn(a, b):
    return lax.dot_general(a, b, (((1,), (0,)), ((), ())), precision=HI, preferred_element_type=jnp.float32)
def dot_tn(a, b):
    return lax.dot_general(a, b, (((0,), (0,)), ((), ())), precision=HI, preferred_element_type=jnp.float32)
def dot_nt(a, b):
    return lax.dot_general(a, b, (((1,), (1,)), ((), ())), precision=HI, preferred_element_type=jnp.float32)

def block_pairs(n):
    return [(i, j) for i in range(n) for j in range(i, n)]

def unpack_blocks(packed, n):
    out = {}
    for index, key in enumerate(block_pairs(n)):
        row, half = divmod(index, 2)
        out[key] = packed[row*SIDE:(row+1)*SIDE, half*SIDE:(half+1)*SIDE]
    return out

def spread_lane(x, lane):
    return jnp.broadcast_to(x[:, lane:lane+1], (x.shape[0], LANES))
def spread_row(x, row):
    return jnp.broadcast_to(x[row:row+1, :], (SUB, x.shape[1]))

def factor_blocks(blocks):
    groups = SIDE // SUB
    eye = (lax.broadcasted_iota(jnp.int32, (SIDE, SIDE), 0) == lax.broadcasted_iota(jnp.int32, (SIDE, SIDE), 1)).astype(jnp.float32)
    sub = lax.broadcasted_iota(jnp.int32, (SUB, LANES), 0)
    states = []
    for d in blocks:
        whole = jnp.concatenate([d, eye], axis=1)
        states.append([whole[g*SUB:(g+1)*SUB] for g in range(groups)])
    done = [[] for _ in blocks]
    for p in range(groups):
        for s, v in enumerate(states):
            cols = {}
            for g in range(p, groups):
                for c in range(SUB):
                    cols[g, c] = spread_lane(v[g], p*SUB + c)
            rows = [spread_row(v[p], c) for c in range(SUB)]
            pivots = {(a, c): spread_row(cols[p, c], a) for c in range(SUB) for a in range(c, SUB)}
            mult = {}
            scale = []
            for c in range(SUB):
                inv = 1.0 / pivots[c, c]
                scale.append(lax.rsqrt(pivots[c, c]))
                for a in range(c + 1, SUB):
                    mult[a, c] = pivots[a, c] * inv
                    rows[a] = rows[a] - mult[a, c] * rows[c]
                    for b in range(c + 1, a + 1):
                        pivots[a, b] = pivots[a, b] - mult[a, c] * pivots[b, c]
            scaled = [rows[c] * scale[c] for c in range(SUB)]
            panel = scaled[0]
            for c in range(1, SUB):
                panel = jnp.where(sub == c, scaled[c], panel)
            done[s].append(panel)
            for g in range(p + 1, groups):
                for c in range(SUB):
                    for a in range(c + 1, SUB):
                        cols[g, a] = cols[g, a] - mult[a, c] * cols[g, c]
                    v[g] = v[g] - (cols[g, c] * scale[c]) * scaled[c]
    out = []
    for panels in done:
        whole = jnp.concatenate(panels, axis=0)
        out.append((whole[:, :SIDE], whole[:, SIDE:]))
    return out

def factor_kernel(n, weight, own_ref, other_ref, loc_ref, out_ref, growth_ref):
    odd = lax.axis_index("tile") % 2 == 1
    own, other = own_ref[...], other_ref[...]
    total = unpack_blocks(jnp.concatenate([jnp.where(odd, other, own), jnp.where(odd, own, other)], axis=0), n)
    local = unpack_blocks(loc_ref[...], n)
    keep = (lax.broadcasted_iota(jnp.int32, (SIDE, SIDE), 0) <= lax.broadcasted_iota(jnp.int32, (SIDE, SIDE), 1))
    diag = (lax.broadcasted_iota(jnp.int32, (SIDE, SIDE), 0) == lax.broadcasted_iota(jnp.int32, (SIDE, SIDE), 1))
    inverse = {}
    answer = {}
    for k in range(n):
        (r_t, i_t), (r_l, i_l) = factor_blocks([total[k, k], local[k, k]])
        inverse[k] = i_t
        local[k, k] = jnp.where(keep, r_l, 0.0)
        growth_ref[0, k*SIDE:(k+1)*SIDE] = jnp.log(jnp.sum(jnp.where(diag, r_t, 0.0), axis=0))
        for grams, inv in ((total, i_t), (local, i_l)):
            if k + 1 < n:
                row = dot_nn(inv, jnp.concatenate([grams[k, j] for j in range(k + 1, n)], axis=1))
                for j in range(k + 1, n):
                    grams[k, j] = row[:, (j-k-1)*SIDE:(j-k)*SIDE]
                for i in range(k + 1, n):
                    rest = dot_tn(grams[k, i], row[:, (i-k-1)*SIDE:])
                    for j in range(i, n):
                        grams[i, j] = grams[i, j] - rest[:, (j-i)*SIDE:(j-i+1)*SIDE]
    for j in range(n):
        for i in range(j + 1):
            rest = local[i, j]
            for m in range(i, j):
                rest = rest - dot_nn(answer[i, m], total[m, j])
            answer[i, j] = dot_nt(rest, inverse[j])
            out_ref[i*SIDE:(i+1)*SIDE, j*SIDE:(j+1)*SIDE] = weight * answer[i, j]
        for i in range(j + 1, n):
            out_ref[i*SIDE:(i+1)*SIDE, j*SIDE:(j+1)*SIDE] = jnp.zeros((SIDE, SIDE), jnp.float32)

def factor_call(own, other, local, k, weight):
    out, growth = local_call(
        functools.partial(factor_kernel, k // SIDE, weight), "factor", [(k, k), (1, k)], [], own, other, local
    )
    return out, growth[0]


def pick(flag, first, second):
    return jnp.where(flag, first, second)


def roll(x, shift):
    return pltpu.roll(x, shift % LANES, 1)


def lane_index(like):
    return lax.broadcasted_iota(jnp.int32, like.shape, like.ndim - 1)


def chunk(g, height):
    return pl.ds(pl.multiple_of(g * height, height), height)


def own_rows(tangents, g, height):
    return [[tangents[f, pl.ds(g * height * SUB + r, height, stride=SUB), :] for r in range(SUB)] for f in range(2)]


def own_coeffs(coeff_self, coeff_cross):
    return [[spread_row(ref[...], r) for r in range(SUB)] for ref in (coeff_self, coeff_cross)]


def tall(x, height):
    return jnp.concatenate([x] * (height // SUB), axis=0)


def edge_kernel(fields, height, tangents_hbm, self_hbm, cross_hbm, last_out, first_out, near, far, tangents, coeff_self, coeff_cross, sems):
    chunks = fields // height
    span = height * SUB
    loads = [
        pltpu.make_async_copy(tangents_hbm.at[:, pl.ds(g * span, span), :], tangents.at[:, pl.ds(g * span, span), :], sems.at[g])
        for g in range(chunks)
    ]
    small = [
        pltpu.make_async_copy(src, dst, sems.at[chunks + i])
        for i, (src, dst) in enumerate(((self_hbm, coeff_self), (cross_hbm, coeff_cross)))
    ]
    for load in loads + small:
        load.start()
    odd = lax.axis_index("tile") % 2 == 1

    def send(at, rows):
        cell = lane_index(rows[0][0]) // SUB
        cells = LANES // SUB
        last, first = None, None
        for f in range(2):
            for r in range(SUB):
                s = f * SUB + r
                turned = roll(rows[f][r], (s + 1) * SUB)
                last = turned if last is None else jnp.where(cell == s, turned, last)
                first = turned if first is None else jnp.where(cell == (s + 1) % cells, turned, first)
        first = roll(first, -SUB)
        last_out[at, :] = last
        first_out[at, :] = first
        half = cell % SUB < STEPS
        to_above = jnp.where(half, last, roll(first, STEPS * SUB))
        to_below = jnp.where(half, roll(last, -STEPS * SUB), first)
        near[at, :] = pick(odd, to_above, to_below)
        far[at, :] = pick(odd, to_below, to_above)

    for g, load in enumerate(loads):
        load.wait()
        send(pl.ds(g * height, height), own_rows(tangents, g, height))
    for load in small:
        load.wait()
    send(pl.ds(fields, SUB), own_coeffs(coeff_self, coeff_cross))


def row_kernel(fields, height, after, tangents, coeff_self, coeff_cross, near, far):
    odd = lax.axis_index("tile") % 2 == 1

    def send(at, rows):
        for f in range(2):
            count = STEPS - f
            for j in range(count):
                top, bottom = rows[f][j], rows[f][SUB - count + j]
                near[f * STEPS + j, at, :] = pick(odd, top, bottom)
                far[f * STEPS + j, at, :] = pick(odd, bottom, top)

    @pl.loop(0, fields // height)
    def _(g):
        send(chunk(g, height), own_rows(tangents, g, height))

    send(pl.ds(fields, SUB), own_coeffs(coeff_self, coeff_cross))


def column_kernel(last, first, near, far, strips, near_out, far_out, outer):
    tile, tiles = lax.axis_index("tile"), lax.axis_size("tile")
    odd, at_top, at_bottom = tile % 2 == 1, tile == 0, tile == tiles - 1
    grp_odd = lax.axis_index("grp") % 2 == 1
    one, two = near[...], far[...]
    lane = lane_index(one)
    cell, low, inner = lane // SUB % SUB, lane < LANES // 2, lane % SUB < STEPS
    half = cell < STEPS
    above, below = pick(odd, one, two), pick(odd, two, one)
    outer[0] = jnp.where(half, below, roll(above, STEPS * SUB))
    outer[1] = jnp.where(half, roll(below, -STEPS * SUB), above)

    @pl.when(at_top | at_bottom)
    def _():
        outside = (half & at_bottom) | (~half & at_top)
        for i, ref in enumerate((last, first)):
            own = ref[...]
            mirrored = roll(own, -7 * SUB)
            for s in range(1, SUB):
                mirrored = jnp.where(cell == s, roll(own, (2 * s - 7) * SUB), mirrored)
            outer[i] = jnp.where(outside, mirrored, outer[i])

    sides = []
    for i, ref in enumerate((last, first)):
        own, more = ref[...], outer[i]
        fast = jnp.where(low, own, roll(more, LANES // 2))
        slow = jnp.where(low, roll(own, LANES // 2), more)
        strips[2 * i] = fast
        strips[2 * i + 1] = slow
        sides.append((fast, slow))
    to_left = jnp.where(inner, sides[1][0], roll(sides[1][1], STEPS))
    to_right = jnp.where(inner, roll(sides[0][0], -STEPS), sides[0][1])
    near_out[...] = pick(grp_odd, to_left, to_right)
    far_out[...] = pick(grp_odd, to_right, to_left)


def strip_neighbours(last, first, halo):
    c = lane_index(last) % SUB
    end, begin = c == SUB - 1, c == 0
    out = []
    for x, after, before in (
        (last, roll(halo, 7), None),
        (first, None, roll(halo, -7)),
        (halo, roll(first, 7), roll(last, -7)),
    ):
        right, left = roll(x, -1), roll(x, 1)
        if after is not None:
            right = jnp.where(end, after, right)
        if before is not None:
            left = jnp.where(begin, before, left)
        out.append(roll(x, SUB) + roll(x, -SUB) + right + left)
    return out


def advance(fast, slow, around, gain, cross):
    return gain * fast + diffusion * around + cross * slow


def relax(fast, slow):
    return (1.0 - slow_rate) * slow + slow_rate * fast


def strip_kernel(fields, height, strips, near, far, ends, halo):
    grp, grps = lax.axis_index("grp"), lax.axis_size("grp")
    grp_odd = grp % 2 == 1
    one, two = near[...], far[...]
    lane = lane_index(one)
    c = lane % SUB
    inner = c < STEPS
    left, right = pick(grp_odd, one, two), pick(grp_odd, two, one)
    halo[0] = jnp.where(inner, right, roll(left, STEPS))
    halo[1] = jnp.where(inner, roll(right, -STEPS), left)

    @pl.when((grp == 0) | (grp == grps - 1))
    def _():
        after, before = inner & (grp == grps - 1), ~inner & (grp == 0)
        for f in range(2):
            tail, start = strips[f], strips[2 + f]
            mirrored = halo[f]
            for s in range(STEPS):
                mirrored = jnp.where(after & (c == s), roll(tail, 2 * s - 7), mirrored)
                mirrored = jnp.where(before & (c == 7 - s), roll(start, 7 - 2 * s), mirrored)
            halo[f] = mirrored

    def parts(f, at):
        return [strips[f, at, :], strips[2 + f, at, :], halo[f, at, :]]

    gains = [tall(x + (1.0 - 4.0 * diffusion), height) for x in parts(0, pl.ds(fields, SUB))]
    crosses = [tall(x, height) for x in parts(1, pl.ds(fields, SUB))]

    @pl.loop(0, fields // height)
    def _(g):
        fast, slow = parts(0, chunk(g, height)), parts(1, chunk(g, height))
        for step in range(STEPS):
            around = strip_neighbours(*fast)
            moved = [advance(fast[p], slow[p], around[p], gains[p], crosses[p]) for p in range(3)]
            slow = [relax(a, b) for a, b in zip(fast, slow)]
            fast = moved
        l = lane_index(fast[0])
        joined = [jnp.where(l % SUB < STEPS, s[1], s[0]) for s in (fast, slow)]
        ends[chunk(g, height), :] = jnp.where(l < LANES // 2, joined[0], roll(joined[1], LANES // 2))


def extended_rows(own, near, far, at):
    tile, tiles = lax.axis_index("tile"), lax.axis_size("tile")
    odd, at_top, at_bottom = tile % 2 == 1, tile == 0, tile == tiles - 1
    out = []
    for f in range(2):
        count = STEPS - f
        rows = dict(enumerate(own[f]))
        for j in range(count):
            one, two = near[f * STEPS + j, at, :], far[f * STEPS + j, at, :]
            rows[j - count] = pick(at_top, own[f][count - 1 - j], pick(odd, one, two))
            rows[SUB + j] = pick(at_bottom, own[f][SUB - 1 - j], pick(odd, two, one))
        out.append(rows)
    return out


def evolve_kernel(fields, height, tangents, coeff_self, coeff_cross, near, far, ends, gram, row_coeffs, cells):
    coeff_rows = extended_rows(own_coeffs(coeff_self, coeff_cross), near, far, pl.ds(fields, SUB))
    for f in range(2):
        for r in range(1 - STEPS, SUB + STEPS - 1):
            row_coeffs[f, r + STEPS - 1, :, :] = coeff_rows[f][r] + (1.0 - 4.0 * diffusion) * (1 - f)

    @pl.loop(0, fields // height)
    def _(g):
        at = chunk(g, height)
        fast, slow = extended_rows(own_rows(tangents, g, height), near, far, at)
        for step in range(1, STEPS + 1):
            margin = STEPS - step
            new_fast = {}
            for r in range(-margin, SUB + margin):
                around = fast[r - 1] + fast[r + 1] + roll(fast[r], 1) + roll(fast[r], -1)
                gain, cross = (tall(row_coeffs[f, r + STEPS - 1], height) for f in range(2))
                new_fast[r] = advance(fast[r], slow[r], around, gain, cross)
            keep = max(margin - 1, 0)
            slow = {r: relax(fast[r], slow[r]) for r in range(-keep, SUB + keep)}
            fast = new_fast
        lane = lane_index(fast[0])
        middle = (lane >= STEPS) & (lane < LANES - STEPS)
        for f, rows in enumerate((fast, slow)):
            for r in range(SUB):
                cells[at, (f * SUB + r) * LANES:(f * SUB + r + 1) * LANES] = jnp.where(middle, rows[r], 0.0)

    whole = dot_nt(cells[...], cells[...]) + dot_nt(ends[...], ends[...])
    for index, (i, j) in enumerate(block_pairs(fields // SIDE)):
        row, half = divmod(index, 2)
        gram[row * SIDE:(row + 1) * SIDE, half * SIDE:(half + 1) * SIDE] = whole[
            i * SIDE:(i + 1) * SIDE, j * SIDE:(j + 1) * SIDE
        ]


def local_call(body, name, out_shapes, scratch, *args, hbm=False):
    spec = pl.BlockSpec(memory_space=pltpu.VMEM)
    return pl.pallas_call(
        body,
        out_shape=[jax.ShapeDtypeStruct(s, jnp.float32) for s in out_shapes],
        in_specs=[pl.BlockSpec(memory_space=pltpu.HBM) if hbm else spec] * len(args),
        out_specs=[spec] * len(out_shapes),
        scratch_shapes=[pltpu.VMEM(s, jnp.float32) if isinstance(s, tuple) else s for s in scratch],
        compiler_params=pltpu.CompilerParams(vmem_limit_bytes=VMEM_BYTES),
        name=name,
    )(*args)


def swap(cells, axis, first, close=False):
    count = lax.axis_size(axis)
    pairs = [(i, i + 1) for i in range(first, count - 1, 2)]
    if close and first:
        pairs.append((0, count - 1))
    return lax.ppermute(cells, axis, pairs + [(b, a) for a, b in pairs])


def exchange(cells, axis, bit):
    count = lax.axis_size(axis)
    return lax.ppermute(cells, axis, [(i, i ^ bit) for i in range(count)])


def sum_blocks(packed):
    half = packed.shape[0] // 2
    odd = lax.axis_index("tile") % 2 == 1
    low, high = packed[:half], packed[half:]
    part = jnp.where(odd, high, low) + exchange(jnp.where(odd, low, high), "tile", 1)
    for axis, first in (("grp", 1), ("tile", 2)):
        bit = first
        while bit < lax.axis_size(axis):
            part = part + exchange(part, axis, bit)
            bit *= 2
    return part, exchange(part, "tile", 1)


def per_device(tangents, reaction_self, reaction_cross):
    fields = tangents.shape[1]
    padded = fields + SUB
    rows = tangents.reshape(2, fields * tangents.shape[2], tangents.shape[3])
    message, strip = (2 * STEPS - 1, padded, LANES), (padded, LANES)
    inputs = (rows, reaction_self, reaction_cross)
    last, first, near_edges, far_edges, *inputs = local_call(
        functools.partial(edge_kernel, fields, HEIGHT_EDGE), "edges", [strip] * 4 + [a.shape for a in inputs],
        [pltpu.SemaphoreType.DMA((fields // HEIGHT_EDGE + 2,))], *inputs, hbm=True,
    )
    near_edges, far_edges = swap(near_edges, "tile", 0), swap(far_edges, "tile", 1)
    near_rows, far_rows = local_call(
        functools.partial(row_kernel, fields, HEIGHT_ROW), "rows", [message] * 2, [], near_edges, *inputs
    )
    far_edges, near_rows, far_rows = lax.optimization_barrier((far_edges, near_rows, far_rows))
    near_rows, far_rows = swap(near_rows, "tile", 0), swap(far_rows, "tile", 1)
    strips, near_cols, far_cols = local_call(
        column_kernel, "columns", [(4,) + strip, strip, strip], [(2,) + strip], last, first, near_edges, far_edges
    )
    near_cols, far_cols = swap(near_cols, "grp", 0), swap(far_cols, "grp", 1, close=True)
    (ends,) = local_call(
        functools.partial(strip_kernel, fields, HEIGHT_STRIP), "strips", [(fields, LANES)], [(2,) + strip], strips, near_cols, far_cols
    )
    side_blocks = fields // SIDE
    blocks = side_blocks * (side_blocks + 1) // 2
    (packed,) = local_call(
        functools.partial(evolve_kernel, fields, HEIGHT_EVOLVE), "evolve", [((blocks + 1) // 2 * SIDE, 2 * SIDE)],
        [(2, SUB + 2 * STEPS - 2, SUB, LANES), (fields, 2 * SUB * LANES)], *inputs, near_rows, far_rows, ends,
    )
    block_total = lax.axis_size("grp") * lax.axis_size("tile")
    corrections, growth = factor_call(*sum_blocks(packed), packed, fields, math.sqrt(block_total))
    return (corrections, growth)


def solution(mesh):
    in_specs = (P(None, None, "tile", "grp"), P("tile", "grp"), P("tile", "grp"))
    out_specs = (P(("grp", "tile"), None), P())
    return jax.shard_map(
        per_device, mesh=mesh, in_specs=in_specs, out_specs=out_specs, check_vma=False
    )
```

```python
import functools
import math

import jax
import jax.numpy as jnp
from jax import lax
from jax.experimental import pallas as pl
from jax.experimental.pallas import tpu as pltpu
from jax.sharding import PartitionSpec as P


STEPS = 4
diffusion = 0.2
slow_rate = 0.05
HEIGHT_EDGE = 48
HEIGHT_STRIP = 96
HEIGHT_EVOLVE = 48
SIDE = 64
VMEM_BYTES = 24 * 1024 * 1024
EDGE_VMEM_BYTES = 52 * 1024 * 1024
LANES = 128
SUB = 8
HI = lax.Precision.HIGHEST

def dot_nn(a, b):
    return lax.dot_general(a, b, (((1,), (0,)), ((), ())), precision=HI, preferred_element_type=jnp.float32)
def dot_tn(a, b):
    return lax.dot_general(a, b, (((0,), (0,)), ((), ())), precision=HI, preferred_element_type=jnp.float32)
def dot_nt(a, b):
    return lax.dot_general(a, b, (((1,), (1,)), ((), ())), precision=HI, preferred_element_type=jnp.float32)

def block_pairs(n):
    return [(i, j) for i in range(n) for j in range(i, n)]

def unpack_blocks(packed, n):
    out = {}
    for index, key in enumerate(block_pairs(n)):
        row, half = divmod(index, 2)
        out[key] = packed[row*SIDE:(row+1)*SIDE, half*SIDE:(half+1)*SIDE]
    return out

def spread_lane(x, lane):
    return jnp.broadcast_to(x[:, lane:lane+1], (x.shape[0], LANES))
def spread_row(x, row):
    return jnp.broadcast_to(x[row:row+1, :], (SUB, x.shape[1]))

def factor_blocks(blocks):
    groups = SIDE // SUB
    eye = (lax.broadcasted_iota(jnp.int32, (SIDE, SIDE), 0) == lax.broadcasted_iota(jnp.int32, (SIDE, SIDE), 1)).astype(jnp.float32)
    sub = lax.broadcasted_iota(jnp.int32, (SUB, LANES), 0)
    states = []
    for d in blocks:
        whole = jnp.concatenate([d, eye], axis=1)
        states.append([whole[g*SUB:(g+1)*SUB] for g in range(groups)])
    done = [[] for _ in blocks]
    for p in range(groups):
        for s, v in enumerate(states):
            cols = {}
            for g in range(p, groups):
                for c in range(SUB):
                    cols[g, c] = spread_lane(v[g], p*SUB + c)
            rows = [spread_row(v[p], c) for c in range(SUB)]
            pivots = {(a, c): spread_row(cols[p, c], a) for c in range(SUB) for a in range(c, SUB)}
            mult = {}
            scale = []
            for c in range(SUB):
                inv = 1.0 / pivots[c, c]
                scale.append(lax.rsqrt(pivots[c, c]))
                for a in range(c + 1, SUB):
                    mult[a, c] = pivots[a, c] * inv
                    rows[a] = rows[a] - mult[a, c] * rows[c]
                    for b in range(c + 1, a + 1):
                        pivots[a, b] = pivots[a, b] - mult[a, c] * pivots[b, c]
            scaled = [rows[c] * scale[c] for c in range(SUB)]
            panel = scaled[0]
            for c in range(1, SUB):
                panel = jnp.where(sub == c, scaled[c], panel)
            done[s].append(panel)
            for g in range(p + 1, groups):
                for c in range(SUB):
                    for a in range(c + 1, SUB):
                        cols[g, a] = cols[g, a] - mult[a, c] * cols[g, c]
                    v[g] = v[g] - (cols[g, c] * scale[c]) * scaled[c]
    out = []
    for panels in done:
        whole = jnp.concatenate(panels, axis=0)
        out.append((whole[:, :SIDE], whole[:, SIDE:]))
    return out

def factor_kernel(n, weight, own_ref, other_ref, loc_ref, out_ref, growth_ref):
    high_half = parity()
    own, other = own_ref[...], other_ref[...]
    total = unpack_blocks(jnp.concatenate([jnp.where(high_half, other, own), jnp.where(high_half, own, other)], axis=0), n)
    local = unpack_blocks(loc_ref[...], n)
    keep = (lax.broadcasted_iota(jnp.int32, (SIDE, SIDE), 0) <= lax.broadcasted_iota(jnp.int32, (SIDE, SIDE), 1))
    diag = (lax.broadcasted_iota(jnp.int32, (SIDE, SIDE), 0) == lax.broadcasted_iota(jnp.int32, (SIDE, SIDE), 1))
    inverse = {}
    answer = {}
    for k in range(n):
        (r_t, i_t), (r_l, i_l) = factor_blocks([total[k, k], local[k, k]])
        inverse[k] = i_t
        local[k, k] = jnp.where(keep, r_l, 0.0)
        growth_ref[0, k*SIDE:(k+1)*SIDE] = jnp.log(jnp.sum(jnp.where(diag, r_t, 0.0), axis=0))
        for grams, inv in ((total, i_t), (local, i_l)):
            if k + 1 < n:
                row = dot_nn(inv, jnp.concatenate([grams[k, j] for j in range(k + 1, n)], axis=1))
                for j in range(k + 1, n):
                    grams[k, j] = row[:, (j-k-1)*SIDE:(j-k)*SIDE]
                for i in range(k + 1, n):
                    rest = dot_tn(grams[k, i], row[:, (i-k-1)*SIDE:])
                    for j in range(i, n):
                        grams[i, j] = grams[i, j] - rest[:, (j-i)*SIDE:(j-i+1)*SIDE]
    for j in range(n):
        for i in range(j + 1):
            rest = local[i, j]
            for m in range(i, j):
                rest = rest - dot_nn(answer[i, m], total[m, j])
            answer[i, j] = dot_nt(rest, inverse[j])
            out_ref[i*SIDE:(i+1)*SIDE, j*SIDE:(j+1)*SIDE] = weight * answer[i, j]
        for i in range(j + 1, n):
            out_ref[i*SIDE:(i+1)*SIDE, j*SIDE:(j+1)*SIDE] = jnp.zeros((SIDE, SIDE), jnp.float32)

def factor_call(own, other, local, k, weight):
    out, growth = local_call(
        functools.partial(factor_kernel, k // SIDE, weight), "factor", [(k, k), (1, k)], [], own, other, local
    )
    return out, growth[0]


def pick(flag, first, second):
    return jnp.where(flag, first, second)


def roll(x, shift):
    return pltpu.roll(x, shift % LANES, 1)


def lane_index(like):
    return lax.broadcasted_iota(jnp.int32, like.shape, like.ndim - 1)


def chunk(g, height):
    return pl.ds(pl.multiple_of(g * height, height), height)


def own_rows(tangents, g, height):
    return [[tangents[f, pl.ds(g * height * SUB + r, height, stride=SUB), :] for r in range(SUB)] for f in range(2)]


def own_coeffs(coeff_self, coeff_cross):
    return [[spread_row(ref[...], r) for r in range(SUB)] for ref in (coeff_self, coeff_cross)]


def tall(x, height):
    return jnp.concatenate([x] * (height // SUB), axis=0)


def edge_kernel(fields, height, tangents_hbm, self_hbm, cross_hbm, last_out, first_out, near, far, near_fast, far_fast, tangents, coeff_self, coeff_cross, sems):
    chunks = fields // height
    span = height * SUB
    loads = [
        pltpu.make_async_copy(tangents_hbm.at[:, pl.ds(g * span, span), :], tangents.at[:, pl.ds(g * span, span), :], sems.at[g])
        for g in range(chunks)
    ]
    small = [
        pltpu.make_async_copy(src, dst, sems.at[chunks + i])
        for i, (src, dst) in enumerate(((self_hbm, coeff_self), (cross_hbm, coeff_cross)))
    ]
    for load in loads + small:
        load.start()
    odd = lax.axis_index("tile") % 2 == 1

    def send(at, rows):
        cell = lane_index(rows[0][0]) // SUB
        cells = LANES // SUB
        last, first = None, None
        for f in range(2):
            for r in range(SUB):
                s = f * SUB + r
                turned = roll(rows[f][r], (s + 1) * SUB)
                last = turned if last is None else jnp.where(cell == s, turned, last)
                first = turned if first is None else jnp.where(cell == (s + 1) % cells, turned, first)
        first = roll(first, -SUB)
        last_out[at, :] = last
        first_out[at, :] = first
        half = cell % SUB < STEPS
        to_above = jnp.where(half, last, roll(first, STEPS * SUB))
        to_below = jnp.where(half, roll(last, -STEPS * SUB), first)
        near[0, at, :] = pick(odd, to_above, to_below)
        far[0, at, :] = pick(odd, to_below, to_above)
        for f in range(2):
            count = STEPS - f
            for j in range(count):
                top, bottom = rows[f][j], rows[f][SUB - count + j]
                (near if f else near_fast)[j + f, at, :] = pick(odd, top, bottom)
                (far if f else far_fast)[j + f, at, :] = pick(odd, bottom, top)

    for g, load in enumerate(loads):
        load.wait()
        send(pl.ds(g * height, height), own_rows(tangents, g, height))
    for load in small:
        load.wait()
    send(pl.ds(fields, SUB), own_coeffs(coeff_self, coeff_cross))


def column_kernel(last, first, near, far, strips, near_out, far_out, outer):
    tile, tiles = lax.axis_index("tile"), lax.axis_size("tile")
    odd, at_top, at_bottom = tile % 2 == 1, tile == 0, tile == tiles - 1
    grp_odd = lax.axis_index("grp") % 2 == 1
    one, two = near[0], far[0]
    lane = lane_index(one)
    cell, low, inner = lane // SUB % SUB, lane < LANES // 2, lane % SUB < STEPS
    half = cell < STEPS
    above, below = pick(odd, one, two), pick(odd, two, one)
    outer[0] = jnp.where(half, below, roll(above, STEPS * SUB))
    outer[1] = jnp.where(half, roll(below, -STEPS * SUB), above)

    @pl.when(at_top | at_bottom)
    def _():
        outside = (half & at_bottom) | (~half & at_top)
        for i, ref in enumerate((last, first)):
            own = ref[...]
            mirrored = roll(own, -7 * SUB)
            for s in range(1, SUB):
                mirrored = jnp.where(cell == s, roll(own, (2 * s - 7) * SUB), mirrored)
            outer[i] = jnp.where(outside, mirrored, outer[i])

    sides = []
    for i, ref in enumerate((last, first)):
        own, more = ref[...], outer[i]
        fast = jnp.where(low, own, roll(more, LANES // 2))
        slow = jnp.where(low, roll(own, LANES // 2), more)
        strips[2 * i] = fast
        strips[2 * i + 1] = slow
        sides.append((fast, slow))
    to_left = jnp.where(inner, sides[1][0], roll(sides[1][1], STEPS))
    to_right = jnp.where(inner, roll(sides[0][0], -STEPS), sides[0][1])
    near_out[...] = pick(grp_odd, to_left, to_right)
    far_out[...] = pick(grp_odd, to_right, to_left)


def strip_neighbours(last, first, halo):
    c = lane_index(last) % SUB
    end, begin = c == SUB - 1, c == 0
    out = []
    for x, after, before in (
        (last, roll(halo, 7), None),
        (first, None, roll(halo, -7)),
        (halo, roll(first, 7), roll(last, -7)),
    ):
        right, left = roll(x, -1), roll(x, 1)
        if after is not None:
            right = jnp.where(end, after, right)
        if before is not None:
            left = jnp.where(begin, before, left)
        out.append(roll(x, SUB) + roll(x, -SUB) + right + left)
    return out


def advance(fast, slow, around, gain, cross):
    return gain * fast + diffusion * around + cross * slow


def relax(fast, slow):
    return (1.0 - slow_rate) * slow + slow_rate * fast


def gram_kernel(fields, height, cells, strips, near, far, gram, halo, ends):
    grp, grps = lax.axis_index("grp"), lax.axis_size("grp")
    grp_odd = grp % 2 == 1
    one, two = near[...], far[...]
    lane = lane_index(one)
    c = lane % SUB
    inner = c < STEPS
    left, right = pick(grp_odd, one, two), pick(grp_odd, two, one)
    halo[0] = jnp.where(inner, right, roll(left, STEPS))
    halo[1] = jnp.where(inner, roll(right, -STEPS), left)

    @pl.when((grp == 0) | (grp == grps - 1))
    def _():
        after, before = inner & (grp == grps - 1), ~inner & (grp == 0)
        for f in range(2):
            tail, start = strips[f], strips[2 + f]
            mirrored = halo[f]
            for s in range(STEPS):
                mirrored = jnp.where(after & (c == s), roll(tail, 2 * s - 7), mirrored)
                mirrored = jnp.where(before & (c == 7 - s), roll(start, 7 - 2 * s), mirrored)
            halo[f] = mirrored

    def parts(f, at):
        return [strips[f, at, :], strips[2 + f, at, :], halo[f, at, :]]

    gains = [tall(x + (1.0 - 4.0 * diffusion), height) for x in parts(0, pl.ds(fields, SUB))]
    crosses = [tall(x, height) for x in parts(1, pl.ds(fields, SUB))]

    @pl.loop(0, fields // height)
    def _(g):
        fast, slow = parts(0, chunk(g, height)), parts(1, chunk(g, height))
        for step in range(STEPS):
            around = strip_neighbours(*fast)
            moved = [advance(fast[p], slow[p], around[p], gains[p], crosses[p]) for p in range(3)]
            slow = [relax(a, b) for a, b in zip(fast, slow)]
            fast = moved
        l = lane_index(fast[0])
        joined = [jnp.where(l % SUB < STEPS, s[1], s[0]) for s in (fast, slow)]
        ends[chunk(g, height), :] = jnp.where(l < LANES // 2, joined[0], roll(joined[1], LANES // 2))

    whole = dot_nt(cells[...], cells[...]) + dot_nt(ends[...], ends[...])
    for index, (i, j) in enumerate(block_pairs(fields // SIDE)):
        row, half = divmod(index, 2)
        gram[row * SIDE:(row + 1) * SIDE, half * SIDE:(half + 1) * SIDE] = whole[
            i * SIDE:(i + 1) * SIDE, j * SIDE:(j + 1) * SIDE
        ]


def extended_rows(own, near, far, near_fast, far_fast, at):
    tile, tiles = lax.axis_index("tile"), lax.axis_size("tile")
    odd, at_top, at_bottom = tile % 2 == 1, tile == 0, tile == tiles - 1
    out = []
    for f in range(2):
        count = STEPS - f
        rows = dict(enumerate(own[f]))
        for j in range(count):
            one, two = ((near if f else near_fast)[j + f, at, :], (far if f else far_fast)[j + f, at, :])
            rows[j - count] = pick(at_top, own[f][count - 1 - j], pick(odd, one, two))
            rows[SUB + j] = pick(at_bottom, own[f][SUB - 1 - j], pick(odd, two, one))
        out.append(rows)
    return out


def evolve_kernel(fields, height, tangents, coeff_self, coeff_cross, near, far, near_fast, far_fast, cells, row_coeffs):
    coeff_rows = extended_rows(own_coeffs(coeff_self, coeff_cross), near, far, near_fast, far_fast, pl.ds(fields, SUB))
    for f in range(2):
        for r in range(1 - STEPS, SUB + STEPS - 1):
            row_coeffs[f, r + STEPS - 1, :, :] = coeff_rows[f][r] + (1.0 - 4.0 * diffusion) * (1 - f)

    @pl.loop(0, fields // height)
    def _(g):
        at = chunk(g, height)
        fast, slow = extended_rows(own_rows(tangents, g, height), near, far, near_fast, far_fast, at)
        for step in range(1, STEPS + 1):
            margin = STEPS - step
            new_fast = {}
            for r in range(-margin, SUB + margin):
                around = fast[r - 1] + fast[r + 1] + roll(fast[r], 1) + roll(fast[r], -1)
                gain, cross = (tall(row_coeffs[f, r + STEPS - 1], height) for f in range(2))
                new_fast[r] = advance(fast[r], slow[r], around, gain, cross)
            keep = max(margin - 1, 0)
            slow = {r: relax(fast[r], slow[r]) for r in range(-keep, SUB + keep)}
            fast = new_fast
        lane = lane_index(fast[0])
        middle = (lane >= STEPS) & (lane < LANES - STEPS)
        for f, rows in enumerate((fast, slow)):
            for r in range(SUB):
                cells[at, (f * SUB + r) * LANES:(f * SUB + r + 1) * LANES] = jnp.where(middle, rows[r], 0.0)


def local_call(body, name, out_shapes, scratch, *args, hbm=False, vmem=VMEM_BYTES):
    spec = pl.BlockSpec(memory_space=pltpu.VMEM)
    return pl.pallas_call(
        body,
        out_shape=[jax.ShapeDtypeStruct(s, jnp.float32) for s in out_shapes],
        in_specs=[pl.BlockSpec(memory_space=pltpu.HBM) if hbm else spec] * len(args),
        out_specs=[spec] * len(out_shapes),
        scratch_shapes=[pltpu.VMEM(s, jnp.float32) if isinstance(s, tuple) else s for s in scratch],
        compiler_params=pltpu.CompilerParams(vmem_limit_bytes=vmem),
        name=name,
    )(*args)


def swap(cells, axis, first, close=False):
    count = lax.axis_size(axis)
    pairs = [(i, i + 1) for i in range(first, count - 1, 2)]
    if close and first:
        pairs.append((0, count - 1))
    return lax.ppermute(cells, axis, pairs + [(b, a) for a, b in pairs])


def exchange(cells, grp_bit, tile_bit):
    grps, tiles = lax.axis_size("grp"), lax.axis_size("tile")
    moves = [(g * tiles + t, (g ^ grp_bit) * tiles + (t ^ tile_bit)) for g in range(grps) for t in range(tiles)]
    return lax.ppermute(cells, ("grp", "tile"), moves)


def parity():
    bits = lax.axis_index("grp") ^ lax.axis_index("tile")
    shift = 1
    while shift < max(lax.axis_size("grp"), lax.axis_size("tile")):
        bits = bits ^ (bits >> shift)
        shift *= 2
    return (bits & 1) == 1


def sum_blocks(packed):
    half = packed.shape[0] // 2
    high_half = parity()
    low, high = packed[:half], packed[half:]
    part = jnp.where(high_half, high, low) + exchange(jnp.where(high_half, low, high), 0, 1)
    for axis in ("grp", "tile"):
        bit = 1 if axis == "grp" else 2
        while bit < lax.axis_size(axis):
            part = part + (exchange(part, bit, 1) if axis == "grp" else exchange(part, 0, bit + 1))
            bit *= 2
    return part, exchange(part, 0, 1)


def per_device(tangents, reaction_self, reaction_cross):
    fields = tangents.shape[1]
    padded = fields + SUB
    rows = tangents.reshape(2, fields * tangents.shape[2], tangents.shape[3])
    message, strip = (STEPS, padded, LANES), (padded, LANES)
    inputs = (rows, reaction_self, reaction_cross)
    last, first, near, far, near_fast, far_fast = local_call(
        functools.partial(edge_kernel, fields, HEIGHT_EDGE), "edges", [strip] * 2 + [message] * 4,
        [a.shape for a in inputs] + [pltpu.SemaphoreType.DMA((fields // HEIGHT_EDGE + 2,))], *inputs,
        hbm=True, vmem=EDGE_VMEM_BYTES,
    )
    near, far = swap(near, "tile", 0), swap(far, "tile", 1)
    near_fast, far_fast = swap(near_fast, "tile", 0), swap(far_fast, "tile", 1)
    strips, near_cols, far_cols = local_call(
        column_kernel, "columns", [(4,) + strip, strip, strip], [(2,) + strip], last, first, near, far
    )
    near_cols, far_cols = swap(near_cols, "grp", 0), swap(far_cols, "grp", 1, close=True)
    (cells,) = local_call(
        functools.partial(evolve_kernel, fields, HEIGHT_EVOLVE), "evolve", [(fields, 2 * SUB * LANES)],
        [(2, SUB + 2 * STEPS - 2, SUB, LANES)], *inputs, near, far, near_fast, far_fast,
    )
    side_blocks = fields // SIDE
    blocks = side_blocks * (side_blocks + 1) // 2
    (packed,) = local_call(
        functools.partial(gram_kernel, fields, HEIGHT_STRIP), "gram", [((blocks + 1) // 2 * SIDE, 2 * SIDE)],
        [(2,) + strip, (fields, LANES)], cells, strips, near_cols, far_cols,
    )
    block_total = lax.axis_size("grp") * lax.axis_size("tile")
    corrections, growth = factor_call(*sum_blocks(packed), packed, fields, math.sqrt(block_total))
    return (corrections, growth)


def solution(mesh):
    in_specs = (P(None, None, "tile", "grp"), P("tile", "grp"), P("tile", "grp"))
    out_specs = (P(("grp", "tile"), None), P())
    return jax.shard_map(
        per_device, mesh=mesh, in_specs=in_specs, out_specs=out_specs, check_vma=False
    )
```

```python
import functools
import math

import jax
import jax.numpy as jnp
from jax import lax
from jax.experimental import pallas as pl
from jax.experimental.pallas import tpu as pltpu
from jax.sharding import PartitionSpec as P


STEPS = 4
diffusion = 0.2
slow_rate = 0.05
HEIGHT_EDGE = 96
HEIGHT_STRIP = 192
HEIGHT_EVOLVE = 48
SIDE = 64
VMEM_BYTES = 24 * 1024 * 1024
EDGE_VMEM_BYTES = 52 * 1024 * 1024
LANES = 128
SUB = 8
HI = lax.Precision.HIGHEST

def dot_nn(a, b):
    return lax.dot_general(a, b, (((1,), (0,)), ((), ())), precision=HI, preferred_element_type=jnp.float32)
def dot_tn(a, b):
    return lax.dot_general(a, b, (((0,), (0,)), ((), ())), precision=HI, preferred_element_type=jnp.float32)
def dot_nt(a, b):
    return lax.dot_general(a, b, (((1,), (1,)), ((), ())), precision=HI, preferred_element_type=jnp.float32)

def block_pairs(n):
    return [(i, j) for i in range(n) for j in range(i, n)]

def unpack_blocks(packed, n):
    out = {}
    for index, key in enumerate(block_pairs(n)):
        row, half = divmod(index, 2)
        out[key] = packed[row*SIDE:(row+1)*SIDE, half*SIDE:(half+1)*SIDE]
    return out

def spread_lane(x, lane):
    return jnp.broadcast_to(x[:, lane:lane+1], (x.shape[0], LANES))
def spread_row(x, row):
    return jnp.broadcast_to(x[row:row+1, :], (SUB, x.shape[1]))

def factor_blocks(blocks):
    groups = SIDE // SUB
    eye = (lax.broadcasted_iota(jnp.int32, (SIDE, SIDE), 0) == lax.broadcasted_iota(jnp.int32, (SIDE, SIDE), 1)).astype(jnp.float32)
    sub = lax.broadcasted_iota(jnp.int32, (SUB, LANES), 0)
    states = []
    for d in blocks:
        whole = jnp.concatenate([d, eye], axis=1)
        states.append([whole[g*SUB:(g+1)*SUB] for g in range(groups)])
    done = [[] for _ in blocks]
    for p in range(groups):
        for s, v in enumerate(states):
            cols = {}
            for g in range(p, groups):
                for c in range(SUB):
                    cols[g, c] = spread_lane(v[g], p*SUB + c)
            rows = [spread_row(v[p], c) for c in range(SUB)]
            pivots = {(a, c): spread_row(cols[p, c], a) for c in range(SUB) for a in range(c, SUB)}
            mult = {}
            scale = []
            for c in range(SUB):
                inv = 1.0 / pivots[c, c]
                scale.append(lax.rsqrt(pivots[c, c]))
                for a in range(c + 1, SUB):
                    mult[a, c] = pivots[a, c] * inv
                    rows[a] = rows[a] - mult[a, c] * rows[c]
                    for b in range(c + 1, a + 1):
                        pivots[a, b] = pivots[a, b] - mult[a, c] * pivots[b, c]
            scaled = [rows[c] * scale[c] for c in range(SUB)]
            panel = scaled[0]
            for c in range(1, SUB):
                panel = jnp.where(sub == c, scaled[c], panel)
            done[s].append(panel)
            if p + 1 == groups:
                continue
            near = [cols[p + 1, c] for c in range(SUB)]
            for c in range(SUB):
                for a in range(c + 1, SUB):
                    near[a] = near[a] - mult[a, c] * near[c]
                v[p + 1] = v[p + 1] - (near[c] * scale[c]) * scaled[c]
            whole = [scaled[c] * scale[c] for c in range(SUB)]
            for c in reversed(range(SUB)):
                for a in range(c):
                    whole[a] = whole[a] - mult[c, a] * whole[c]
            for g in range(p + 2, groups):
                for c in range(SUB):
                    v[g] = v[g] - cols[g, c] * whole[c]
    out = []
    for panels in done:
        whole = jnp.concatenate(panels, axis=0)
        out.append((whole[:, :SIDE], whole[:, SIDE:]))
    return out

def factor_kernel(n, weight, own_ref, other_ref, loc_ref, out_ref, growth_ref):
    high_half = parity()
    own, other = own_ref[...], other_ref[...]
    total = unpack_blocks(jnp.concatenate([jnp.where(high_half, other, own), jnp.where(high_half, own, other)], axis=0), n)
    local = unpack_blocks(loc_ref[...], n)
    keep = (lax.broadcasted_iota(jnp.int32, (SIDE, SIDE), 0) <= lax.broadcasted_iota(jnp.int32, (SIDE, SIDE), 1))
    diag = (lax.broadcasted_iota(jnp.int32, (SIDE, SIDE), 0) == lax.broadcasted_iota(jnp.int32, (SIDE, SIDE), 1))
    rest = {j: [] for j in range(n)}
    for k in range(n):
        (r_t, i_t), (r_l, i_l) = factor_blocks([total[k, k], local[k, k]])
        growth_ref[0, k*SIDE:(k+1)*SIDE] = jnp.log(jnp.sum(jnp.where(diag, r_t, 0.0), axis=0))
        panels = []
        for grams, inv in ((total, i_t), (local, i_l)):
            if k + 1 < n:
                row = dot_nn(inv, jnp.concatenate([grams[k, j] for j in range(k + 1, n)], axis=1))
                for i in range(k + 1, n):
                    less = dot_tn(row[:, (i-k-1)*SIDE:(i-k)*SIDE], row[:, (i-k-1)*SIDE:])
                    for j in range(i, n):
                        grams[i, j] = grams[i, j] - less[:, (j-i)*SIDE:(j-i+1)*SIDE]
                panels.append(row)
        rest[k].append(jnp.where(keep, r_l, 0.0))
        answer = dot_nt(jnp.concatenate(rest[k], axis=0), i_t)
        out_ref[:(k+1)*SIDE, k*SIDE:(k+1)*SIDE] = weight * answer
        if k + 1 < n:
            out_ref[(k+1)*SIDE:, k*SIDE:(k+1)*SIDE] = jnp.zeros(((n-k-1)*SIDE, SIDE), jnp.float32)
            less = dot_nn(answer, panels[0])
            for j in range(k + 1, n):
                at = (j-k-1)*SIDE
                rest[j].append(panels[1][:, at:at+SIDE])
                rest[j] = [part - less[i*SIDE:(i+1)*SIDE, at:at+SIDE] for i, part in enumerate(rest[j])]


def factor_call(own, other, local, k, weight):
    out, growth = local_call(
        functools.partial(factor_kernel, k // SIDE, weight), "factor", [(k, k), (1, k)], [], own, other, local
    )
    return out, growth[0]


def pick(flag, first, second):
    return jnp.where(flag, first, second)


def roll(x, shift):
    return pltpu.roll(x, shift % LANES, 1)


def lane_index(like):
    return lax.broadcasted_iota(jnp.int32, like.shape, like.ndim - 1)


def chunk(g, height):
    return pl.ds(pl.multiple_of(g * height, height), height)


def own_rows(tangents, g, height):
    return [[tangents[f, pl.ds(g * height * SUB + r, height, stride=SUB), :] for r in range(SUB)] for f in range(2)]


def own_coeffs(coeff_self, coeff_cross):
    return [[spread_row(ref[...], r) for r in range(SUB)] for ref in (coeff_self, coeff_cross)]


def tall(x, height):
    return jnp.concatenate([x] * (height // SUB), axis=0)


def edge_kernel(fields, height, tangents_hbm, self_hbm, cross_hbm, last_out, first_out, near, far, near_fast, far_fast, tangents, coeff_self, coeff_cross, sems):
    chunks = fields // height
    span = height * SUB
    loads = [
        pltpu.make_async_copy(tangents_hbm.at[:, pl.ds(g * span, span), :], tangents.at[:, pl.ds(g * span, span), :], sems.at[g])
        for g in range(chunks)
    ]
    small = [
        pltpu.make_async_copy(src, dst, sems.at[chunks + i])
        for i, (src, dst) in enumerate(((self_hbm, coeff_self), (cross_hbm, coeff_cross)))
    ]
    for load in loads + small:
        load.start()
    odd = lax.axis_index("tile") % 2 == 1

    def send(at, rows):
        cell = lane_index(rows[0][0]) // SUB
        cells = LANES // SUB
        last, first = None, None
        for f in range(2):
            for r in range(SUB):
                s = f * SUB + r
                turned = roll(rows[f][r], (s + 1) * SUB)
                last = turned if last is None else jnp.where(cell == s, turned, last)
                first = turned if first is None else jnp.where(cell == (s + 1) % cells, turned, first)
        first = roll(first, -SUB)
        last_out[at, :] = last
        first_out[at, :] = first
        half = cell % SUB < STEPS
        to_above = jnp.where(half, last, roll(first, STEPS * SUB))
        to_below = jnp.where(half, roll(last, -STEPS * SUB), first)
        near[0, at, :] = pick(odd, to_above, to_below)
        far[0, at, :] = pick(odd, to_below, to_above)
        for f in range(2):
            count = STEPS - f
            for j in range(count):
                top, bottom = rows[f][j], rows[f][SUB - count + j]
                (near if f else near_fast)[j + f, at, :] = pick(odd, top, bottom)
                (far if f else far_fast)[j + f, at, :] = pick(odd, bottom, top)

    for g, load in enumerate(loads):
        load.wait()
        send(pl.ds(g * height, height), own_rows(tangents, g, height))
    for load in small:
        load.wait()
    send(pl.ds(fields, SUB), own_coeffs(coeff_self, coeff_cross))


def column_kernel(last, first, near, far, strips, near_out, far_out, outer):
    tile, tiles = lax.axis_index("tile"), lax.axis_size("tile")
    odd, at_top, at_bottom = tile % 2 == 1, tile == 0, tile == tiles - 1
    grp_odd = lax.axis_index("grp") % 2 == 1
    one, two = near[0], far[0]
    lane = lane_index(one)
    cell, low, inner = lane // SUB % SUB, lane < LANES // 2, lane % SUB < STEPS
    half = cell < STEPS
    above, below = pick(odd, one, two), pick(odd, two, one)
    outer[0] = jnp.where(half, below, roll(above, STEPS * SUB))
    outer[1] = jnp.where(half, roll(below, -STEPS * SUB), above)

    @pl.when(at_top | at_bottom)
    def _():
        outside = (half & at_bottom) | (~half & at_top)
        for i, ref in enumerate((last, first)):
            own = ref[...]
            mirrored = roll(own, -7 * SUB)
            for s in range(1, SUB):
                mirrored = jnp.where(cell == s, roll(own, (2 * s - 7) * SUB), mirrored)
            outer[i] = jnp.where(outside, mirrored, outer[i])

    sides = []
    for i, ref in enumerate((last, first)):
        own, more = ref[...], outer[i]
        fast = jnp.where(low, own, roll(more, LANES // 2))
        slow = jnp.where(low, roll(own, LANES // 2), more)
        strips[2 * i] = fast
        strips[2 * i + 1] = slow
        sides.append((fast, slow))
    to_left = jnp.where(inner, sides[1][0], roll(sides[1][1], STEPS))
    to_right = jnp.where(inner, roll(sides[0][0], -STEPS), sides[0][1])
    near_out[...] = pick(grp_odd, to_left, to_right)
    far_out[...] = pick(grp_odd, to_right, to_left)


def strip_neighbours(last, first, halo, wanted):
    c = lane_index(last) % SUB
    end, begin = c == SUB - 1, c == 0
    out = []
    sides = (lambda: (last, roll(halo, 7), None), lambda: (first, None, roll(halo, -7)), lambda: (halo, roll(first, 7), roll(last, -7)))
    for side in sides[:wanted]:
        x, after, before = side()
        right, left = roll(x, -1), roll(x, 1)
        if after is not None:
            right = jnp.where(end, after, right)
        if before is not None:
            left = jnp.where(begin, before, left)
        out.append(roll(x, SUB) + roll(x, -SUB) + right + left)
    return out


def advance(fast, slow, around, gain, cross):
    return gain * fast + diffusion * around + cross * slow


def relax(fast, slow):
    return (1.0 - slow_rate) * slow + slow_rate * fast


def gram_kernel(fields, height, middle_gram, strips, near, far, gram, halo, ends):
    grp, grps = lax.axis_index("grp"), lax.axis_size("grp")
    grp_odd = grp % 2 == 1
    one, two = near[...], far[...]
    lane = lane_index(one)
    c = lane % SUB
    inner = c < STEPS
    left, right = pick(grp_odd, one, two), pick(grp_odd, two, one)
    halo[0] = jnp.where(inner, right, roll(left, STEPS))
    halo[1] = jnp.where(inner, roll(right, -STEPS), left)

    @pl.when((grp == 0) | (grp == grps - 1))
    def _():
        after, before = inner & (grp == grps - 1), ~inner & (grp == 0)
        for f in range(2):
            tail, start = strips[f], strips[2 + f]
            mirrored = halo[f]
            for s in range(STEPS):
                mirrored = jnp.where(after & (c == s), roll(tail, 2 * s - 7), mirrored)
                mirrored = jnp.where(before & (c == 7 - s), roll(start, 7 - 2 * s), mirrored)
            halo[f] = mirrored

    def parts(f, at):
        return [strips[f, at, :], strips[2 + f, at, :], halo[f, at, :]]

    gains = [tall(x + (1.0 - 4.0 * diffusion), height) for x in parts(0, pl.ds(fields, SUB))]
    crosses = [tall(x, height) for x in parts(1, pl.ds(fields, SUB))]

    @pl.loop(0, fields // height)
    def _(g):
        fast, slow = parts(0, chunk(g, height)), parts(1, chunk(g, height))
        for step in range(STEPS):
            wanted = 3 if step + 1 < STEPS else 2
            around = strip_neighbours(*fast, wanted)
            moved = [advance(fast[p], slow[p], around[p], gains[p], crosses[p]) for p in range(wanted)]
            slow = [relax(fast[p], slow[p]) for p in range(wanted)]
            fast = moved
        l = lane_index(fast[0])
        joined = [jnp.where(l % SUB < STEPS, s[1], s[0]) for s in (fast, slow)]
        ends[chunk(g, height), :] = jnp.where(l < LANES // 2, joined[0], roll(joined[1], LANES // 2))

    whole = middle_gram[...] + dot_nt(ends[...], ends[...])
    for index, (i, j) in enumerate(block_pairs(fields // SIDE)):
        row, half = divmod(index, 2)
        gram[row * SIDE:(row + 1) * SIDE, half * SIDE:(half + 1) * SIDE] = whole[
            i * SIDE:(i + 1) * SIDE, j * SIDE:(j + 1) * SIDE
        ]


def extended_rows(own, near, far, near_fast, far_fast, at):
    tile, tiles = lax.axis_index("tile"), lax.axis_size("tile")
    odd, at_top, at_bottom = tile % 2 == 1, tile == 0, tile == tiles - 1
    out = []
    for f in range(2):
        count = STEPS - f
        rows = dict(enumerate(own[f]))
        for j in range(count):
            one, two = ((near if f else near_fast)[j + f, at, :], (far if f else far_fast)[j + f, at, :])
            rows[j - count] = pick(at_top, own[f][count - 1 - j], pick(odd, one, two))
            rows[SUB + j] = pick(at_bottom, own[f][SUB - 1 - j], pick(odd, two, one))
        out.append(rows)
    return out


def evolve_kernel(fields, height, tangents, coeff_self, coeff_cross, near, far, near_fast, far_fast, middle_gram, row_coeffs, cells):
    coeff_rows = extended_rows(own_coeffs(coeff_self, coeff_cross), near, far, near_fast, far_fast, pl.ds(fields, SUB))
    for f in range(2):
        for r in range(1 - STEPS, SUB + STEPS - 1):
            row_coeffs[f, r + STEPS - 1, :, :] = coeff_rows[f][r] + (1.0 - 4.0 * diffusion) * (1 - f)

    @pl.loop(0, fields // height)
    def _(g):
        at = chunk(g, height)
        fast, slow = extended_rows(own_rows(tangents, g, height), near, far, near_fast, far_fast, at)
        for step in range(1, STEPS + 1):
            margin = STEPS - step
            new_fast = {}
            for r in range(-margin, SUB + margin):
                around = fast[r - 1] + fast[r + 1] + roll(fast[r], 1) + roll(fast[r], -1)
                gain, cross = (tall(row_coeffs[f, r + STEPS - 1], height) for f in range(2))
                new_fast[r] = advance(fast[r], slow[r], around, gain, cross)
            keep = max(margin - 1, 0)
            slow = {r: relax(fast[r], slow[r]) for r in range(-keep, SUB + keep)}
            fast = new_fast
        lane = lane_index(fast[0])
        middle = (lane >= STEPS) & (lane < LANES - STEPS)
        for f, rows in enumerate((fast, slow)):
            for r in range(SUB):
                cells[at, (f * SUB + r) * LANES:(f * SUB + r + 1) * LANES] = jnp.where(middle, rows[r], 0.0)

    middle_gram[...] = dot_nt(cells[...], cells[...])


def local_call(body, name, out_shapes, scratch, *args, hbm=False, vmem=VMEM_BYTES):
    spec = pl.BlockSpec(memory_space=pltpu.VMEM)
    return pl.pallas_call(
        body,
        out_shape=[jax.ShapeDtypeStruct(s, jnp.float32) for s in out_shapes],
        in_specs=[pl.BlockSpec(memory_space=pltpu.HBM) if hbm else spec] * len(args),
        out_specs=[spec] * len(out_shapes),
        scratch_shapes=[pltpu.VMEM(s, jnp.float32) if isinstance(s, tuple) else s for s in scratch],
        compiler_params=pltpu.CompilerParams(vmem_limit_bytes=vmem),
        name=name,
    )(*args)


def swap(cells, axis, first, close=False):
    count = lax.axis_size(axis)
    pairs = [(i, i + 1) for i in range(first, count - 1, 2)]
    if close and first:
        pairs.append((0, count - 1))
    return lax.ppermute(cells, axis, pairs + [(b, a) for a, b in pairs])


def exchange(cells, grp_bit, tile_bit):
    grps, tiles = lax.axis_size("grp"), lax.axis_size("tile")
    moves = [(g * tiles + t, (g ^ grp_bit) * tiles + (t ^ tile_bit)) for g in range(grps) for t in range(tiles)]
    return lax.ppermute(cells, ("grp", "tile"), moves)


def parity():
    bits = lax.axis_index("grp") ^ lax.axis_index("tile")
    shift = 1
    while shift < max(lax.axis_size("grp"), lax.axis_size("tile")):
        bits = bits ^ (bits >> shift)
        shift *= 2
    return (bits & 1) == 1


def sum_blocks(packed):
    half = packed.shape[0] // 2
    high_half = parity()
    low, high = packed[:half], packed[half:]
    part = jnp.where(high_half, high, low) + exchange(jnp.where(high_half, low, high), 0, 1)
    for axis in ("grp", "tile"):
        bit = 1 if axis == "grp" else 2
        while bit < lax.axis_size(axis):
            part = part + (exchange(part, bit, 1) if axis == "grp" else exchange(part, 0, bit + 1))
            bit *= 2
    return part, exchange(part, 0, 1)


def per_device(tangents, reaction_self, reaction_cross):
    fields = tangents.shape[1]
    padded = fields + SUB
    rows = tangents.reshape(2, fields * tangents.shape[2], tangents.shape[3])
    message, strip = (STEPS, padded, LANES), (padded, LANES)
    inputs = (rows, reaction_self, reaction_cross)
    last, first, near, far, near_fast, far_fast = local_call(
        functools.partial(edge_kernel, fields, HEIGHT_EDGE), "edges", [strip] * 2 + [message] * 4,
        [a.shape for a in inputs] + [pltpu.SemaphoreType.DMA((fields // HEIGHT_EDGE + 2,))], *inputs,
        hbm=True, vmem=EDGE_VMEM_BYTES,
    )
    near, far = swap(near, "tile", 0), swap(far, "tile", 1)
    near_fast, far_fast = swap(near_fast, "tile", 0), swap(far_fast, "tile", 1)
    strips, near_cols, far_cols = local_call(
        column_kernel, "columns", [(4,) + strip, strip, strip], [(2,) + strip], last, first, near, far
    )
    far_cols = swap(far_cols, "grp", 1, close=True)
    near_cols = swap(near_cols, "grp", 0)
    (middle_gram,) = local_call(
        functools.partial(evolve_kernel, fields, HEIGHT_EVOLVE), "evolve", [(fields, fields)],
        [(2, SUB + 2 * STEPS - 2, SUB, LANES), (fields, 2 * SUB * LANES)], *inputs, near, far, near_fast, far_fast,
    )
    side_blocks = fields // SIDE
    blocks = side_blocks * (side_blocks + 1) // 2
    (packed,) = local_call(
        functools.partial(gram_kernel, fields, HEIGHT_STRIP), "gram", [((blocks + 1) // 2 * SIDE, 2 * SIDE)],
        [(2,) + strip, (fields, LANES)], middle_gram, strips, near_cols, far_cols,
    )
    block_total = lax.axis_size("grp") * lax.axis_size("tile")
    corrections, growth = factor_call(*sum_blocks(packed), packed, fields, math.sqrt(block_total))
    return (corrections, growth)


def solution(mesh):
    in_specs = (P(None, None, "tile", "grp"), P("tile", "grp"), P("tile", "grp"))
    out_specs = (P(("grp", "tile"), None), P())
    return jax.shard_map(
        per_device, mesh=mesh, in_specs=in_specs, out_specs=out_specs, check_vma=False
    )
```

```python
import functools
import math

import jax
import jax.numpy as jnp
from jax import lax
from jax.experimental import pallas as pl
from jax.experimental.pallas import tpu as pltpu
from jax.sharding import PartitionSpec as P


STEPS = 4
diffusion = 0.2
slow_rate = 0.05
HEIGHT_EDGE = 96
HEIGHT_STRIP = 192
HEIGHT_EVOLVE = 48
SIDE = 64
VMEM_BYTES = 24 * 1024 * 1024
LOCAL_COST = pl.CostEstimate(flops=10**9, bytes_accessed=10**6, transcendentals=0)
EDGE_VMEM_BYTES = 52 * 1024 * 1024
LANES = 128
SUB = 8
HI = lax.Precision.HIGHEST

def dot_nn(a, b):
    return lax.dot_general(a, b, (((1,), (0,)), ((), ())), precision=HI, preferred_element_type=jnp.float32)
def dot_tn(a, b):
    return lax.dot_general(a, b, (((0,), (0,)), ((), ())), precision=HI, preferred_element_type=jnp.float32)
def dot_nt(a, b):
    return lax.dot_general(a, b, (((1,), (1,)), ((), ())), precision=HI, preferred_element_type=jnp.float32)

def block_pairs(n):
    return [(i, j) for i in range(n) for j in range(i, n)]

def unpack_blocks(packed, n):
    out = {}
    for index, key in enumerate(block_pairs(n)):
        row, half = divmod(index, 2)
        out[key] = packed[row*SIDE:(row+1)*SIDE, half*SIDE:(half+1)*SIDE]
    return out

def spread_lane(x, lane):
    return jnp.broadcast_to(x[:, lane:lane+1], (x.shape[0], LANES))
def spread_row(x, row):
    return jnp.broadcast_to(x[row:row+1, :], (SUB, x.shape[1]))

def factor_blocks(blocks):
    groups = SIDE // SUB
    eye = (lax.broadcasted_iota(jnp.int32, (SIDE, SIDE), 0) == lax.broadcasted_iota(jnp.int32, (SIDE, SIDE), 1)).astype(jnp.float32)
    sub = lax.broadcasted_iota(jnp.int32, (SUB, LANES), 0)
    states = []
    for d in blocks:
        whole = jnp.concatenate([d, eye], axis=1)
        states.append([whole[g*SUB:(g+1)*SUB] for g in range(groups)])
    done = [[] for _ in blocks]
    ready = [None for _ in blocks]
    for p in range(groups):
        for s, v in enumerate(states):
            spread = {(g, c): spread_lane(v[g], p*SUB + c) for g in range(p + 1, groups) for c in range(SUB)}
            if p + 1 < groups:
                coming = [spread_lane(v[p + 1], (p + 1)*SUB + c) for c in range(SUB)]
            columns = ready[s] or [spread_lane(v[p], p*SUB + c) for c in range(SUB)]
            rows = [spread_row(v[p], c) for c in range(SUB)]
            pivots = {(a, c): spread_row(columns[c], a) for c in range(SUB) for a in range(c, SUB)}
            mult, inverses, scale = {}, [], []
            for c in range(SUB):
                inverses.append(1.0 / pivots[c, c])
                scale.append(lax.rsqrt(pivots[c, c]))
                for a in range(c + 1, SUB):
                    mult[a, c] = pivots[a, c] * inverses[c]
                    rows[a] = rows[a] - mult[a, c] * rows[c]
                    for b in range(c + 1, a + 1):
                        pivots[a, b] = pivots[a, b] - mult[a, c] * pivots[b, c]
            scaled = [rows[c] * scale[c] for c in range(SUB)]
            panel = scaled[0]
            for c in range(1, SUB):
                panel = jnp.where(sub == c, scaled[c], panel)
            done[s].append(panel)
            for g in range(p + 1, min(p + 3, groups)):
                cols = [spread[g, c] for c in range(SUB)]
                for c in range(SUB):
                    for a in range(c + 1, SUB):
                        cols[a] = cols[a] - mult[a, c] * cols[c]
                    if g == p + 1:
                        part = cols[c] * inverses[c]
                        coming = [x - part * spread_row(cols[c], b) for b, x in enumerate(coming)]
                    v[g] = v[g] - (cols[c] * scale[c]) * scaled[c]
                if g == p + 1:
                    ready[s] = coming
            if p + 3 < groups:
                solved = [scaled[c] * scale[c] for c in range(SUB)]
                for c in reversed(range(SUB)):
                    for a in range(c):
                        solved[a] = solved[a] - mult[c, a] * solved[c]
                for g in range(p + 3, groups):
                    for c in range(SUB):
                        v[g] = v[g] - spread[g, c] * solved[c]
    out = []
    for panels in done:
        whole = jnp.concatenate(panels, axis=0)
        out.append((whole[:, :SIDE], whole[:, SIDE:]))
    return out

def square_masks():
    row = lax.broadcasted_iota(jnp.int32, (SIDE, SIDE), 0)
    col = lax.broadcasted_iota(jnp.int32, (SIDE, SIDE), 1)
    return row <= col, row == col


def local_kernel(n, packed, gram, panel, *after):
    blocks = unpack_blocks(gram[...], n) if packed else {
        (i, j): gram[i*SIDE:(i+1)*SIDE, j*SIDE:(j+1)*SIDE] for i, j in block_pairs(n)
    }
    ((factor, inverse),) = factor_blocks([blocks[0, 0]])
    panel[:, :SIDE] = jnp.where(square_masks()[0], factor, 0.0)
    if n > 1:
        row = dot_nn(inverse, jnp.concatenate([blocks[0, j] for j in range(1, n)], axis=1))
        panel[:, SIDE:] = row
        less = dot_tn(row, row)
        for i, j in block_pairs(n - 1):
            at = (slice(i*SIDE, (i+1)*SIDE), slice(j*SIDE, (j+1)*SIDE))
            after[0][at] = blocks[i + 1, j + 1] - less[at]


def local_factor(packed, n):
    panels, left = [], packed
    for k in range(n):
        m = n - k
        shapes = [(SIDE, m*SIDE)] + ([((m-1)*SIDE, (m-1)*SIDE)] if m > 1 else [])
        panel, *left = local_call(functools.partial(local_kernel, m, k == 0), "local_factor", shapes, [], left, cost=LOCAL_COST)
        left = left[0] if left else None
        panels.append(panel)
    return panels


def factor_kernel(n, weight, own_ref, other_ref, *refs):
    local, (out_ref, growth_ref) = refs[:n], refs[n:]
    high_half = parity()
    own, other = own_ref[...], other_ref[...]
    total = unpack_blocks(jnp.concatenate([jnp.where(high_half, other, own), jnp.where(high_half, own, other)], axis=0), n)
    diag = square_masks()[1]
    rest = {j: [local[i][:, (j-i)*SIDE:(j-i+1)*SIDE] for i in range(j + 1)] for j in range(n)}
    for k in range(n):
        ((factor, inverse),) = factor_blocks([total[k, k]])
        growth_ref[0, k*SIDE:(k+1)*SIDE] = jnp.log(jnp.sum(jnp.where(diag, factor, 0.0), axis=0))
        if k + 1 < n:
            row = dot_nn(inverse, jnp.concatenate([total[k, j] for j in range(k + 1, n)], axis=1))
            for i in range(k + 1, n):
                less = dot_tn(row[:, (i-k-1)*SIDE:(i-k)*SIDE], row[:, (i-k-1)*SIDE:])
                for j in range(i, n):
                    total[i, j] = total[i, j] - less[:, (j-i)*SIDE:(j-i+1)*SIDE]
        answer = dot_nt(jnp.concatenate(rest[k], axis=0), inverse)
        out_ref[:(k+1)*SIDE, k*SIDE:(k+1)*SIDE] = weight * answer
        if k + 1 < n:
            out_ref[(k+1)*SIDE:, k*SIDE:(k+1)*SIDE] = jnp.zeros(((n-k-1)*SIDE, SIDE), jnp.float32)
            less = dot_nn(answer, row)
            for j in range(k + 1, n):
                at = (j-k-1)*SIDE
                rest[j] = [
                    part - less[i*SIDE:(i+1)*SIDE, at:at+SIDE] if i <= k else part for i, part in enumerate(rest[j])
                ]


def factor_call(own, other, local, k, weight):
    out, growth = local_call(
        functools.partial(factor_kernel, k // SIDE, weight), "factor", [(k, k), (1, k)], [], own, other, *local
    )
    return out, growth[0]


def pick(flag, first, second):
    return jnp.where(flag, first, second)


def roll(x, shift):
    return pltpu.roll(x, shift % LANES, 1)


def lane_index(like):
    return lax.broadcasted_iota(jnp.int32, like.shape, like.ndim - 1)


def chunk(g, height):
    return pl.ds(pl.multiple_of(g * height, height), height)


def own_rows(tangents, g, height):
    return [[tangents[f, pl.ds(g * height * SUB + r, height, stride=SUB), :] for r in range(SUB)] for f in range(2)]


def own_coeffs(coeff_self, coeff_cross):
    return [[spread_row(ref[...], r) for r in range(SUB)] for ref in (coeff_self, coeff_cross)]


def tall(x, height):
    return jnp.concatenate([x] * (height // SUB), axis=0)


def edge_kernel(fields, height, tangents_hbm, self_hbm, cross_hbm, last_out, first_out, near, far, near_fast, far_fast, tangents, coeff_self, coeff_cross, sems):
    chunks = fields // height
    span = height * SUB
    loads = [
        pltpu.make_async_copy(tangents_hbm.at[:, pl.ds(g * span, span), :], tangents.at[:, pl.ds(g * span, span), :], sems.at[g])
        for g in range(chunks)
    ]
    small = [
        pltpu.make_async_copy(src, dst, sems.at[chunks + i])
        for i, (src, dst) in enumerate(((self_hbm, coeff_self), (cross_hbm, coeff_cross)))
    ]
    for load in loads + small:
        load.start()
    odd = lax.axis_index("tile") % 2 == 1

    def send(at, rows):
        cell = lane_index(rows[0][0]) // SUB
        cells = LANES // SUB
        last, first = None, None
        for f in range(2):
            for r in range(SUB):
                s = f * SUB + r
                turned = roll(rows[f][r], (s + 1) * SUB)
                last = turned if last is None else jnp.where(cell == s, turned, last)
                first = turned if first is None else jnp.where(cell == (s + 1) % cells, turned, first)
        first = roll(first, -SUB)
        last_out[at, :] = last
        first_out[at, :] = first
        half = cell % SUB < STEPS
        to_above = jnp.where(half, last, roll(first, STEPS * SUB))
        to_below = jnp.where(half, roll(last, -STEPS * SUB), first)
        near[0, at, :] = pick(odd, to_above, to_below)
        far[0, at, :] = pick(odd, to_below, to_above)
        for f in range(2):
            count = STEPS - f
            for j in range(count):
                top, bottom = rows[f][j], rows[f][SUB - count + j]
                (near if f else near_fast)[j + f, at, :] = pick(odd, top, bottom)
                (far if f else far_fast)[j + f, at, :] = pick(odd, bottom, top)

    for g, load in enumerate(loads):
        load.wait()
        send(pl.ds(g * height, height), own_rows(tangents, g, height))
    for load in small:
        load.wait()
    send(pl.ds(fields, SUB), own_coeffs(coeff_self, coeff_cross))


def column_kernel(last, first, near, far, strips, near_out, far_out, outer):
    tile, tiles = lax.axis_index("tile"), lax.axis_size("tile")
    odd, at_top, at_bottom = tile % 2 == 1, tile == 0, tile == tiles - 1
    grp_odd = lax.axis_index("grp") % 2 == 1
    one, two = near[0], far[0]
    lane = lane_index(one)
    cell, low, inner = lane // SUB % SUB, lane < LANES // 2, lane % SUB < STEPS
    half = cell < STEPS
    above, below = pick(odd, one, two), pick(odd, two, one)
    outer[0] = jnp.where(half, below, roll(above, STEPS * SUB))
    outer[1] = jnp.where(half, roll(below, -STEPS * SUB), above)

    @pl.when(at_top | at_bottom)
    def _():
        outside = (half & at_bottom) | (~half & at_top)
        for i, ref in enumerate((last, first)):
            own = ref[...]
            mirrored = roll(own, -7 * SUB)
            for s in range(1, SUB):
                mirrored = jnp.where(cell == s, roll(own, (2 * s - 7) * SUB), mirrored)
            outer[i] = jnp.where(outside, mirrored, outer[i])

    sides = []
    for i, ref in enumerate((last, first)):
        own, more = ref[...], outer[i]
        fast = jnp.where(low, own, roll(more, LANES // 2))
        slow = jnp.where(low, roll(own, LANES // 2), more)
        strips[2 * i] = fast
        strips[2 * i + 1] = slow
        sides.append((fast, slow))
    to_left = jnp.where(inner, sides[1][0], roll(sides[1][1], STEPS))
    to_right = jnp.where(inner, roll(sides[0][0], -STEPS), sides[0][1])
    near_out[...] = pick(grp_odd, to_left, to_right)
    far_out[...] = pick(grp_odd, to_right, to_left)


def strip_neighbours(last, first, halo, wanted):
    c = lane_index(last) % SUB
    end, begin = c == SUB - 1, c == 0
    out = []
    sides = (lambda: (last, roll(halo, 7), None), lambda: (first, None, roll(halo, -7)), lambda: (halo, roll(first, 7), roll(last, -7)))
    for side in sides[:wanted]:
        x, after, before = side()
        right, left = roll(x, -1), roll(x, 1)
        if after is not None:
            right = jnp.where(end, after, right)
        if before is not None:
            left = jnp.where(begin, before, left)
        out.append(roll(x, SUB) + roll(x, -SUB) + right + left)
    return out


def advance(fast, slow, around, gain, cross):
    return gain * fast + diffusion * around + cross * slow


def relax(fast, slow):
    return (1.0 - slow_rate) * slow + slow_rate * fast


def gram_kernel(fields, height, middle_gram, strips, near, far, gram, halo, ends):
    grp, grps = lax.axis_index("grp"), lax.axis_size("grp")
    grp_odd = grp % 2 == 1
    one, two = near[...], far[...]
    lane = lane_index(one)
    c = lane % SUB
    inner = c < STEPS
    left, right = pick(grp_odd, one, two), pick(grp_odd, two, one)
    halo[0] = jnp.where(inner, right, roll(left, STEPS))
    halo[1] = jnp.where(inner, roll(right, -STEPS), left)

    @pl.when((grp == 0) | (grp == grps - 1))
    def _():
        after, before = inner & (grp == grps - 1), ~inner & (grp == 0)
        for f in range(2):
            tail, start = strips[f], strips[2 + f]
            mirrored = halo[f]
            for s in range(STEPS):
                mirrored = jnp.where(after & (c == s), roll(tail, 2 * s - 7), mirrored)
                mirrored = jnp.where(before & (c == 7 - s), roll(start, 7 - 2 * s), mirrored)
            halo[f] = mirrored

    def parts(f, at):
        return [strips[f, at, :], strips[2 + f, at, :], halo[f, at, :]]

    gains = [tall(x + (1.0 - 4.0 * diffusion), height) for x in parts(0, pl.ds(fields, SUB))]
    crosses = [tall(x, height) for x in parts(1, pl.ds(fields, SUB))]

    @pl.loop(0, fields // height)
    def _(g):
        fast, slow = parts(0, chunk(g, height)), parts(1, chunk(g, height))
        for step in range(STEPS):
            wanted = 3 if step + 1 < STEPS else 2
            around = strip_neighbours(*fast, wanted)
            moved = [advance(fast[p], slow[p], around[p], gains[p], crosses[p]) for p in range(wanted)]
            slow = [relax(fast[p], slow[p]) for p in range(wanted)]
            fast = moved
        l = lane_index(fast[0])
        joined = [jnp.where(l % SUB < STEPS, s[1], s[0]) for s in (fast, slow)]
        ends[chunk(g, height), :] = jnp.where(l < LANES // 2, joined[0], roll(joined[1], LANES // 2))

    whole = middle_gram[...] + dot_nt(ends[...], ends[...])
    for index, (i, j) in enumerate(block_pairs(fields // SIDE)):
        row, half = divmod(index, 2)
        gram[row * SIDE:(row + 1) * SIDE, half * SIDE:(half + 1) * SIDE] = whole[
            i * SIDE:(i + 1) * SIDE, j * SIDE:(j + 1) * SIDE
        ]


def extended_rows(own, near, far, near_fast, far_fast, at):
    tile, tiles = lax.axis_index("tile"), lax.axis_size("tile")
    odd, at_top, at_bottom = tile % 2 == 1, tile == 0, tile == tiles - 1
    out = []
    for f in range(2):
        count = STEPS - f
        rows = dict(enumerate(own[f]))
        for j in range(count):
            one, two = ((near if f else near_fast)[j + f, at, :], (far if f else far_fast)[j + f, at, :])
            rows[j - count] = pick(at_top, own[f][count - 1 - j], pick(odd, one, two))
            rows[SUB + j] = pick(at_bottom, own[f][SUB - 1 - j], pick(odd, two, one))
        out.append(rows)
    return out


def evolve_kernel(fields, height, tangents, coeff_self, coeff_cross, near, far, near_fast, far_fast, middle_gram, row_coeffs, cells):
    coeff_rows = extended_rows(own_coeffs(coeff_self, coeff_cross), near, far, near_fast, far_fast, pl.ds(fields, SUB))
    for f in range(2):
        for r in range(1 - STEPS, SUB + STEPS - 1):
            row_coeffs[f, r + STEPS - 1, :, :] = coeff_rows[f][r] + (1.0 - 4.0 * diffusion) * (1 - f)

    @pl.loop(0, fields // height)
    def _(g):
        at = chunk(g, height)
        fast, slow = extended_rows(own_rows(tangents, g, height), near, far, near_fast, far_fast, at)
        for step in range(1, STEPS + 1):
            margin = STEPS - step
            new_fast = {}
            for r in range(-margin, SUB + margin):
                around = fast[r - 1] + fast[r + 1] + roll(fast[r], 1) + roll(fast[r], -1)
                gain, cross = (tall(row_coeffs[f, r + STEPS - 1], height) for f in range(2))
                new_fast[r] = advance(fast[r], slow[r], around, gain, cross)
            keep = max(margin - 1, 0)
            slow = {r: relax(fast[r], slow[r]) for r in range(-keep, SUB + keep)}
            fast = new_fast
        lane = lane_index(fast[0])
        middle = (lane >= STEPS) & (lane < LANES - STEPS)
        for f, rows in enumerate((fast, slow)):
            for r in range(SUB):
                cells[at, (f * SUB + r) * LANES:(f * SUB + r + 1) * LANES] = jnp.where(middle, rows[r], 0.0)

    middle_gram[...] = dot_nt(cells[...], cells[...])


def local_call(body, name, out_shapes, scratch, *args, hbm=False, vmem=VMEM_BYTES, cost=None):
    spec = pl.BlockSpec(memory_space=pltpu.VMEM)
    return pl.pallas_call(
        body,
        out_shape=[jax.ShapeDtypeStruct(s, jnp.float32) for s in out_shapes],
        in_specs=[pl.BlockSpec(memory_space=pltpu.HBM) if hbm else spec] * len(args),
        out_specs=[spec] * len(out_shapes),
        scratch_shapes=[pltpu.VMEM(s, jnp.float32) if isinstance(s, tuple) else s for s in scratch],
        compiler_params=pltpu.CompilerParams(vmem_limit_bytes=vmem),
        name=name,
        cost_estimate=cost,
    )(*args)


def swap(cells, axis, first, close=False):
    count = lax.axis_size(axis)
    pairs = [(i, i + 1) for i in range(first, count - 1, 2)]
    if close and first:
        pairs.append((0, count - 1))
    return lax.ppermute(cells, axis, pairs + [(b, a) for a, b in pairs])


def exchange(cells, grp_bit, tile_bit):
    grps, tiles = lax.axis_size("grp"), lax.axis_size("tile")
    moves = [(g * tiles + t, (g ^ grp_bit) * tiles + (t ^ tile_bit)) for g in range(grps) for t in range(tiles)]
    return lax.ppermute(cells, ("grp", "tile"), moves)


def parity():
    bits = lax.axis_index("grp") ^ lax.axis_index("tile")
    shift = 1
    while shift < max(lax.axis_size("grp"), lax.axis_size("tile")):
        bits = bits ^ (bits >> shift)
        shift *= 2
    return (bits & 1) == 1


def sum_blocks(packed):
    half = packed.shape[0] // 2
    high_half = parity()
    low, high = packed[:half], packed[half:]
    part = jnp.where(high_half, high, low) + exchange(jnp.where(high_half, low, high), 0, 1)
    for axis in ("grp", "tile"):
        bit = 1 if axis == "grp" else 2
        while bit < lax.axis_size(axis):
            part = part + (exchange(part, bit, 1) if axis == "grp" else exchange(part, 0, bit + 1))
            bit *= 2
    return part, exchange(part, 0, 1)


def per_device(tangents, reaction_self, reaction_cross):
    fields = tangents.shape[1]
    padded = fields + SUB
    rows = tangents.reshape(2, fields * tangents.shape[2], tangents.shape[3])
    message, strip = (STEPS, padded, LANES), (padded, LANES)
    inputs = (rows, reaction_self, reaction_cross)
    last, first, near, far, near_fast, far_fast = local_call(
        functools.partial(edge_kernel, fields, HEIGHT_EDGE), "edges", [strip] * 2 + [message] * 4,
        [a.shape for a in inputs] + [pltpu.SemaphoreType.DMA((fields // HEIGHT_EDGE + 2,))], *inputs,
        hbm=True, vmem=EDGE_VMEM_BYTES,
    )
    near, far = swap(near, "tile", 0), swap(far, "tile", 1)
    near_fast, far_fast = swap(near_fast, "tile", 0), swap(far_fast, "tile", 1)
    strips, near_cols, far_cols = local_call(
        column_kernel, "columns", [(4,) + strip, strip, strip], [(2,) + strip], last, first, near, far
    )
    far_cols = swap(far_cols, "grp", 1, close=True)
    near_cols = swap(near_cols, "grp", 0)
    (middle_gram,) = local_call(
        functools.partial(evolve_kernel, fields, HEIGHT_EVOLVE), "evolve", [(fields, fields)],
        [(2, SUB + 2 * STEPS - 2, SUB, LANES), (fields, 2 * SUB * LANES)], *inputs, near, far, near_fast, far_fast,
    )
    side_blocks = fields // SIDE
    blocks = side_blocks * (side_blocks + 1) // 2
    (packed,) = local_call(
        functools.partial(gram_kernel, fields, HEIGHT_STRIP), "gram", [((blocks + 1) // 2 * SIDE, 2 * SIDE)],
        [(2,) + strip, (fields, LANES)], middle_gram, strips, near_cols, far_cols,
    )
    block_total = lax.axis_size("grp") * lax.axis_size("tile")
    corrections, growth = factor_call(*sum_blocks(packed), local_factor(packed, side_blocks), fields, math.sqrt(block_total))
    return (corrections, growth)


def solution(mesh):
    in_specs = (P(None, None, "tile", "grp"), P("tile", "grp"), P("tile", "grp"))
    out_specs = (P(("grp", "tile"), None), P())
    return jax.shard_map(
        per_device, mesh=mesh, in_specs=in_specs, out_specs=out_specs, check_vma=False
    )
```

```python
import functools
import math

import jax
import jax.numpy as jnp
from jax import lax
from jax.experimental import pallas as pl
from jax.experimental.pallas import tpu as pltpu
from jax.sharding import PartitionSpec as P


STEPS = 4
diffusion = 0.2
slow_rate = 0.05
HEIGHT_EDGE = 96
HEIGHT_STRIP = 192
HEIGHT_EVOLVE = 48
SIDE = 64
VMEM_BYTES = 24 * 1024 * 1024
LOCAL_COST = pl.CostEstimate(flops=10**9, bytes_accessed=10**6, transcendentals=0)
EDGE_VMEM_BYTES = 52 * 1024 * 1024
LANES = 128
SUB = 8
HI = lax.Precision.HIGHEST

def dot_nn(a, b):
    return lax.dot_general(a, b, (((1,), (0,)), ((), ())), precision=HI, preferred_element_type=jnp.float32)
def dot_tn(a, b):
    return lax.dot_general(a, b, (((0,), (0,)), ((), ())), precision=HI, preferred_element_type=jnp.float32)
def dot_nt(a, b):
    return lax.dot_general(a, b, (((1,), (1,)), ((), ())), precision=HI, preferred_element_type=jnp.float32)

def gram_of(cells):
    high = cells.astype(jnp.bfloat16)
    left = cells - high.astype(jnp.float32)
    middle = left.astype(jnp.bfloat16)
    low = (left - middle.astype(jnp.float32)).astype(jnp.bfloat16)

    def product(a, b):
        return lax.dot_general(a, b, (((1,), (1,)), ((), ())), preferred_element_type=jnp.float32)

    mixed = product(middle, high) + product(low, high)
    return product(high, high) + product(middle, middle) + (mixed + mixed.T)


def block_pairs(n):
    return [(i, j) for i in range(n) for j in range(i, n)]

def unpack_blocks(packed, n):
    out = {}
    for index, key in enumerate(block_pairs(n)):
        row, half = divmod(index, 2)
        out[key] = packed[row*SIDE:(row+1)*SIDE, half*SIDE:(half+1)*SIDE]
    return out

def spread_lane(x, lane):
    return jnp.broadcast_to(x[:, lane:lane+1], (x.shape[0], LANES))
def spread_row(x, row):
    return jnp.broadcast_to(x[row:row+1, :], (SUB, x.shape[1]))

def factor_blocks(blocks):
    groups = SIDE // SUB
    eye = (lax.broadcasted_iota(jnp.int32, (SIDE, SIDE), 0) == lax.broadcasted_iota(jnp.int32, (SIDE, SIDE), 1)).astype(jnp.float32)
    sub = lax.broadcasted_iota(jnp.int32, (SUB, LANES), 0)
    states = []
    for d in blocks:
        whole = jnp.concatenate([d, eye], axis=1)
        states.append([whole[g*SUB:(g+1)*SUB] for g in range(groups)])
    done = [[] for _ in blocks]
    ready = [None for _ in blocks]
    for p in range(groups):
        for s, v in enumerate(states):
            spread = {(g, c): spread_lane(v[g], p*SUB + c) for g in range(p + 1, groups) for c in range(SUB)}
            if p + 1 < groups:
                coming = [spread_lane(v[p + 1], (p + 1)*SUB + c) for c in range(SUB)]
            columns = ready[s] or [spread_lane(v[p], p*SUB + c) for c in range(SUB)]
            rows = [spread_row(v[p], c) for c in range(SUB)]
            pivots = {(a, c): spread_row(columns[c], a) for c in range(SUB) for a in range(c, SUB)}
            mult, inverses, scale = {}, [], []
            for c in range(SUB):
                inverses.append(1.0 / pivots[c, c])
                scale.append(lax.rsqrt(pivots[c, c]))
                for a in range(c + 1, SUB):
                    mult[a, c] = pivots[a, c] * inverses[c]
                    rows[a] = rows[a] - mult[a, c] * rows[c]
                    for b in range(c + 1, a + 1):
                        pivots[a, b] = pivots[a, b] - mult[a, c] * pivots[b, c]
            scaled = [rows[c] * scale[c] for c in range(SUB)]
            panel = scaled[0]
            for c in range(1, SUB):
                panel = jnp.where(sub == c, scaled[c], panel)
            done[s].append(panel)
            for g in range(p + 1, min(p + 3, groups)):
                cols = [spread[g, c] for c in range(SUB)]
                for c in range(SUB):
                    for a in range(c + 1, SUB):
                        cols[a] = cols[a] - mult[a, c] * cols[c]
                    if g == p + 1:
                        part = cols[c] * inverses[c]
                        coming = [x - part * spread_row(cols[c], b) for b, x in enumerate(coming)]
                    v[g] = v[g] - (cols[c] * scale[c]) * scaled[c]
                if g == p + 1:
                    ready[s] = coming
            if p + 3 < groups:
                solved = [scaled[c] * scale[c] for c in range(SUB)]
                for c in reversed(range(SUB)):
                    for a in range(c):
                        solved[a] = solved[a] - mult[c, a] * solved[c]
                for g in range(p + 3, groups):
                    for c in range(SUB):
                        v[g] = v[g] - spread[g, c] * solved[c]
    out = []
    for panels in done:
        whole = jnp.concatenate(panels, axis=0)
        out.append((whole[:, :SIDE], whole[:, SIDE:]))
    return out

def square_masks():
    row = lax.broadcasted_iota(jnp.int32, (SIDE, SIDE), 0)
    col = lax.broadcasted_iota(jnp.int32, (SIDE, SIDE), 1)
    return row <= col, row == col


def local_kernel(n, packed, gram, panel, *after):
    blocks = unpack_blocks(gram[...], n) if packed else {
        (i, j): gram[i*SIDE:(i+1)*SIDE, j*SIDE:(j+1)*SIDE] for i, j in block_pairs(n)
    }
    ((factor, inverse),) = factor_blocks([blocks[0, 0]])
    panel[:, :SIDE] = jnp.where(square_masks()[0], factor, 0.0)
    if n > 1:
        row = dot_nn(inverse, jnp.concatenate([blocks[0, j] for j in range(1, n)], axis=1))
        panel[:, SIDE:] = row
        less = dot_tn(row, row)
        for i, j in block_pairs(n - 1):
            at = (slice(i*SIDE, (i+1)*SIDE), slice(j*SIDE, (j+1)*SIDE))
            after[0][at] = blocks[i + 1, j + 1] - less[at]


def local_factor(packed, n):
    panels, left = [], packed
    for k in range(n):
        m = n - k
        shapes = [(SIDE, m*SIDE)] + ([((m-1)*SIDE, (m-1)*SIDE)] if m > 1 else [])
        panel, *left = local_call(functools.partial(local_kernel, m, k == 0), "local_factor", shapes, [], left, cost=LOCAL_COST)
        left = left[0] if left else None
        panels.append(panel)
    return panels


def factor_kernel(n, weight, own_ref, other_ref, *refs):
    local, (out_ref, growth_ref) = refs[:n], refs[n:]
    high_half = parity()
    own, other = own_ref[...], other_ref[...]
    total = unpack_blocks(jnp.concatenate([jnp.where(high_half, other, own), jnp.where(high_half, own, other)], axis=0), n)
    diag = square_masks()[1]
    rest = {j: [local[i][:, (j-i)*SIDE:(j-i+1)*SIDE] for i in range(j + 1)] for j in range(n)}
    for k in range(n):
        ((factor, inverse),) = factor_blocks([total[k, k]])
        growth_ref[0, k*SIDE:(k+1)*SIDE] = jnp.log(jnp.sum(jnp.where(diag, factor, 0.0), axis=0))
        if k + 1 < n:
            row = dot_nn(inverse, jnp.concatenate([total[k, j] for j in range(k + 1, n)], axis=1))
            for i in range(k + 1, n):
                less = dot_tn(row[:, (i-k-1)*SIDE:(i-k)*SIDE], row[:, (i-k-1)*SIDE:])
                for j in range(i, n):
                    total[i, j] = total[i, j] - less[:, (j-i)*SIDE:(j-i+1)*SIDE]
        answer = dot_nt(jnp.concatenate(rest[k], axis=0), inverse)
        out_ref[:(k+1)*SIDE, k*SIDE:(k+1)*SIDE] = weight * answer
        if k + 1 < n:
            out_ref[(k+1)*SIDE:, k*SIDE:(k+1)*SIDE] = jnp.zeros(((n-k-1)*SIDE, SIDE), jnp.float32)
            less = dot_nn(answer, row)
            for j in range(k + 1, n):
                at = (j-k-1)*SIDE
                rest[j] = [
                    part - less[i*SIDE:(i+1)*SIDE, at:at+SIDE] if i <= k else part for i, part in enumerate(rest[j])
                ]


def factor_call(own, other, local, k, weight):
    out, growth = local_call(
        functools.partial(factor_kernel, k // SIDE, weight), "factor", [(k, k), (1, k)], [], own, other, *local
    )
    return out, growth[0]


def pick(flag, first, second):
    return jnp.where(flag, first, second)


def roll(x, shift):
    return pltpu.roll(x, shift % LANES, 1)


def lane_index(like):
    return lax.broadcasted_iota(jnp.int32, like.shape, like.ndim - 1)


def chunk(g, height):
    return pl.ds(pl.multiple_of(g * height, height), height)


def own_rows(tangents, g, height):
    return [[tangents[f, pl.ds(g * height * SUB + r, height, stride=SUB), :] for r in range(SUB)] for f in range(2)]


def own_coeffs(coeffs):
    return [[spread_row(coeffs[f], r) for r in range(SUB)] for f in range(2)]


def tall(x, height):
    return jnp.concatenate([x] * (height // SUB), axis=0)


def edge_kernel(fields, height, tangents_hbm, coeffs_hbm, last_out, first_out, near, far, near_fast, far_fast, tangents, coeffs, sems):
    chunks = fields // height
    span = height * SUB
    loads = [
        pltpu.make_async_copy(tangents_hbm.at[:, pl.ds(g * span, span), :], tangents.at[:, pl.ds(g * span, span), :], sems.at[g])
        for g in range(chunks)
    ]
    small = pltpu.make_async_copy(coeffs_hbm, coeffs, sems.at[chunks])
    for load in loads + [small]:
        load.start()
    odd = lax.axis_index("tile") % 2 == 1

    def send(at, rows):
        cell = lane_index(rows[0][0]) // SUB
        cells = LANES // SUB
        last, first = None, None
        for f in range(2):
            for r in range(SUB):
                s = f * SUB + r
                turned = roll(rows[f][r], (s + 1) * SUB)
                last = turned if last is None else jnp.where(cell == s, turned, last)
                first = turned if first is None else jnp.where(cell == (s + 1) % cells, turned, first)
        first = roll(first, -SUB)
        last_out[at, :] = last
        first_out[at, :] = first
        half = cell % SUB < STEPS
        to_above = jnp.where(half, last, roll(first, STEPS * SUB))
        to_below = jnp.where(half, roll(last, -STEPS * SUB), first)
        near[0, at, :] = pick(odd, to_above, to_below)
        far[0, at, :] = pick(odd, to_below, to_above)
        for f in range(2):
            count = STEPS - f
            for j in range(count):
                top, bottom = rows[f][j], rows[f][SUB - count + j]
                (near if f else near_fast)[j + f, at, :] = pick(odd, top, bottom)
                (far if f else far_fast)[j + f, at, :] = pick(odd, bottom, top)

    for g, load in enumerate(loads):
        load.wait()
        send(pl.ds(g * height, height), own_rows(tangents, g, height))
    small.wait()
    send(pl.ds(fields, SUB), own_coeffs(coeffs))


def column_kernel(last, first, near, far, strips, near_out, far_out, outer):
    tile, tiles = lax.axis_index("tile"), lax.axis_size("tile")
    odd, at_top, at_bottom = tile % 2 == 1, tile == 0, tile == tiles - 1
    grp_odd = lax.axis_index("grp") % 2 == 1
    one, two = near[0], far[0]
    lane = lane_index(one)
    cell, low, inner = lane // SUB % SUB, lane < LANES // 2, lane % SUB < STEPS
    half = cell < STEPS
    above, below = pick(odd, one, two), pick(odd, two, one)
    outer[0] = jnp.where(half, below, roll(above, STEPS * SUB))
    outer[1] = jnp.where(half, roll(below, -STEPS * SUB), above)

    @pl.when(at_top | at_bottom)
    def _():
        outside = (half & at_bottom) | (~half & at_top)
        for i, ref in enumerate((last, first)):
            own = ref[...]
            mirrored = roll(own, -7 * SUB)
            for s in range(1, SUB):
                mirrored = jnp.where(cell == s, roll(own, (2 * s - 7) * SUB), mirrored)
            outer[i] = jnp.where(outside, mirrored, outer[i])

    sides = []
    for i, ref in enumerate((last, first)):
        own, more = ref[...], outer[i]
        fast = jnp.where(low, own, roll(more, LANES // 2))
        slow = jnp.where(low, roll(own, LANES // 2), more)
        strips[2 * i] = fast
        strips[2 * i + 1] = slow
        sides.append((fast, slow))
    to_left = jnp.where(inner, sides[1][0], roll(sides[1][1], STEPS))
    to_right = jnp.where(inner, roll(sides[0][0], -STEPS), sides[0][1])
    near_out[...] = pick(grp_odd, to_left, to_right)
    far_out[...] = pick(grp_odd, to_right, to_left)


def strip_neighbours(last, first, halo, wanted):
    c = lane_index(last) % SUB
    end, begin = c == SUB - 1, c == 0
    out = []
    sides = (lambda: (last, roll(halo, 7), None), lambda: (first, None, roll(halo, -7)), lambda: (halo, roll(first, 7), roll(last, -7)))
    for side in sides[:wanted]:
        x, after, before = side()
        right, left = roll(x, -1), roll(x, 1)
        if after is not None:
            right = jnp.where(end, after, right)
        if before is not None:
            left = jnp.where(begin, before, left)
        out.append(roll(x, SUB) + roll(x, -SUB) + right + left)
    return out


def advance(fast, slow, around, gain, cross):
    return gain * fast + diffusion * around + cross * slow


def relax(fast, slow):
    return (1.0 - slow_rate) * slow + slow_rate * fast


def gram_kernel(fields, height, middle_gram, strips, near, far, gram, halo, ends):
    grp, grps = lax.axis_index("grp"), lax.axis_size("grp")
    grp_odd = grp % 2 == 1
    one, two = near[...], far[...]
    lane = lane_index(one)
    c = lane % SUB
    inner = c < STEPS
    left, right = pick(grp_odd, one, two), pick(grp_odd, two, one)
    halo[0] = jnp.where(inner, right, roll(left, STEPS))
    halo[1] = jnp.where(inner, roll(right, -STEPS), left)

    @pl.when((grp == 0) | (grp == grps - 1))
    def _():
        after, before = inner & (grp == grps - 1), ~inner & (grp == 0)
        for f in range(2):
            tail, start = strips[f], strips[2 + f]
            mirrored = halo[f]
            for s in range(STEPS):
                mirrored = jnp.where(after & (c == s), roll(tail, 2 * s - 7), mirrored)
                mirrored = jnp.where(before & (c == 7 - s), roll(start, 7 - 2 * s), mirrored)
            halo[f] = mirrored

    def parts(f, at):
        return [strips[f, at, :], strips[2 + f, at, :], halo[f, at, :]]

    gains = [tall(x + (1.0 - 4.0 * diffusion), height) for x in parts(0, pl.ds(fields, SUB))]
    crosses = [tall(x, height) for x in parts(1, pl.ds(fields, SUB))]

    @pl.loop(0, fields // height)
    def _(g):
        fast, slow = parts(0, chunk(g, height)), parts(1, chunk(g, height))
        for step in range(STEPS):
            wanted = 3 if step + 1 < STEPS else 2
            around = strip_neighbours(*fast, wanted)
            moved = [advance(fast[p], slow[p], around[p], gains[p], crosses[p]) for p in range(wanted)]
            slow = [relax(fast[p], slow[p]) for p in range(wanted)]
            fast = moved
        l = lane_index(fast[0])
        joined = [jnp.where(l % SUB < STEPS, s[1], s[0]) for s in (fast, slow)]
        ends[chunk(g, height), :] = jnp.where(l < LANES // 2, joined[0], roll(joined[1], LANES // 2))

    whole = middle_gram[...] + gram_of(ends[...])
    for index, (i, j) in enumerate(block_pairs(fields // SIDE)):
        row, half = divmod(index, 2)
        gram[row * SIDE:(row + 1) * SIDE, half * SIDE:(half + 1) * SIDE] = whole[
            i * SIDE:(i + 1) * SIDE, j * SIDE:(j + 1) * SIDE
        ]


def extended_rows(own, near, far, near_fast, far_fast, at):
    tile, tiles = lax.axis_index("tile"), lax.axis_size("tile")
    odd, at_top, at_bottom = tile % 2 == 1, tile == 0, tile == tiles - 1
    out = []
    for f in range(2):
        count = STEPS - f
        rows = dict(enumerate(own[f]))
        for j in range(count):
            one, two = ((near if f else near_fast)[j + f, at, :], (far if f else far_fast)[j + f, at, :])
            rows[j - count] = pick(at_top, own[f][count - 1 - j], pick(odd, one, two))
            rows[SUB + j] = pick(at_bottom, own[f][SUB - 1 - j], pick(odd, two, one))
        out.append(rows)
    return out


def evolve_kernel(fields, height, tangents, coeffs, near, far, near_fast, far_fast, middle_gram, row_coeffs, cells):
    coeff_rows = extended_rows(own_coeffs(coeffs), near, far, near_fast, far_fast, pl.ds(fields, SUB))
    for f in range(2):
        for r in range(1 - STEPS, SUB + STEPS - 1):
            row_coeffs[f, r + STEPS - 1, :, :] = coeff_rows[f][r] + (1.0 - 4.0 * diffusion) * (1 - f)

    @pl.loop(0, fields // height)
    def _(g):
        at = chunk(g, height)
        fast, slow = extended_rows(own_rows(tangents, g, height), near, far, near_fast, far_fast, at)
        for step in range(1, STEPS + 1):
            margin = STEPS - step
            new_fast = {}
            for r in range(-margin, SUB + margin):
                around = fast[r - 1] + fast[r + 1] + roll(fast[r], 1) + roll(fast[r], -1)
                gain, cross = (tall(row_coeffs[f, r + STEPS - 1], height) for f in range(2))
                new_fast[r] = advance(fast[r], slow[r], around, gain, cross)
            keep = max(margin - 1, 0)
            slow = {r: relax(fast[r], slow[r]) for r in range(-keep, SUB + keep)}
            fast = new_fast
        lane = lane_index(fast[0])
        middle = (lane >= STEPS) & (lane < LANES - STEPS)
        for f, rows in enumerate((fast, slow)):
            for r in range(SUB):
                cells[at, (f * SUB + r) * LANES:(f * SUB + r + 1) * LANES] = jnp.where(middle, rows[r], 0.0)

    middle_gram[...] = gram_of(cells[...])


def local_call(body, name, out_shapes, scratch, *args, hbm=False, vmem=VMEM_BYTES, cost=None):
    spec = pl.BlockSpec(memory_space=pltpu.VMEM)
    return pl.pallas_call(
        body,
        out_shape=[jax.ShapeDtypeStruct(s, jnp.float32) for s in out_shapes],
        in_specs=[pl.BlockSpec(memory_space=pltpu.HBM) if hbm else spec] * len(args),
        out_specs=[spec] * len(out_shapes),
        scratch_shapes=[pltpu.VMEM(s, jnp.float32) if isinstance(s, tuple) else s for s in scratch],
        compiler_params=pltpu.CompilerParams(vmem_limit_bytes=vmem),
        name=name,
        cost_estimate=cost,
    )(*args)


def swap(cells, axis, first, close=False):
    count = lax.axis_size(axis)
    pairs = [(i, i + 1) for i in range(first, count - 1, 2)]
    if close and first:
        pairs.append((0, count - 1))
    return lax.ppermute(cells, axis, pairs + [(b, a) for a, b in pairs])


def exchange(cells, grp_bit, tile_bit):
    grps, tiles = lax.axis_size("grp"), lax.axis_size("tile")
    moves = [(g * tiles + t, (g ^ grp_bit) * tiles + (t ^ tile_bit)) for g in range(grps) for t in range(tiles)]
    return lax.ppermute(cells, ("grp", "tile"), moves)


def parity():
    bits = lax.axis_index("grp") ^ lax.axis_index("tile")
    shift = 1
    while shift < max(lax.axis_size("grp"), lax.axis_size("tile")):
        bits = bits ^ (bits >> shift)
        shift *= 2
    return (bits & 1) == 1


def sum_blocks(packed):
    half = packed.shape[0] // 2
    high_half = parity()
    low, high = packed[:half], packed[half:]
    part = jnp.where(high_half, high, low) + exchange(jnp.where(high_half, low, high), 0, 1)
    for axis in ("grp", "tile"):
        bit = 1 if axis == "grp" else 2
        while bit < lax.axis_size(axis):
            part = part + (exchange(part, bit, 1) if axis == "grp" else exchange(part, 0, bit + 1))
            bit *= 2
    return part, exchange(part, 0, 1)


def per_device(tangents, reaction_self, reaction_cross):
    fields = tangents.shape[1]
    padded = fields + SUB
    rows = tangents.reshape(2, fields * tangents.shape[2], tangents.shape[3])
    message, strip = (STEPS, padded, LANES), (padded, LANES)
    inputs = (rows, jnp.stack([reaction_self, reaction_cross]))
    last, first, near, far, near_fast, far_fast = local_call(
        functools.partial(edge_kernel, fields, HEIGHT_EDGE), "edges", [strip] * 2 + [message] * 4,
        [a.shape for a in inputs] + [pltpu.SemaphoreType.DMA((fields // HEIGHT_EDGE + 1,))], *inputs,
        hbm=True, vmem=EDGE_VMEM_BYTES,
    )
    near, far = swap(near, "tile", 0), swap(far, "tile", 1)
    near_fast, far_fast = swap(near_fast, "tile", 0), swap(far_fast, "tile", 1)
    strips, near_cols, far_cols = local_call(
        column_kernel, "columns", [(4,) + strip, strip, strip], [(2,) + strip], last, first, near, far
    )
    far_cols = swap(far_cols, "grp", 1, close=True)
    near_cols = swap(near_cols, "grp", 0)
    (middle_gram,) = local_call(
        functools.partial(evolve_kernel, fields, HEIGHT_EVOLVE), "evolve", [(fields, fields)],
        [(2, SUB + 2 * STEPS - 2, SUB, LANES), (fields, 2 * SUB * LANES)], *inputs, near, far, near_fast, far_fast,
    )
    side_blocks = fields // SIDE
    blocks = side_blocks * (side_blocks + 1) // 2
    (packed,) = local_call(
        functools.partial(gram_kernel, fields, HEIGHT_STRIP), "gram", [((blocks + 1) // 2 * SIDE, 2 * SIDE)],
        [(2,) + strip, (fields, LANES)], middle_gram, strips, near_cols, far_cols,
    )
    block_total = lax.axis_size("grp") * lax.axis_size("tile")
    corrections, growth = factor_call(*sum_blocks(packed), local_factor(packed, side_blocks), fields, math.sqrt(block_total))
    return (corrections, growth)


def solution(mesh):
    in_specs = (P(None, None, "tile", "grp"), P("tile", "grp"), P("tile", "grp"))
    out_specs = (P(("grp", "tile"), None), P())
    return jax.shard_map(
        per_device, mesh=mesh, in_specs=in_specs, out_specs=out_specs, check_vma=False
    )
```

```python
import functools
import math

import jax
import jax.numpy as jnp
from jax import lax
from jax.experimental import pallas as pl
from jax.experimental.pallas import tpu as pltpu
from jax.sharding import PartitionSpec as P


STEPS = 4
diffusion = 0.2
slow_rate = 0.05
HEIGHT_EDGE = 96
HEIGHT_STRIP = 192
HEIGHT_EVOLVE = 24
SIDE = 64
VMEM_BYTES = 24 * 1024 * 1024
LOCAL_COST = pl.CostEstimate(flops=10**9, bytes_accessed=10**6, transcendentals=0)
EDGE_VMEM_BYTES = 52 * 1024 * 1024
LANES = 128
SUB = 8
HI = lax.Precision.HIGHEST

def dot_nn(a, b):
    return lax.dot_general(a, b, (((1,), (0,)), ((), ())), precision=HI, preferred_element_type=jnp.float32)
def dot_tn(a, b):
    return lax.dot_general(a, b, (((0,), (0,)), ((), ())), precision=HI, preferred_element_type=jnp.float32)
def dot_nt(a, b):
    return lax.dot_general(a, b, (((1,), (1,)), ((), ())), precision=HI, preferred_element_type=jnp.float32)

def gram_of(cells):
    high = cells.astype(jnp.bfloat16)
    left = cells - high.astype(jnp.float32)
    middle = left.astype(jnp.bfloat16)
    low = (left - middle.astype(jnp.float32)).astype(jnp.bfloat16)

    def product(a, b):
        return lax.dot_general(a, b, (((1,), (1,)), ((), ())), preferred_element_type=jnp.float32)

    mixed = product(middle, high) + product(low, high)
    return product(high, high) + product(middle, middle) + (mixed + mixed.T)


def block_pairs(n):
    return [(i, j) for i in range(n) for j in range(i, n)]

def unpack_blocks(packed, n):
    out = {}
    for index, key in enumerate(block_pairs(n)):
        row, half = divmod(index, 2)
        out[key] = packed[row*SIDE:(row+1)*SIDE, half*SIDE:(half+1)*SIDE]
    return out

def spread_lane(x, lane):
    return jnp.broadcast_to(x[:, lane:lane+1], (x.shape[0], LANES))
def spread_row(x, row):
    return jnp.broadcast_to(x[row:row+1, :], (SUB, x.shape[1]))

def factor_blocks(blocks):
    groups = SIDE // SUB
    eye = (lax.broadcasted_iota(jnp.int32, (SIDE, SIDE), 0) == lax.broadcasted_iota(jnp.int32, (SIDE, SIDE), 1)).astype(jnp.float32)
    sub = lax.broadcasted_iota(jnp.int32, (SUB, LANES), 0)
    states = []
    for d in blocks:
        whole = jnp.concatenate([d, eye], axis=1)
        states.append([whole[g*SUB:(g+1)*SUB] for g in range(groups)])
    done = [[] for _ in blocks]
    ready = [None for _ in blocks]
    for p in range(groups):
        for s, v in enumerate(states):
            spread = {(g, c): spread_lane(v[g], p*SUB + c) for g in range(p + 1, groups) for c in range(SUB)}
            if p + 1 < groups:
                coming = [spread_lane(v[p + 1], (p + 1)*SUB + c) for c in range(SUB)]
            columns = ready[s] or [spread_lane(v[p], p*SUB + c) for c in range(SUB)]
            rows = [spread_row(v[p], c) for c in range(SUB)]
            pivots = {(a, c): spread_row(columns[c], a) for c in range(SUB) for a in range(c, SUB)}
            mult, inverses, scale = {}, [], []
            for c in range(SUB):
                inverses.append(1.0 / pivots[c, c])
                scale.append(lax.rsqrt(pivots[c, c]))
                for a in range(c + 1, SUB):
                    mult[a, c] = pivots[a, c] * inverses[c]
                    rows[a] = rows[a] - mult[a, c] * rows[c]
                    for b in range(c + 1, a + 1):
                        pivots[a, b] = pivots[a, b] - mult[a, c] * pivots[b, c]
            scaled = [rows[c] * scale[c] for c in range(SUB)]
            panel = scaled[0]
            for c in range(1, SUB):
                panel = jnp.where(sub == c, scaled[c], panel)
            done[s].append(panel)
            for g in range(p + 1, min(p + 3, groups)):
                cols = [spread[g, c] for c in range(SUB)]
                for c in range(SUB):
                    for a in range(c + 1, SUB):
                        cols[a] = cols[a] - mult[a, c] * cols[c]
                    if g == p + 1:
                        part = cols[c] * inverses[c]
                        coming = [x - part * spread_row(cols[c], b) for b, x in enumerate(coming)]
                    v[g] = v[g] - (cols[c] * scale[c]) * scaled[c]
                if g == p + 1:
                    ready[s] = coming
            if p + 3 < groups:
                solved = [scaled[c] * scale[c] for c in range(SUB)]
                for c in reversed(range(SUB)):
                    for a in range(c):
                        solved[a] = solved[a] - mult[c, a] * solved[c]
                for g in range(p + 3, groups):
                    for c in range(SUB):
                        v[g] = v[g] - spread[g, c] * solved[c]
    out = []
    for panels in done:
        whole = jnp.concatenate(panels, axis=0)
        out.append((whole[:, :SIDE], whole[:, SIDE:]))
    return out

def square_masks():
    row = lax.broadcasted_iota(jnp.int32, (SIDE, SIDE), 0)
    col = lax.broadcasted_iota(jnp.int32, (SIDE, SIDE), 1)
    return row <= col, row == col


def local_kernel(n, packed, gram, panel, *after):
    blocks = unpack_blocks(gram[...], n) if packed else {
        (i, j): gram[i*SIDE:(i+1)*SIDE, j*SIDE:(j+1)*SIDE] for i, j in block_pairs(n)
    }
    ((factor, inverse),) = factor_blocks([blocks[0, 0]])
    panel[:, :SIDE] = jnp.where(square_masks()[0], factor, 0.0)
    if n > 1:
        row = dot_nn(inverse, jnp.concatenate([blocks[0, j] for j in range(1, n)], axis=1))
        panel[:, SIDE:] = row
        less = dot_tn(row, row)
        for i, j in block_pairs(n - 1):
            at = (slice(i*SIDE, (i+1)*SIDE), slice(j*SIDE, (j+1)*SIDE))
            after[0][at] = blocks[i + 1, j + 1] - less[at]


def local_factor(packed, n):
    panels, left = [], packed
    for k in range(n):
        m = n - k
        shapes = [(SIDE, m*SIDE)] + ([((m-1)*SIDE, (m-1)*SIDE)] if m > 1 else [])
        panel, *left = local_call(functools.partial(local_kernel, m, k == 0), "local_factor", shapes, [], left, cost=LOCAL_COST)
        left = left[0] if left else None
        panels.append(panel)
    return panels


def factor_kernel(n, weight, own_ref, other_ref, *refs):
    local, (out_ref, growth_ref) = refs[:n], refs[n:]
    high_half = parity()
    own, other = own_ref[...], other_ref[...]
    total = unpack_blocks(jnp.concatenate([jnp.where(high_half, other, own), jnp.where(high_half, own, other)], axis=0), n)
    diag = square_masks()[1]
    rest = {j: [local[i][:, (j-i)*SIDE:(j-i+1)*SIDE] for i in range(j + 1)] for j in range(n)}
    for k in range(n):
        ((factor, inverse),) = factor_blocks([total[k, k]])
        growth_ref[0, k*SIDE:(k+1)*SIDE] = jnp.log(jnp.sum(jnp.where(diag, factor, 0.0), axis=0))
        if k + 1 < n:
            row = dot_nn(inverse, jnp.concatenate([total[k, j] for j in range(k + 1, n)], axis=1))
            for i in range(k + 1, n):
                less = dot_tn(row[:, (i-k-1)*SIDE:(i-k)*SIDE], row[:, (i-k-1)*SIDE:])
                for j in range(i, n):
                    total[i, j] = total[i, j] - less[:, (j-i)*SIDE:(j-i+1)*SIDE]
        answer = dot_nt(jnp.concatenate(rest[k], axis=0), inverse)
        out_ref[:(k+1)*SIDE, k*SIDE:(k+1)*SIDE] = weight * answer
        if k + 1 < n:
            out_ref[(k+1)*SIDE:, k*SIDE:(k+1)*SIDE] = jnp.zeros(((n-k-1)*SIDE, SIDE), jnp.float32)
            less = dot_nn(answer, row)
            for j in range(k + 1, n):
                at = (j-k-1)*SIDE
                rest[j] = [
                    part - less[i*SIDE:(i+1)*SIDE, at:at+SIDE] if i <= k else part for i, part in enumerate(rest[j])
                ]


def factor_call(own, other, local, k, weight):
    out, growth = local_call(
        functools.partial(factor_kernel, k // SIDE, weight), "factor", [(k, k), (1, k)], [], own, other, *local
    )
    return out, growth[0]


def pick(flag, first, second):
    return jnp.where(flag, first, second)


def roll(x, shift):
    return pltpu.roll(x, shift % LANES, 1)


def lane_index(like):
    return lax.broadcasted_iota(jnp.int32, like.shape, like.ndim - 1)


def chunk(g, height):
    return pl.ds(pl.multiple_of(g * height, height), height)


def own_rows(tangents, g, height):
    return [[tangents[f, pl.ds(g * height * SUB + r, height, stride=SUB), :] for r in range(SUB)] for f in range(2)]


def own_coeffs(coeffs):
    return [[spread_row(coeffs[f], r) for r in range(SUB)] for f in range(2)]


def tall(x, height):
    return jnp.concatenate([x] * (height // SUB), axis=0)


def edge_kernel(fields, height, tangents_hbm, coeffs_hbm, last_out, first_out, near, far, near_fast, far_fast, tangents, coeffs, sems):
    chunks = fields // height
    span = height * SUB
    loads = [
        pltpu.make_async_copy(tangents_hbm.at[:, pl.ds(g * span, span), :], tangents.at[:, pl.ds(g * span, span), :], sems.at[g])
        for g in range(chunks)
    ]
    small = pltpu.make_async_copy(coeffs_hbm, coeffs, sems.at[chunks])
    for load in loads + [small]:
        load.start()
    odd = lax.axis_index("tile") % 2 == 1

    def send(at, rows):
        cell = lane_index(rows[0][0]) // SUB
        cells = LANES // SUB
        last, first = None, None
        for f in range(2):
            for r in range(SUB):
                s = f * SUB + r
                turned = roll(rows[f][r], (s + 1) * SUB)
                last = turned if last is None else jnp.where(cell == s, turned, last)
                first = turned if first is None else jnp.where(cell == (s + 1) % cells, turned, first)
        first = roll(first, -SUB)
        last_out[at, :] = last
        first_out[at, :] = first
        half = cell % SUB < STEPS
        to_above = jnp.where(half, last, roll(first, STEPS * SUB))
        to_below = jnp.where(half, roll(last, -STEPS * SUB), first)
        near[0, at, :] = pick(odd, to_above, to_below)
        far[0, at, :] = pick(odd, to_below, to_above)
        for f in range(2):
            count = STEPS - f
            for j in range(count):
                top, bottom = rows[f][j], rows[f][SUB - count + j]
                (near if f else near_fast)[j + f, at, :] = pick(odd, top, bottom)
                (far if f else far_fast)[j + f, at, :] = pick(odd, bottom, top)

    for g, load in enumerate(loads):
        load.wait()
        send(pl.ds(g * height, height), own_rows(tangents, g, height))
    small.wait()
    send(pl.ds(fields, SUB), own_coeffs(coeffs))


def column_kernel(last, first, near, far, strips, near_out, far_out, outer):
    tile, tiles = lax.axis_index("tile"), lax.axis_size("tile")
    odd, at_top, at_bottom = tile % 2 == 1, tile == 0, tile == tiles - 1
    grp_odd = lax.axis_index("grp") % 2 == 1
    one, two = near[0], far[0]
    lane = lane_index(one)
    cell, low, inner = lane // SUB % SUB, lane < LANES // 2, lane % SUB < STEPS
    half = cell < STEPS
    above, below = pick(odd, one, two), pick(odd, two, one)
    outer[0] = jnp.where(half, below, roll(above, STEPS * SUB))
    outer[1] = jnp.where(half, roll(below, -STEPS * SUB), above)

    @pl.when(at_top | at_bottom)
    def _():
        outside = (half & at_bottom) | (~half & at_top)
        for i, ref in enumerate((last, first)):
            own = ref[...]
            mirrored = roll(own, -7 * SUB)
            for s in range(1, SUB):
                mirrored = jnp.where(cell == s, roll(own, (2 * s - 7) * SUB), mirrored)
            outer[i] = jnp.where(outside, mirrored, outer[i])

    sides = []
    for i, ref in enumerate((last, first)):
        own, more = ref[...], outer[i]
        fast = jnp.where(low, own, roll(more, LANES // 2))
        slow = jnp.where(low, roll(own, LANES // 2), more)
        strips[2 * i] = fast
        strips[2 * i + 1] = slow
        sides.append((fast, slow))
    to_left = jnp.where(inner, sides[1][0], roll(sides[1][1], STEPS))
    to_right = jnp.where(inner, roll(sides[0][0], -STEPS), sides[0][1])
    near_out[...] = pick(grp_odd, to_left, to_right)
    far_out[...] = pick(grp_odd, to_right, to_left)


def strip_neighbours(last, first, halo, wanted):
    c = lane_index(last) % SUB
    end, begin = c == SUB - 1, c == 0
    out = []
    sides = (lambda: (last, roll(halo, 7), None), lambda: (first, None, roll(halo, -7)), lambda: (halo, roll(first, 7), roll(last, -7)))
    for side in sides[:wanted]:
        x, after, before = side()
        right, left = roll(x, -1), roll(x, 1)
        if after is not None:
            right = jnp.where(end, after, right)
        if before is not None:
            left = jnp.where(begin, before, left)
        out.append(roll(x, SUB) + roll(x, -SUB) + right + left)
    return out


def advance(fast, slow, around, gain, cross):
    return gain * fast + diffusion * around + cross * slow


def relax(fast, slow):
    return (1.0 - slow_rate) * slow + slow_rate * fast


def gram_kernel(fields, height, middle_gram, strips, near, far, gram, halo, ends):
    grp, grps = lax.axis_index("grp"), lax.axis_size("grp")
    grp_odd = grp % 2 == 1
    one, two = near[...], far[...]
    lane = lane_index(one)
    c = lane % SUB
    inner = c < STEPS
    left, right = pick(grp_odd, one, two), pick(grp_odd, two, one)
    halo[0] = jnp.where(inner, right, roll(left, STEPS))
    halo[1] = jnp.where(inner, roll(right, -STEPS), left)

    @pl.when((grp == 0) | (grp == grps - 1))
    def _():
        after, before = inner & (grp == grps - 1), ~inner & (grp == 0)
        for f in range(2):
            tail, start = strips[f], strips[2 + f]
            mirrored = halo[f]
            for s in range(STEPS):
                mirrored = jnp.where(after & (c == s), roll(tail, 2 * s - 7), mirrored)
                mirrored = jnp.where(before & (c == 7 - s), roll(start, 7 - 2 * s), mirrored)
            halo[f] = mirrored

    def parts(f, at):
        return [strips[f, at, :], strips[2 + f, at, :], halo[f, at, :]]

    gains = [tall(x + (1.0 - 4.0 * diffusion), height) for x in parts(0, pl.ds(fields, SUB))]
    crosses = [tall(x, height) for x in parts(1, pl.ds(fields, SUB))]

    @pl.loop(0, fields // height)
    def _(g):
        fast, slow = parts(0, chunk(g, height)), parts(1, chunk(g, height))
        for step in range(STEPS):
            wanted = 3 if step + 1 < STEPS else 2
            around = strip_neighbours(*fast, wanted)
            moved = [advance(fast[p], slow[p], around[p], gains[p], crosses[p]) for p in range(wanted)]
            slow = [relax(fast[p], slow[p]) for p in range(wanted)]
            fast = moved
        l = lane_index(fast[0])
        joined = [jnp.where(l % SUB < STEPS, s[1], s[0]) for s in (fast, slow)]
        ends[chunk(g, height), :] = jnp.where(l < LANES // 2, joined[0], roll(joined[1], LANES // 2))

    whole = middle_gram[...] + gram_of(ends[...])
    for index, (i, j) in enumerate(block_pairs(fields // SIDE)):
        row, half = divmod(index, 2)
        gram[row * SIDE:(row + 1) * SIDE, half * SIDE:(half + 1) * SIDE] = whole[
            i * SIDE:(i + 1) * SIDE, j * SIDE:(j + 1) * SIDE
        ]


def extended_rows(own, near, far, near_fast, far_fast, at):
    tile, tiles = lax.axis_index("tile"), lax.axis_size("tile")
    odd, at_top, at_bottom = tile % 2 == 1, tile == 0, tile == tiles - 1
    out = []
    for f in range(2):
        count = STEPS - f
        rows = dict(enumerate(own[f]))
        for j in range(count):
            one, two = ((near if f else near_fast)[j + f, at, :], (far if f else far_fast)[j + f, at, :])
            rows[j - count] = pick(at_top, own[f][count - 1 - j], pick(odd, one, two))
            rows[SUB + j] = pick(at_bottom, own[f][SUB - 1 - j], pick(odd, two, one))
        out.append(rows)
    return out


def evolve_kernel(fields, height, tangents, coeffs, near, far, near_fast, far_fast, middle_gram, row_coeffs, cells):
    coeff_rows = extended_rows(own_coeffs(coeffs), near, far, near_fast, far_fast, pl.ds(fields, SUB))
    for f in range(2):
        for r in range(1 - STEPS, SUB + STEPS - 1):
            row_coeffs[f, r + STEPS - 1, :, :] = coeff_rows[f][r] + (1.0 - 4.0 * diffusion) * (1 - f)

    for g in range(fields // height):
        at = chunk(g, height)
        fast, slow = extended_rows(own_rows(tangents, g, height), near, far, near_fast, far_fast, at)
        for step in range(1, STEPS + 1):
            margin = STEPS - step
            new_fast = {}
            for r in range(-margin, SUB + margin):
                around = fast[r - 1] + fast[r + 1] + roll(fast[r], 1) + roll(fast[r], -1)
                gain, cross = (tall(row_coeffs[f, r + STEPS - 1], height) for f in range(2))
                new_fast[r] = advance(fast[r], slow[r], around, gain, cross)
            keep = max(margin - 1, 0)
            slow = {r: relax(fast[r], slow[r]) for r in range(-keep, SUB + keep)}
            fast = new_fast
        lane = lane_index(fast[0])
        middle = (lane >= STEPS) & (lane < LANES - STEPS)
        for f, rows in enumerate((fast, slow)):
            for r in range(SUB):
                cells[at, (f * SUB + r) * LANES:(f * SUB + r + 1) * LANES] = jnp.where(middle, rows[r], 0.0)

    middle_gram[...] = gram_of(cells[...])


def local_call(body, name, out_shapes, scratch, *args, hbm=False, vmem=VMEM_BYTES, cost=None):
    spec = pl.BlockSpec(memory_space=pltpu.VMEM)
    return pl.pallas_call(
        body,
        out_shape=[jax.ShapeDtypeStruct(s, jnp.float32) for s in out_shapes],
        in_specs=[pl.BlockSpec(memory_space=pltpu.HBM) if hbm else spec] * len(args),
        out_specs=[spec] * len(out_shapes),
        scratch_shapes=[pltpu.VMEM(s, jnp.float32) if isinstance(s, tuple) else s for s in scratch],
        compiler_params=pltpu.CompilerParams(vmem_limit_bytes=vmem),
        name=name,
        cost_estimate=cost,
    )(*args)


def swap(cells, axis, first, close=False):
    count = lax.axis_size(axis)
    pairs = [(i, i + 1) for i in range(first, count - 1, 2)]
    if close and first:
        pairs.append((0, count - 1))
    return lax.ppermute(cells, axis, pairs + [(b, a) for a, b in pairs])


def exchange(cells, grp_bit, tile_bit):
    grps, tiles = lax.axis_size("grp"), lax.axis_size("tile")
    moves = [(g * tiles + t, (g ^ grp_bit) * tiles + (t ^ tile_bit)) for g in range(grps) for t in range(tiles)]
    return lax.ppermute(cells, ("grp", "tile"), moves)


def parity():
    bits = lax.axis_index("grp") ^ lax.axis_index("tile")
    shift = 1
    while shift < max(lax.axis_size("grp"), lax.axis_size("tile")):
        bits = bits ^ (bits >> shift)
        shift *= 2
    return (bits & 1) == 1


def sum_blocks(packed, beside):
    half = packed.shape[0] // 2
    high_half = parity()
    low, high = packed[:half], packed[half:]
    part = jnp.where(high_half, high, low) + exchange(jnp.where(high_half, low, high), 0, 1)
    for axis in ("grp", "tile"):
        bit = 1 if axis == "grp" else 2
        while bit < lax.axis_size(axis):
            if axis == "tile" and 2 * bit >= lax.axis_size(axis):
                part, beside = lax.optimization_barrier((part, beside))
            part = part + (exchange(part, bit, 1) if axis == "grp" else exchange(part, 0, bit + 1))
            bit *= 2
    return part, exchange(part, 0, 1), beside


def per_device(tangents, reaction_self, reaction_cross):
    fields = tangents.shape[1]
    padded = fields + SUB
    rows = tangents.reshape(2, fields * tangents.shape[2], tangents.shape[3])
    message, strip = (STEPS, padded, LANES), (padded, LANES)
    inputs = (rows, jnp.stack([reaction_self, reaction_cross]))
    last, first, near, far, near_fast, far_fast = local_call(
        functools.partial(edge_kernel, fields, HEIGHT_EDGE), "edges", [strip] * 2 + [message] * 4,
        [a.shape for a in inputs] + [pltpu.SemaphoreType.DMA((fields // HEIGHT_EDGE + 1,))], *inputs,
        hbm=True, vmem=EDGE_VMEM_BYTES,
    )
    near, far = swap(near, "tile", 0), swap(far, "tile", 1)
    near_fast, far_fast = swap(near_fast, "tile", 0), swap(far_fast, "tile", 1)
    strips, near_cols, far_cols = local_call(
        column_kernel, "columns", [(4,) + strip, strip, strip], [(2,) + strip], last, first, near, far
    )
    far_cols = swap(far_cols, "grp", 1, close=True)
    near_cols = swap(near_cols, "grp", 0)
    (middle_gram,) = local_call(
        functools.partial(evolve_kernel, fields, HEIGHT_EVOLVE), "evolve", [(fields, fields)],
        [(2, SUB + 2 * STEPS - 2, SUB, LANES), (fields, 2 * SUB * LANES)], *inputs, near, far, near_fast, far_fast,
    )
    side_blocks = fields // SIDE
    blocks = side_blocks * (side_blocks + 1) // 2
    (packed,) = local_call(
        functools.partial(gram_kernel, fields, HEIGHT_STRIP), "gram", [((blocks + 1) // 2 * SIDE, 2 * SIDE)],
        [(2,) + strip, (fields, LANES)], middle_gram, strips, near_cols, far_cols,
    )
    block_total = lax.axis_size("grp") * lax.axis_size("tile")
    corrections, growth = factor_call(*sum_blocks(packed, local_factor(packed, side_blocks)), fields, math.sqrt(block_total))
    return (corrections, growth)


def solution(mesh):
    in_specs = (P(None, None, "tile", "grp"), P("tile", "grp"), P("tile", "grp"))
    out_specs = (P(("grp", "tile"), None), P())
    return jax.shard_map(
        per_device, mesh=mesh, in_specs=in_specs, out_specs=out_specs, check_vma=False
    )
```

```python
import functools
import math

import jax
import jax.numpy as jnp
from jax import lax
from jax.experimental import pallas as pl
from jax.experimental.pallas import tpu as pltpu
from jax.sharding import PartitionSpec as P


STEPS = 4
diffusion = 0.2
slow_rate = 0.05
HEIGHT_EDGE = 96
HEIGHT_STRIP = 8
HEIGHT_EVOLVE = 24
SIDE = 64
VMEM_BYTES = 24 * 1024 * 1024
LOCAL_COST = pl.CostEstimate(flops=10**9, bytes_accessed=10**6, transcendentals=0)
EDGE_VMEM_BYTES = 52 * 1024 * 1024
LANES = 128
SUB = 8
HI = lax.Precision.HIGHEST

def dot_nn(a, b):
    return lax.dot_general(a, b, (((1,), (0,)), ((), ())), precision=HI, preferred_element_type=jnp.float32)
def dot_tn(a, b):
    return lax.dot_general(a, b, (((0,), (0,)), ((), ())), precision=HI, preferred_element_type=jnp.float32)
def dot_nt(a, b):
    return lax.dot_general(a, b, (((1,), (1,)), ((), ())), precision=HI, preferred_element_type=jnp.float32)

def gram_of(cells):
    high = cells.astype(jnp.bfloat16)
    left = cells - high.astype(jnp.float32)
    middle = left.astype(jnp.bfloat16)
    low = (left - middle.astype(jnp.float32)).astype(jnp.bfloat16)

    def product(a, b):
        return lax.dot_general(a, b, (((1,), (1,)), ((), ())), preferred_element_type=jnp.float32)

    mixed = product(middle, high) + product(low, high)
    return product(high, high) + product(middle, middle) + (mixed + mixed.T)


def block_pairs(n):
    return [(i, j) for i in range(n) for j in range(i, n)]

def unpack_blocks(packed, n):
    out = {}
    for index, key in enumerate(block_pairs(n)):
        row, half = divmod(index, 2)
        out[key] = packed[row*SIDE:(row+1)*SIDE, half*SIDE:(half+1)*SIDE]
    return out

def spread_lane(x, lane):
    return jnp.broadcast_to(x[:, lane:lane+1], (x.shape[0], LANES))
def spread_row(x, row):
    return jnp.broadcast_to(x[row:row+1, :], (SUB, x.shape[1]))

def factor_blocks(blocks):
    groups = SIDE // SUB
    eye = (lax.broadcasted_iota(jnp.int32, (SIDE, SIDE), 0) == lax.broadcasted_iota(jnp.int32, (SIDE, SIDE), 1)).astype(jnp.float32)
    sub = lax.broadcasted_iota(jnp.int32, (SUB, LANES), 0)
    states = []
    for d in blocks:
        whole = jnp.concatenate([d, eye], axis=1)
        states.append([whole[g*SUB:(g+1)*SUB] for g in range(groups)])
    done = [[] for _ in blocks]
    ready = [None for _ in blocks]
    for p in range(groups):
        for s, v in enumerate(states):
            spread = {(g, c): spread_lane(v[g], p*SUB + c) for g in range(p + 1, groups) for c in range(SUB)}
            if p + 1 < groups:
                coming = [spread_lane(v[p + 1], (p + 1)*SUB + c) for c in range(SUB)]
            columns = ready[s] or [spread_lane(v[p], p*SUB + c) for c in range(SUB)]
            rows = [spread_row(v[p], c) for c in range(SUB)]
            pivots = {(a, c): spread_row(columns[c], a) for c in range(SUB) for a in range(c, SUB)}
            mult, inverses, scale = {}, [], []
            for c in range(SUB):
                inverses.append(1.0 / pivots[c, c])
                scale.append(lax.rsqrt(pivots[c, c]))
                for a in range(c + 1, SUB):
                    mult[a, c] = pivots[a, c] * inverses[c]
                    rows[a] = rows[a] - mult[a, c] * rows[c]
                    for b in range(c + 1, a + 1):
                        pivots[a, b] = pivots[a, b] - mult[a, c] * pivots[b, c]
            scaled = [rows[c] * scale[c] for c in range(SUB)]
            panel = scaled[0]
            for c in range(1, SUB):
                panel = jnp.where(sub == c, scaled[c], panel)
            done[s].append(panel)
            for g in range(p + 1, min(p + 3, groups)):
                cols = [spread[g, c] for c in range(SUB)]
                for c in range(SUB):
                    for a in range(c + 1, SUB):
                        cols[a] = cols[a] - mult[a, c] * cols[c]
                    if g == p + 1:
                        part = cols[c] * inverses[c]
                        coming = [x - part * spread_row(cols[c], b) for b, x in enumerate(coming)]
                    v[g] = v[g] - (cols[c] * scale[c]) * scaled[c]
                if g == p + 1:
                    ready[s] = coming
            if p + 3 < groups:
                solved = [scaled[c] * scale[c] for c in range(SUB)]
                for c in reversed(range(SUB)):
                    for a in range(c):
                        solved[a] = solved[a] - mult[c, a] * solved[c]
                for g in range(p + 3, groups):
                    for c in range(SUB):
                        v[g] = v[g] - spread[g, c] * solved[c]
    out = []
    for panels in done:
        whole = jnp.concatenate(panels, axis=0)
        out.append((whole[:, :SIDE], whole[:, SIDE:]))
    return out

def square_masks():
    row = lax.broadcasted_iota(jnp.int32, (SIDE, SIDE), 0)
    col = lax.broadcasted_iota(jnp.int32, (SIDE, SIDE), 1)
    return row <= col, row == col


def local_kernel(n, packed, gram, panel, *after):
    blocks = unpack_blocks(gram[...], n) if packed else {
        (i, j): gram[i*SIDE:(i+1)*SIDE, j*SIDE:(j+1)*SIDE] for i, j in block_pairs(n)
    }
    ((factor, inverse),) = factor_blocks([blocks[0, 0]])
    panel[:, :SIDE] = jnp.where(square_masks()[0], factor, 0.0)
    if n > 1:
        row = dot_nn(inverse, jnp.concatenate([blocks[0, j] for j in range(1, n)], axis=1))
        panel[:, SIDE:] = row
        less = dot_tn(row, row)
        for i, j in block_pairs(n - 1):
            at = (slice(i*SIDE, (i+1)*SIDE), slice(j*SIDE, (j+1)*SIDE))
            after[0][at] = blocks[i + 1, j + 1] - less[at]


def local_factor(packed, n):
    panels, left = [], packed
    for k in range(n):
        m = n - k
        shapes = [(SIDE, m*SIDE)] + ([((m-1)*SIDE, (m-1)*SIDE)] if m > 1 else [])
        panel, *left = local_call(functools.partial(local_kernel, m, k == 0), "local_factor", shapes, [], left, cost=LOCAL_COST)
        left = left[0] if left else None
        panels.append(panel)
    return panels


def factor_kernel(n, weight, own_ref, other_ref, *refs):
    local, (out_ref, growth_ref) = refs[:n], refs[n:]
    high_half = parity()
    own, other = own_ref[...], other_ref[...]
    total = unpack_blocks(jnp.concatenate([jnp.where(high_half, other, own), jnp.where(high_half, own, other)], axis=0), n)
    diag = square_masks()[1]
    rest = {j: [local[i][:, (j-i)*SIDE:(j-i+1)*SIDE] for i in range(j + 1)] for j in range(n)}
    for k in range(n):
        ((factor, inverse),) = factor_blocks([total[k, k]])
        growth_ref[0, k*SIDE:(k+1)*SIDE] = jnp.log(jnp.sum(jnp.where(diag, factor, 0.0), axis=0))
        if k + 1 < n:
            row = dot_nn(inverse, jnp.concatenate([total[k, j] for j in range(k + 1, n)], axis=1))
            for i in range(k + 1, n):
                less = dot_tn(row[:, (i-k-1)*SIDE:(i-k)*SIDE], row[:, (i-k-1)*SIDE:])
                for j in range(i, n):
                    total[i, j] = total[i, j] - less[:, (j-i)*SIDE:(j-i+1)*SIDE]
        answer = dot_nt(jnp.concatenate(rest[k], axis=0), inverse)
        out_ref[:(k+1)*SIDE, k*SIDE:(k+1)*SIDE] = weight * answer
        if k + 1 < n:
            out_ref[(k+1)*SIDE:, k*SIDE:(k+1)*SIDE] = jnp.zeros(((n-k-1)*SIDE, SIDE), jnp.float32)
            less = dot_nn(answer, row)
            for j in range(k + 1, n):
                at = (j-k-1)*SIDE
                rest[j] = [
                    part - less[i*SIDE:(i+1)*SIDE, at:at+SIDE] if i <= k else part for i, part in enumerate(rest[j])
                ]


def factor_call(own, other, local, k, weight):
    out, growth = local_call(
        functools.partial(factor_kernel, k // SIDE, weight), "factor", [(k, k), (1, k)], [], own, other, *local
    )
    return out, growth[0]


def pick(flag, first, second):
    return jnp.where(flag, first, second)


def roll(x, shift):
    return pltpu.roll(x, shift % LANES, 1)


def lane_index(like):
    return lax.broadcasted_iota(jnp.int32, like.shape, like.ndim - 1)


def chunk(g, height):
    return pl.ds(pl.multiple_of(g * height, height), height)


def own_rows(tangents, g, height):
    return [[tangents[f, pl.ds(g * height * SUB + r, height, stride=SUB), :] for r in range(SUB)] for f in range(2)]


def own_coeffs(coeffs):
    return [[spread_row(coeffs[f], r) for r in range(SUB)] for f in range(2)]


def tall(x, height):
    return jnp.concatenate([x] * (height // SUB), axis=0)


def edge_kernel(fields, height, tangents_hbm, coeffs_hbm, last_out, first_out, near, far, near_fast, far_fast, tangents, coeffs, sems):
    chunks = fields // height
    span = height * SUB
    loads = [
        pltpu.make_async_copy(tangents_hbm.at[:, pl.ds(g * span, span), :], tangents.at[:, pl.ds(g * span, span), :], sems.at[g])
        for g in range(chunks)
    ]
    small = pltpu.make_async_copy(coeffs_hbm, coeffs, sems.at[chunks])
    for load in loads + [small]:
        load.start()
    odd = lax.axis_index("tile") % 2 == 1

    def send(at, rows):
        cell = lane_index(rows[0][0]) // SUB
        cells = LANES // SUB
        last, first = None, None
        for f in range(2):
            for r in range(SUB):
                s = f * SUB + r
                turned = roll(rows[f][r], (s + 1) * SUB)
                last = turned if last is None else jnp.where(cell == s, turned, last)
                first = turned if first is None else jnp.where(cell == (s + 1) % cells, turned, first)
        first = roll(first, -SUB)
        last_out[at, :] = last
        first_out[at, :] = first
        half = cell % SUB < STEPS
        to_above = jnp.where(half, last, roll(first, STEPS * SUB))
        to_below = jnp.where(half, roll(last, -STEPS * SUB), first)
        near[0, at, :] = pick(odd, to_above, to_below)
        far[0, at, :] = pick(odd, to_below, to_above)
        for f in range(2):
            count = STEPS - f
            for j in range(count):
                top, bottom = rows[f][j], rows[f][SUB - count + j]
                (near if f else near_fast)[j + f, at, :] = pick(odd, top, bottom)
                (far if f else far_fast)[j + f, at, :] = pick(odd, bottom, top)

    for g, load in enumerate(loads):
        load.wait()
        send(pl.ds(g * height, height), own_rows(tangents, g, height))
    small.wait()
    send(pl.ds(fields, SUB), own_coeffs(coeffs))


def row_mirror_kernel(last, first, mirrored):
    tile, tiles = lax.axis_index("tile"), lax.axis_size("tile")

    @pl.when((tile == 0) | (tile == tiles - 1))
    def _():
        for i, ref in enumerate((last, first)):
            own = ref[...]
            cell = lane_index(own) // SUB % SUB
            turned = roll(own, -7 * SUB)
            for s in range(1, SUB):
                turned = jnp.where(cell == s, roll(own, (2 * s - 7) * SUB), turned)
            mirrored[i] = turned

    @pl.when((tile != 0) & (tile != tiles - 1))
    def _():
        mirrored[...] = jnp.zeros(mirrored.shape, jnp.float32)


def column_kernel(last, first, mirrored, near, far, strips, near_out, far_out):
    tile, tiles = lax.axis_index("tile"), lax.axis_size("tile")
    odd, at_top, at_bottom = tile % 2 == 1, tile == 0, tile == tiles - 1
    grp_odd = lax.axis_index("grp") % 2 == 1
    one, two = near[0], far[0]
    lane = lane_index(one)
    cell, low, inner = lane // SUB % SUB, lane < LANES // 2, lane % SUB < STEPS
    half = cell < STEPS
    above, below = pick(odd, one, two), pick(odd, two, one)
    outside = (half & at_bottom) | (~half & at_top)
    received = (jnp.where(half, below, roll(above, STEPS * SUB)), jnp.where(half, roll(below, -STEPS * SUB), above))
    sides = []
    for i, ref in enumerate((last, first)):
        own, more = ref[...], jnp.where(outside, mirrored[i], received[i])
        fast = jnp.where(low, own, roll(more, LANES // 2))
        slow = jnp.where(low, roll(own, LANES // 2), more)
        strips[2 * i] = fast
        strips[2 * i + 1] = slow
        sides.append((fast, slow))
    to_left = jnp.where(inner, sides[1][0], roll(sides[1][1], STEPS))
    to_right = jnp.where(inner, roll(sides[0][0], -STEPS), sides[0][1])
    near_out[...] = pick(grp_odd, to_left, to_right)
    far_out[...] = pick(grp_odd, to_right, to_left)


def strip_neighbours(last, first, halo, wanted):
    c = lane_index(last) % SUB
    end, begin = c == SUB - 1, c == 0
    out = []
    sides = (lambda: (last, roll(halo, 7), None), lambda: (first, None, roll(halo, -7)), lambda: (halo, roll(first, 7), roll(last, -7)))
    for side in sides[:wanted]:
        x, after, before = side()
        right, left = roll(x, -1), roll(x, 1)
        if after is not None:
            right = jnp.where(end, after, right)
        if before is not None:
            left = jnp.where(begin, before, left)
        out.append(roll(x, SUB) + roll(x, -SUB) + right + left)
    return out


def advance(fast, slow, around, gain, cross):
    return gain * fast + diffusion * around + cross * slow


def relax(fast, slow):
    return (1.0 - slow_rate) * slow + slow_rate * fast


def column_mirror_kernel(strips, mirrored):
    grp, grps = lax.axis_index("grp"), lax.axis_size("grp")

    @pl.when((grp == 0) | (grp == grps - 1))
    def _():
        for f in range(2):
            tail, start = strips[f], strips[2 + f]
            c = lane_index(tail) % SUB
            turned = roll(tail, -7)
            for s in range(STEPS):
                turned = jnp.where(c == s, roll(tail, 2 * s - 7), turned)
                turned = jnp.where(c == 7 - s, roll(start, 7 - 2 * s), turned)
            mirrored[f] = turned

    @pl.when((grp != 0) & (grp != grps - 1))
    def _():
        mirrored[...] = jnp.zeros(mirrored.shape, jnp.float32)


def gram_kernel(fields, height, middle_gram, strips, mirrored, near, far, gram, halo, ends):
    grp, grps = lax.axis_index("grp"), lax.axis_size("grp")
    grp_odd = grp % 2 == 1
    one, two = near[...], far[...]
    lane = lane_index(one)
    c = lane % SUB
    inner = c < STEPS
    left, right = pick(grp_odd, one, two), pick(grp_odd, two, one)
    outside = (inner & (grp == grps - 1)) | (~inner & (grp == 0))
    halo[0] = jnp.where(outside, mirrored[0], jnp.where(inner, right, roll(left, STEPS)))
    halo[1] = jnp.where(outside, mirrored[1], jnp.where(inner, roll(right, -STEPS), left))

    def parts(f, at):
        return [strips[f, at, :], strips[2 + f, at, :], halo[f, at, :]]

    gains = [tall(x + (1.0 - 4.0 * diffusion), height) for x in parts(0, pl.ds(fields, SUB))]
    crosses = [tall(x, height) for x in parts(1, pl.ds(fields, SUB))]
    places = [pl.ds(at, height) for at in range(0, fields, height)]
    held = [(parts(0, at), parts(1, at)) for at in places]
    for step in range(STEPS):
        wanted = 3 if step + 1 < STEPS else 2
        for i, (fast, slow) in enumerate(held):
            around = strip_neighbours(*fast, wanted)
            moved = [advance(fast[p], slow[p], around[p], gains[p], crosses[p]) for p in range(wanted)]
            held[i] = (moved, [relax(fast[p], slow[p]) for p in range(wanted)])
    for at, pair in zip(places, held):
        l = lane_index(pair[0][0])
        joined = [jnp.where(l % SUB < STEPS, side[1], side[0]) for side in pair]
        ends[at, :] = jnp.where(l < LANES // 2, joined[0], roll(joined[1], LANES // 2))

    whole = middle_gram[...] + gram_of(ends[...])
    for index, (i, j) in enumerate(block_pairs(fields // SIDE)):
        row, half = divmod(index, 2)
        gram[row * SIDE:(row + 1) * SIDE, half * SIDE:(half + 1) * SIDE] = whole[
            i * SIDE:(i + 1) * SIDE, j * SIDE:(j + 1) * SIDE
        ]


def extended_rows(own, near, far, near_fast, far_fast, at):
    tile, tiles = lax.axis_index("tile"), lax.axis_size("tile")
    odd, at_top, at_bottom = tile % 2 == 1, tile == 0, tile == tiles - 1
    out = []
    for f in range(2):
        count = STEPS - f
        rows = dict(enumerate(own[f]))
        for j in range(count):
            one, two = ((near if f else near_fast)[j + f, at, :], (far if f else far_fast)[j + f, at, :])
            rows[j - count] = pick(at_top, own[f][count - 1 - j], pick(odd, one, two))
            rows[SUB + j] = pick(at_bottom, own[f][SUB - 1 - j], pick(odd, two, one))
        out.append(rows)
    return out


def evolve_kernel(fields, height, tangents, coeffs, near, far, near_fast, far_fast, middle_gram, row_coeffs, cells):
    coeff_rows = extended_rows(own_coeffs(coeffs), near, far, near_fast, far_fast, pl.ds(fields, SUB))
    for f in range(2):
        for r in range(1 - STEPS, SUB + STEPS - 1):
            row_coeffs[f, r + STEPS - 1, :, :] = coeff_rows[f][r] + (1.0 - 4.0 * diffusion) * (1 - f)

    for g in range(fields // height):
        at = chunk(g, height)
        fast, slow = extended_rows(own_rows(tangents, g, height), near, far, near_fast, far_fast, at)
        for step in range(1, STEPS + 1):
            margin = STEPS - step
            new_fast = {}
            for r in range(-margin, SUB + margin):
                around = fast[r - 1] + fast[r + 1] + roll(fast[r], 1) + roll(fast[r], -1)
                gain, cross = (tall(row_coeffs[f, r + STEPS - 1], height) for f in range(2))
                new_fast[r] = advance(fast[r], slow[r], around, gain, cross)
            keep = max(margin - 1, 0)
            slow = {r: relax(fast[r], slow[r]) for r in range(-keep, SUB + keep)}
            fast = new_fast
        lane = lane_index(fast[0])
        middle = (lane >= STEPS) & (lane < LANES - STEPS)
        for f, rows in enumerate((fast, slow)):
            for r in range(SUB):
                cells[at, (f * SUB + r) * LANES:(f * SUB + r + 1) * LANES] = jnp.where(middle, rows[r], 0.0)

    middle_gram[...] = gram_of(cells[...])


def local_call(body, name, out_shapes, scratch, *args, hbm=False, vmem=VMEM_BYTES, cost=None):
    spec = pl.BlockSpec(memory_space=pltpu.VMEM)
    return pl.pallas_call(
        body,
        out_shape=[jax.ShapeDtypeStruct(s, jnp.float32) for s in out_shapes],
        in_specs=[pl.BlockSpec(memory_space=pltpu.HBM) if hbm else spec] * len(args),
        out_specs=[spec] * len(out_shapes),
        scratch_shapes=[pltpu.VMEM(s, jnp.float32) if isinstance(s, tuple) else s for s in scratch],
        compiler_params=pltpu.CompilerParams(vmem_limit_bytes=vmem),
        name=name,
        cost_estimate=cost,
    )(*args)


def swap(cells, axis, first, close=False):
    count = lax.axis_size(axis)
    pairs = [(i, i + 1) for i in range(first, count - 1, 2)]
    if close and first:
        pairs.append((0, count - 1))
    return lax.ppermute(cells, axis, pairs + [(b, a) for a, b in pairs])


def exchange(cells, grp_bit, tile_bit):
    grps, tiles = lax.axis_size("grp"), lax.axis_size("tile")
    moves = [(g * tiles + t, (g ^ grp_bit) * tiles + (t ^ tile_bit)) for g in range(grps) for t in range(tiles)]
    return lax.ppermute(cells, ("grp", "tile"), moves)


def parity():
    bits = lax.axis_index("grp") ^ lax.axis_index("tile")
    shift = 1
    while shift < max(lax.axis_size("grp"), lax.axis_size("tile")):
        bits = bits ^ (bits >> shift)
        shift *= 2
    return (bits & 1) == 1


def sum_blocks(packed, beside):
    half = packed.shape[0] // 2
    high_half = parity()
    low, high = packed[:half], packed[half:]
    part = jnp.where(high_half, high, low) + exchange(jnp.where(high_half, low, high), 0, 1)
    for axis in ("grp", "tile"):
        bit = 1 if axis == "grp" else 2
        while bit < lax.axis_size(axis):
            if axis == "tile" and 2 * bit >= lax.axis_size(axis):
                part, beside = lax.optimization_barrier((part, beside))
            part = part + (exchange(part, bit, 1) if axis == "grp" else exchange(part, 0, bit + 1))
            bit *= 2
    return part, exchange(part, 0, 1), beside


def per_device(tangents, reaction_self, reaction_cross):
    fields = tangents.shape[1]
    padded = fields + SUB
    rows = tangents.reshape(2, fields * tangents.shape[2], tangents.shape[3])
    message, strip = (STEPS, padded, LANES), (padded, LANES)
    inputs = (rows, jnp.stack([reaction_self, reaction_cross]))
    last, first, near, far, near_fast, far_fast = local_call(
        functools.partial(edge_kernel, fields, HEIGHT_EDGE), "edges", [strip] * 2 + [message] * 4,
        [a.shape for a in inputs] + [pltpu.SemaphoreType.DMA((fields // HEIGHT_EDGE + 1,))], *inputs,
        hbm=True, vmem=EDGE_VMEM_BYTES,
    )
    near, far = swap(near, "tile", 0), swap(far, "tile", 1)
    near_fast, far_fast = swap(near_fast, "tile", 0), swap(far_fast, "tile", 1)
    (row_mirror,) = local_call(row_mirror_kernel, "row_mirror", [(2,) + strip], [], last, first)
    strips, near_cols, far_cols = local_call(
        column_kernel, "columns", [(4,) + strip, strip, strip], [], last, first, row_mirror, near, far
    )
    (column_mirror,) = local_call(column_mirror_kernel, "column_mirror", [(2,) + strip], [], strips)
    far_cols = swap(far_cols, "grp", 1, close=True)
    near_cols = swap(near_cols, "grp", 0)
    (middle_gram,) = local_call(
        functools.partial(evolve_kernel, fields, HEIGHT_EVOLVE), "evolve", [(fields, fields)],
        [(2, SUB + 2 * STEPS - 2, SUB, LANES), (fields, 2 * SUB * LANES)], *inputs, near, far, near_fast, far_fast,
    )
    side_blocks = fields // SIDE
    blocks = side_blocks * (side_blocks + 1) // 2
    (packed,) = local_call(
        functools.partial(gram_kernel, fields, HEIGHT_STRIP), "gram", [((blocks + 1) // 2 * SIDE, 2 * SIDE)],
        [(2,) + strip, (fields, LANES)], middle_gram, strips, column_mirror, near_cols, far_cols,
    )
    block_total = lax.axis_size("grp") * lax.axis_size("tile")
    corrections, growth = factor_call(*sum_blocks(packed, local_factor(packed, side_blocks)), fields, math.sqrt(block_total))
    return (corrections, growth)


def solution(mesh):
    in_specs = (P(None, None, "tile", "grp"), P("tile", "grp"), P("tile", "grp"))
    out_specs = (P(("grp", "tile"), None), P())
    return jax.shard_map(
        per_device, mesh=mesh, in_specs=in_specs, out_specs=out_specs, check_vma=False
    )
```

```python
import functools
import math

import jax
import jax.numpy as jnp
from jax import lax
from jax.experimental import pallas as pl
from jax.experimental.pallas import tpu as pltpu
from jax.sharding import PartitionSpec as P


STEPS = 4
diffusion = 0.2
slow_rate = 0.05
HEIGHT_EDGE = 96
HEIGHT_STRIP = 8
HEIGHT_EVOLVE = 24
SIDE = 64
VMEM_BYTES = 24 * 1024 * 1024
EARLY_ROWS = 3
LOCAL_COST = pl.CostEstimate(flops=10**9, bytes_accessed=10**6, transcendentals=0)
EDGE_VMEM_BYTES = 52 * 1024 * 1024
LANES = 128
SUB = 8
HI = lax.Precision.HIGHEST

def dot_nn(a, b):
    return lax.dot_general(a, b, (((1,), (0,)), ((), ())), precision=HI, preferred_element_type=jnp.float32)
def dot_tn(a, b):
    return lax.dot_general(a, b, (((0,), (0,)), ((), ())), precision=HI, preferred_element_type=jnp.float32)
def dot_nt(a, b):
    return lax.dot_general(a, b, (((1,), (1,)), ((), ())), precision=HI, preferred_element_type=jnp.float32)

def gram_of(cells):
    high = cells.astype(jnp.bfloat16)
    left = cells - high.astype(jnp.float32)
    middle = left.astype(jnp.bfloat16)
    low = (left - middle.astype(jnp.float32)).astype(jnp.bfloat16)

    def product(a, b):
        return lax.dot_general(a, b, (((1,), (1,)), ((), ())), preferred_element_type=jnp.float32)

    mixed = product(middle, high) + product(low, high)
    return product(high, high) + product(middle, middle) + (mixed + mixed.T)


def block_pairs(n):
    return [(i, j) for i in range(n) for j in range(i, n)]

def unpack_blocks(packed, n):
    out = {}
    for index, key in enumerate(block_pairs(n)):
        row, half = divmod(index, 2)
        out[key] = packed[row*SIDE:(row+1)*SIDE, half*SIDE:(half+1)*SIDE]
    return out

def spread_lane(x, lane):
    return jnp.broadcast_to(x[:, lane:lane+1], (x.shape[0], LANES))
def spread_row(x, row):
    return jnp.broadcast_to(x[row:row+1, :], (SUB, x.shape[1]))

def factor_blocks(blocks):
    groups = SIDE // SUB
    eye = (lax.broadcasted_iota(jnp.int32, (SIDE, SIDE), 0) == lax.broadcasted_iota(jnp.int32, (SIDE, SIDE), 1)).astype(jnp.float32)
    sub = lax.broadcasted_iota(jnp.int32, (SUB, LANES), 0)
    states = []
    for d in blocks:
        whole = jnp.concatenate([d, eye], axis=1)
        states.append([whole[g*SUB:(g+1)*SUB] for g in range(groups)])
    done = [[] for _ in blocks]
    ready = [None for _ in blocks]
    for p in range(groups):
        for s, v in enumerate(states):
            spread = {(g, c): spread_lane(v[g], p*SUB + c) for g in range(p + 1, groups) for c in range(SUB)}
            if p + 1 < groups:
                coming = [spread_lane(v[p + 1], (p + 1)*SUB + c) for c in range(SUB)]
            columns = ready[s] or [spread_lane(v[p], p*SUB + c) for c in range(SUB)]
            rows = [spread_row(v[p], c) for c in range(SUB)]
            pivots = {(a, c): spread_row(columns[c], a) for c in range(SUB) for a in range(c, SUB)}
            mult, inverses, scale = {}, [], []
            for c in range(SUB):
                inverses.append(1.0 / pivots[c, c])
                scale.append(lax.rsqrt(pivots[c, c]))
                for a in range(c + 1, SUB):
                    mult[a, c] = pivots[a, c] * inverses[c]
                    rows[a] = rows[a] - mult[a, c] * rows[c]
                    for b in range(c + 1, a + 1):
                        pivots[a, b] = pivots[a, b] - mult[a, c] * pivots[b, c]
            scaled = [rows[c] * scale[c] for c in range(SUB)]
            panel = scaled[0]
            for c in range(1, SUB):
                panel = jnp.where(sub == c, scaled[c], panel)
            done[s].append(panel)
            for g in range(p + 1, min(p + 3, groups)):
                cols = [spread[g, c] for c in range(SUB)]
                for c in range(SUB):
                    for a in range(c + 1, SUB):
                        cols[a] = cols[a] - mult[a, c] * cols[c]
                    if g == p + 1:
                        part = cols[c] * inverses[c]
                        coming = [x - part * spread_row(cols[c], b) for b, x in enumerate(coming)]
                    v[g] = v[g] - (cols[c] * scale[c]) * scaled[c]
                if g == p + 1:
                    ready[s] = coming
            if p + 3 < groups:
                solved = [scaled[c] * scale[c] for c in range(SUB)]
                for c in reversed(range(SUB)):
                    for a in range(c):
                        solved[a] = solved[a] - mult[c, a] * solved[c]
                for g in range(p + 3, groups):
                    for c in range(SUB):
                        v[g] = v[g] - spread[g, c] * solved[c]
    out = []
    for panels in done:
        whole = jnp.concatenate(panels, axis=0)
        out.append((whole[:, :SIDE], whole[:, SIDE:]))
    return out

def square_masks():
    row = lax.broadcasted_iota(jnp.int32, (SIDE, SIDE), 0)
    col = lax.broadcasted_iota(jnp.int32, (SIDE, SIDE), 1)
    return row <= col, row == col


def local_kernel(n, packed, gram, panel, *after):
    blocks = unpack_blocks(gram[...], n) if packed else {
        (i, j): gram[i*SIDE:(i+1)*SIDE, j*SIDE:(j+1)*SIDE] for i, j in block_pairs(n)
    }
    ((factor, inverse),) = factor_blocks([blocks[0, 0]])
    panel[:, :SIDE] = jnp.where(square_masks()[0], factor, 0.0)
    if n > 1:
        row = dot_nn(inverse, jnp.concatenate([blocks[0, j] for j in range(1, n)], axis=1))
        panel[:, SIDE:] = row
        less = dot_tn(row, row)
        for i, j in block_pairs(n - 1):
            at = (slice(i*SIDE, (i+1)*SIDE), slice(j*SIDE, (j+1)*SIDE))
            after[0][at] = blocks[i + 1, j + 1] - less[at]


def local_factor(packed, n):
    panels, left = [], packed
    for k in range(n):
        m = n - k
        shapes = [(SIDE, m*SIDE)] + ([((m-1)*SIDE, (m-1)*SIDE)] if m > 1 else [])
        panel, *left = local_call(functools.partial(local_kernel, m, k == 0), "local_factor", shapes, [], left, cost=LOCAL_COST)
        left = left[0] if left else None
        panels.append(panel)
    return panels


def factor_kernel(n, weight, own_ref, other_ref, *refs):
    local, (out_ref, growth_ref) = refs[:n], refs[n:]
    high_half = parity()
    own, other = own_ref[...], other_ref[...]
    total = unpack_blocks(jnp.concatenate([jnp.where(high_half, other, own), jnp.where(high_half, own, other)], axis=0), n)
    diag = square_masks()[1]
    rest = {j: [local[i][:, (j-i)*SIDE:(j-i+1)*SIDE] for i in range(j + 1)] for j in range(n)}
    for k in range(n):
        ((factor, inverse),) = factor_blocks([total[k, k]])
        growth_ref[0, k*SIDE:(k+1)*SIDE] = jnp.log(jnp.sum(jnp.where(diag, factor, 0.0), axis=0))
        if k + 1 < n:
            row = dot_nn(inverse, jnp.concatenate([total[k, j] for j in range(k + 1, n)], axis=1))
            for i in range(k + 1, n):
                less = dot_tn(row[:, (i-k-1)*SIDE:(i-k)*SIDE], row[:, (i-k-1)*SIDE:])
                for j in range(i, n):
                    total[i, j] = total[i, j] - less[:, (j-i)*SIDE:(j-i+1)*SIDE]
        answer = dot_nt(jnp.concatenate(rest[k], axis=0), inverse)
        out_ref[:(k+1)*SIDE, k*SIDE:(k+1)*SIDE] = weight * answer
        if k + 1 < n:
            out_ref[(k+1)*SIDE:, k*SIDE:(k+1)*SIDE] = jnp.zeros(((n-k-1)*SIDE, SIDE), jnp.float32)
            less = dot_nn(answer, row)
            for j in range(k + 1, n):
                at = (j-k-1)*SIDE
                rest[j] = [
                    part - less[i*SIDE:(i+1)*SIDE, at:at+SIDE] if i <= k else part for i, part in enumerate(rest[j])
                ]


def factor_call(own, other, local, k, weight):
    out, growth = local_call(
        functools.partial(factor_kernel, k // SIDE, weight), "factor", [(k, k), (1, k)], [], own, other, *local
    )
    return out, growth[0]


def pick(flag, first, second):
    return jnp.where(flag, first, second)


def roll(x, shift):
    return pltpu.roll(x, shift % LANES, 1)


def lane_index(like):
    return lax.broadcasted_iota(jnp.int32, like.shape, like.ndim - 1)


def chunk(g, height):
    return pl.ds(pl.multiple_of(g * height, height), height)


def own_rows(tangents, g, height):
    return [[tangents[f, pl.ds(g * height * SUB + r, height, stride=SUB), :] for r in range(SUB)] for f in range(2)]


def own_coeffs(coeffs):
    return [[spread_row(coeffs[f], r) for r in range(SUB)] for f in range(2)]


def tall(x, height):
    return jnp.concatenate([x] * (height // SUB), axis=0)


def edge_kernel(fields, height, tangents_hbm, coeffs_hbm, last_out, first_out, near, far, far_late, tangents, coeffs, sems):
    chunks = fields // height
    span = height * SUB
    loads = [
        pltpu.make_async_copy(tangents_hbm.at[:, pl.ds(g * span, span), :], tangents.at[:, pl.ds(g * span, span), :], sems.at[g])
        for g in range(chunks)
    ]
    small = pltpu.make_async_copy(coeffs_hbm, coeffs, sems.at[chunks])
    for load in loads + [small]:
        load.start()
    odd = lax.axis_index("tile") % 2 == 1

    def send(at, rows):
        cell = lane_index(rows[0][0]) // SUB
        cells = LANES // SUB
        last, first = None, None
        for f in range(2):
            for r in range(SUB):
                s = f * SUB + r
                turned = roll(rows[f][r], (s + 1) * SUB)
                last = turned if last is None else jnp.where(cell == s, turned, last)
                first = turned if first is None else jnp.where(cell == (s + 1) % cells, turned, first)
        first = roll(first, -SUB)
        last_out[at, :] = last
        first_out[at, :] = first
        half = cell % SUB < STEPS
        to_above = jnp.where(half, last, roll(first, STEPS * SUB))
        to_below = jnp.where(half, roll(last, -STEPS * SUB), first)
        near[0, at, :] = pick(odd, to_above, to_below)
        far[0, at, :] = pick(odd, to_below, to_above)
        for f in range(2):
            count = STEPS - f
            for j in range(count):
                top, bottom = rows[f][j], rows[f][SUB - count + j]
                row = f * STEPS + j
                near[1 + row, at, :] = pick(odd, top, bottom)
                if row < EARLY_ROWS:
                    far[1 + row, at, :] = pick(odd, bottom, top)
                else:
                    far_late[row - EARLY_ROWS, at, :] = pick(odd, bottom, top)

    for g, load in enumerate(loads):
        load.wait()
        send(pl.ds(g * height, height), own_rows(tangents, g, height))
    small.wait()
    send(pl.ds(fields, SUB), own_coeffs(coeffs))


def row_mirror_kernel(last, first, mirrored):
    tile, tiles = lax.axis_index("tile"), lax.axis_size("tile")

    @pl.when((tile == 0) | (tile == tiles - 1))
    def _():
        for i, ref in enumerate((last, first)):
            own = ref[...]
            cell = lane_index(own) // SUB % SUB
            turned = roll(own, -7 * SUB)
            for s in range(1, SUB):
                turned = jnp.where(cell == s, roll(own, (2 * s - 7) * SUB), turned)
            mirrored[i] = turned

    @pl.when((tile != 0) & (tile != tiles - 1))
    def _():
        mirrored[...] = jnp.zeros(mirrored.shape, jnp.float32)


def column_kernel(last, first, mirrored, near, far, strips, near_out, far_out):
    tile, tiles = lax.axis_index("tile"), lax.axis_size("tile")
    odd, at_top, at_bottom = tile % 2 == 1, tile == 0, tile == tiles - 1
    grp_odd = lax.axis_index("grp") % 2 == 1
    one, two = near[0], far[0]
    lane = lane_index(one)
    cell, low, inner = lane // SUB % SUB, lane < LANES // 2, lane % SUB < STEPS
    half = cell < STEPS
    above, below = pick(odd, one, two), pick(odd, two, one)
    outside = (half & at_bottom) | (~half & at_top)
    received = (jnp.where(half, below, roll(above, STEPS * SUB)), jnp.where(half, roll(below, -STEPS * SUB), above))
    sides = []
    for i, ref in enumerate((last, first)):
        own, more = ref[...], jnp.where(outside, mirrored[i], received[i])
        fast = jnp.where(low, own, roll(more, LANES // 2))
        slow = jnp.where(low, roll(own, LANES // 2), more)
        strips[2 * i] = fast
        strips[2 * i + 1] = slow
        sides.append((fast, slow))
    to_left = jnp.where(inner, sides[1][0], roll(sides[1][1], STEPS))
    to_right = jnp.where(inner, roll(sides[0][0], -STEPS), sides[0][1])
    near_out[...] = pick(grp_odd, to_left, to_right)
    far_out[...] = pick(grp_odd, to_right, to_left)


def strip_neighbours(last, first, halo, wanted):
    c = lane_index(last) % SUB
    end, begin = c == SUB - 1, c == 0
    out = []
    sides = (lambda: (last, roll(halo, 7), None), lambda: (first, None, roll(halo, -7)), lambda: (halo, roll(first, 7), roll(last, -7)))
    for side in sides[:wanted]:
        x, after, before = side()
        right, left = roll(x, -1), roll(x, 1)
        if after is not None:
            right = jnp.where(end, after, right)
        if before is not None:
            left = jnp.where(begin, before, left)
        out.append(roll(x, SUB) + roll(x, -SUB) + right + left)
    return out


def advance(fast, slow, around, gain, cross):
    return gain * fast + diffusion * around + cross * slow


def relax(fast, slow):
    return (1.0 - slow_rate) * slow + slow_rate * fast


def column_mirror_kernel(strips, mirrored):
    grp, grps = lax.axis_index("grp"), lax.axis_size("grp")

    @pl.when((grp == 0) | (grp == grps - 1))
    def _():
        for f in range(2):
            tail, start = strips[f], strips[2 + f]
            c = lane_index(tail) % SUB
            turned = roll(tail, -7)
            for s in range(STEPS):
                turned = jnp.where(c == s, roll(tail, 2 * s - 7), turned)
                turned = jnp.where(c == 7 - s, roll(start, 7 - 2 * s), turned)
            mirrored[f] = turned

    @pl.when((grp != 0) & (grp != grps - 1))
    def _():
        mirrored[...] = jnp.zeros(mirrored.shape, jnp.float32)


def gram_kernel(fields, height, middle_gram, strips, mirrored, near, far, gram, halo, ends):
    grp, grps = lax.axis_index("grp"), lax.axis_size("grp")
    grp_odd = grp % 2 == 1
    one, two = near[...], far[...]
    lane = lane_index(one)
    c = lane % SUB
    inner = c < STEPS
    left, right = pick(grp_odd, one, two), pick(grp_odd, two, one)
    outside = (inner & (grp == grps - 1)) | (~inner & (grp == 0))
    halo[0] = jnp.where(outside, mirrored[0], jnp.where(inner, right, roll(left, STEPS)))
    halo[1] = jnp.where(outside, mirrored[1], jnp.where(inner, roll(right, -STEPS), left))

    def parts(f, at):
        return [strips[f, at, :], strips[2 + f, at, :], halo[f, at, :]]

    gains = [tall(x + (1.0 - 4.0 * diffusion), height) for x in parts(0, pl.ds(fields, SUB))]
    crosses = [tall(x, height) for x in parts(1, pl.ds(fields, SUB))]
    places = [pl.ds(at, height) for at in range(0, fields, height)]
    held = [(parts(0, at), parts(1, at)) for at in places]
    for step in range(STEPS):
        wanted = 3 if step + 1 < STEPS else 2
        for i, (fast, slow) in enumerate(held):
            around = strip_neighbours(*fast, wanted)
            moved = [advance(fast[p], slow[p], around[p], gains[p], crosses[p]) for p in range(wanted)]
            held[i] = (moved, [relax(fast[p], slow[p]) for p in range(wanted)])
    for at, pair in zip(places, held):
        l = lane_index(pair[0][0])
        joined = [jnp.where(l % SUB < STEPS, side[1], side[0]) for side in pair]
        ends[at, :] = jnp.where(l < LANES // 2, joined[0], roll(joined[1], LANES // 2))

    whole = middle_gram[...] + gram_of(ends[...])
    for index, (i, j) in enumerate(block_pairs(fields // SIDE)):
        row, half = divmod(index, 2)
        gram[row * SIDE:(row + 1) * SIDE, half * SIDE:(half + 1) * SIDE] = whole[
            i * SIDE:(i + 1) * SIDE, j * SIDE:(j + 1) * SIDE
        ]


def extended_rows(own, near, far, far_late, at):
    tile, tiles = lax.axis_index("tile"), lax.axis_size("tile")
    odd, at_top, at_bottom = tile % 2 == 1, tile == 0, tile == tiles - 1
    out = []
    for f in range(2):
        count = STEPS - f
        rows = dict(enumerate(own[f]))
        for j in range(count):
            row = f * STEPS + j
            one = near[1 + row, at, :]
            two = far[1 + row, at, :] if row < EARLY_ROWS else far_late[row - EARLY_ROWS, at, :]
            rows[j - count] = pick(at_top, own[f][count - 1 - j], pick(odd, one, two))
            rows[SUB + j] = pick(at_bottom, own[f][SUB - 1 - j], pick(odd, two, one))
        out.append(rows)
    return out


def evolve_kernel(fields, height, tangents, coeffs, near, far, far_late, middle_gram, row_coeffs, cells):
    coeff_rows = extended_rows(own_coeffs(coeffs), near, far, far_late, pl.ds(fields, SUB))
    for f in range(2):
        for r in range(1 - STEPS, SUB + STEPS - 1):
            row_coeffs[f, r + STEPS - 1, :, :] = coeff_rows[f][r] + (1.0 - 4.0 * diffusion) * (1 - f)

    for g in range(fields // height):
        at = chunk(g, height)
        fast, slow = extended_rows(own_rows(tangents, g, height), near, far, far_late, at)
        for step in range(1, STEPS + 1):
            margin = STEPS - step
            new_fast = {}
            for r in range(-margin, SUB + margin):
                around = fast[r - 1] + fast[r + 1] + roll(fast[r], 1) + roll(fast[r], -1)
                gain, cross = (tall(row_coeffs[f, r + STEPS - 1], height) for f in range(2))
                new_fast[r] = advance(fast[r], slow[r], around, gain, cross)
            keep = max(margin - 1, 0)
            slow = {r: relax(fast[r], slow[r]) for r in range(-keep, SUB + keep)}
            fast = new_fast
        lane = lane_index(fast[0])
        middle = (lane >= STEPS) & (lane < LANES - STEPS)
        for f, rows in enumerate((fast, slow)):
            for r in range(SUB):
                cells[at, (f * SUB + r) * LANES:(f * SUB + r + 1) * LANES] = jnp.where(middle, rows[r], 0.0)

    middle_gram[...] = gram_of(cells[...])


def local_call(body, name, out_shapes, scratch, *args, hbm=False, vmem=VMEM_BYTES, cost=None):
    spec = pl.BlockSpec(memory_space=pltpu.VMEM)
    return pl.pallas_call(
        body,
        out_shape=[jax.ShapeDtypeStruct(s, jnp.float32) for s in out_shapes],
        in_specs=[pl.BlockSpec(memory_space=pltpu.HBM) if hbm else spec] * len(args),
        out_specs=[spec] * len(out_shapes),
        scratch_shapes=[pltpu.VMEM(s, jnp.float32) if isinstance(s, tuple) else s for s in scratch],
        compiler_params=pltpu.CompilerParams(vmem_limit_bytes=vmem),
        name=name,
        cost_estimate=cost,
    )(*args)


def swap(cells, axis, first, close=False):
    count = lax.axis_size(axis)
    pairs = [(i, i + 1) for i in range(first, count - 1, 2)]
    if close and first:
        pairs.append((0, count - 1))
    return lax.ppermute(cells, axis, pairs + [(b, a) for a, b in pairs])


def exchange(cells, grp_bit, tile_bit):
    grps, tiles = lax.axis_size("grp"), lax.axis_size("tile")
    moves = [(g * tiles + t, (g ^ grp_bit) * tiles + (t ^ tile_bit)) for g in range(grps) for t in range(tiles)]
    return lax.ppermute(cells, ("grp", "tile"), moves)


def parity():
    bits = lax.axis_index("grp") ^ lax.axis_index("tile")
    shift = 1
    while shift < max(lax.axis_size("grp"), lax.axis_size("tile")):
        bits = bits ^ (bits >> shift)
        shift *= 2
    return (bits & 1) == 1


def sum_blocks(packed, beside):
    half = packed.shape[0] // 2
    high_half = parity()
    low, high = packed[:half], packed[half:]
    part = jnp.where(high_half, high, low) + exchange(jnp.where(high_half, low, high), 0, 1)
    for axis in ("grp", "tile"):
        bit = 1 if axis == "grp" else 2
        while bit < lax.axis_size(axis):
            if axis == "tile" and 2 * bit >= lax.axis_size(axis):
                part, beside = lax.optimization_barrier((part, beside))
            part = part + (exchange(part, bit, 1) if axis == "grp" else exchange(part, 0, bit + 1))
            bit *= 2
    return part, exchange(part, 0, 1), beside


def per_device(tangents, reaction_self, reaction_cross):
    fields = tangents.shape[1]
    padded = fields + SUB
    rows = tangents.reshape(2, fields * tangents.shape[2], tangents.shape[3])
    strip = (padded, LANES)
    early, late = (1 + EARLY_ROWS,) + strip, (2 * STEPS - 1 - EARLY_ROWS,) + strip
    inputs = (rows, jnp.stack([reaction_self, reaction_cross]))
    last, first, near, far, far_late = local_call(
        functools.partial(edge_kernel, fields, HEIGHT_EDGE), "edges", [strip] * 2 + [(2 * STEPS, padded, LANES), early, late],
        [a.shape for a in inputs] + [pltpu.SemaphoreType.DMA((fields // HEIGHT_EDGE + 1,))], *inputs,
        hbm=True, vmem=EDGE_VMEM_BYTES,
    )
    near, far, far_late = swap(near, "tile", 0), swap(far, "tile", 1), swap(far_late, "tile", 1)
    (row_mirror,) = local_call(row_mirror_kernel, "row_mirror", [(2,) + strip], [], last, first)
    strips, near_cols, far_cols = local_call(
        column_kernel, "columns", [(4,) + strip, strip, strip], [], last, first, row_mirror, near, far
    )
    (column_mirror,) = local_call(column_mirror_kernel, "column_mirror", [(2,) + strip], [], strips)
    far_cols = swap(far_cols, "grp", 1, close=True)
    near_cols = swap(near_cols, "grp", 0)
    (middle_gram,) = local_call(
        functools.partial(evolve_kernel, fields, HEIGHT_EVOLVE), "evolve", [(fields, fields)],
        [(2, SUB + 2 * STEPS - 2, SUB, LANES), (fields, 2 * SUB * LANES)], *inputs, near, far, far_late,
    )
    side_blocks = fields // SIDE
    blocks = side_blocks * (side_blocks + 1) // 2
    (packed,) = local_call(
        functools.partial(gram_kernel, fields, HEIGHT_STRIP), "gram", [((blocks + 1) // 2 * SIDE, 2 * SIDE)],
        [(2,) + strip, (fields, LANES)], middle_gram, strips, column_mirror, near_cols, far_cols,
    )
    block_total = lax.axis_size("grp") * lax.axis_size("tile")
    corrections, growth = factor_call(*sum_blocks(packed, local_factor(packed, side_blocks)), fields, math.sqrt(block_total))
    return (corrections, growth)


def solution(mesh):
    in_specs = (P(None, None, "tile", "grp"), P("tile", "grp"), P("tile", "grp"))
    out_specs = (P(("grp", "tile"), None), P())
    return jax.shard_map(
        per_device, mesh=mesh, in_specs=in_specs, out_specs=out_specs, check_vma=False
    )
```

```python
import functools
import math

import jax
import jax.numpy as jnp
from jax import lax
from jax.experimental import pallas as pl
from jax.experimental.pallas import tpu as pltpu
from jax.sharding import PartitionSpec as P


STEPS = 4
diffusion = 0.2
slow_rate = 0.05
HEIGHT_EDGE = 96
HEIGHT_STRIP = 8
HEIGHT_EVOLVE = 24
SIDE = 64
VMEM_BYTES = 24 * 1024 * 1024
EARLY_ROWS = 3
LOCAL_COST = pl.CostEstimate(flops=10**9, bytes_accessed=10**6, transcendentals=0)
EDGE_VMEM_BYTES = 52 * 1024 * 1024
LANES = 128
SUB = 8
HI = lax.Precision.HIGHEST

def dot_nn(a, b):
    return lax.dot_general(a, b, (((1,), (0,)), ((), ())), precision=HI, preferred_element_type=jnp.float32)
def dot_tn(a, b):
    return lax.dot_general(a, b, (((0,), (0,)), ((), ())), precision=HI, preferred_element_type=jnp.float32)
def dot_nt(a, b):
    return lax.dot_general(a, b, (((1,), (1,)), ((), ())), precision=HI, preferred_element_type=jnp.float32)

def gram_of(cells):
    high = cells.astype(jnp.bfloat16)
    left = cells - high.astype(jnp.float32)
    middle = left.astype(jnp.bfloat16)
    low = (left - middle.astype(jnp.float32)).astype(jnp.bfloat16)

    def product(a, b):
        return lax.dot_general(a, b, (((1,), (1,)), ((), ())), preferred_element_type=jnp.float32)

    mixed = product(middle, high) + product(low, high)
    return product(high, high) + product(middle, middle) + (mixed + mixed.T)


def block_pairs(n):
    return [(i, j) for i in range(n) for j in range(i, n)]

def square_masks():
    row = lax.broadcasted_iota(jnp.int32, (SIDE, SIDE), 0)
    col = lax.broadcasted_iota(jnp.int32, (SIDE, SIDE), 1)
    return row, col


def packed_rows(n):
    count = n // 2 + n * (n - 1) // 2 + 1
    return count * SIDE // 2


def pack_blocks(whole, n):
    row, col = square_masks()

    def block(i, j):
        return whole[i*SIDE:(i+1)*SIDE, j*SIDE:(j+1)*SIDE]

    squares, below = [], jnp.zeros((SIDE, SIDE), jnp.float32)
    for m in range(n // 2):
        second = block(2*m + 1, 2*m + 1)
        line = jnp.sum(jnp.where(row == col, second, 0.0), axis=0, keepdims=True)
        at = SIDE - 1 - 2*m
        turned = jnp.concatenate([line[:, at:], line[:, :at]], axis=1)
        below = jnp.where(row == at, line, jnp.where(row == at - 1, turned, below))
        squares.append(jnp.where(row <= col, block(2*m, 2*m), second))
    squares += [block(i, j) for i, j in block_pairs(n) if i < j]
    squares.append(jnp.where(row <= col, block(n - 1, n - 1), below) if n % 2 else below)
    lines = [jnp.concatenate(squares[i:i+2], axis=1) for i in range(0, len(squares) - 1, 2)]
    if len(squares) % 2:
        lines.append(jnp.concatenate([squares[-1][:SIDE // 2], squares[-1][SIDE // 2:]], axis=1))
    return jnp.concatenate(lines, axis=0)


def unpack_blocks(packed, n):
    row, col = square_masks()
    count = packed.shape[0] * 2 // SIDE
    squares = []
    for i in range(count // 2):
        squares += [packed[i*SIDE:(i+1)*SIDE, :SIDE], packed[i*SIDE:(i+1)*SIDE, SIDE:]]
    if count % 2:
        rest = packed[count // 2 * SIDE:]
        squares.append(jnp.concatenate([rest[:, :SIDE], rest[:, SIDE:]], axis=0))
    last = squares[-1]
    blocks = dict(zip([(i, j) for i, j in block_pairs(n) if i < j], squares[n // 2:-1]))
    for m in range(n // 2):
        both, other = squares[m], squares[m].T
        at = SIDE - 1 - 2*m
        line, turned = last[at:at + 1], last[at - 1:at]
        turned = jnp.concatenate([turned[:, SIDE - at:], turned[:, :SIDE - at]], axis=1)
        line = jnp.where(col[:1] < at, line, turned)
        blocks[2*m, 2*m] = jnp.where(row <= col, both, other)
        blocks[2*m + 1, 2*m + 1] = jnp.where(row > col, both, jnp.where(row < col, other, line))
    if n % 2:
        blocks[n - 1, n - 1] = jnp.where(row <= col, last, last.T)
    return blocks


def spread_lane(x, lane):
    return jnp.broadcast_to(x[:, lane:lane+1], (x.shape[0], LANES))
def spread_row(x, row):
    return jnp.broadcast_to(x[row:row+1, :], (SUB, x.shape[1]))

def factor_blocks(blocks):
    groups = SIDE // SUB
    eye = (lax.broadcasted_iota(jnp.int32, (SIDE, SIDE), 0) == lax.broadcasted_iota(jnp.int32, (SIDE, SIDE), 1)).astype(jnp.float32)
    sub = lax.broadcasted_iota(jnp.int32, (SUB, LANES), 0)
    states = []
    for d in blocks:
        whole = jnp.concatenate([d, eye], axis=1)
        states.append([whole[g*SUB:(g+1)*SUB] for g in range(groups)])
    done = [[] for _ in blocks]
    ready = [None for _ in blocks]
    for p in range(groups):
        for s, v in enumerate(states):
            spread = {(g, c): spread_lane(v[g], p*SUB + c) for g in range(p + 1, groups) for c in range(SUB)}
            if p + 1 < groups:
                coming = [spread_lane(v[p + 1], (p + 1)*SUB + c) for c in range(SUB)]
            columns = ready[s] or [spread_lane(v[p], p*SUB + c) for c in range(SUB)]
            rows = [spread_row(v[p], c) for c in range(SUB)]
            pivots = {(a, c): spread_row(columns[c], a) for c in range(SUB) for a in range(c, SUB)}
            mult, inverses, scale = {}, [], []
            for c in range(SUB):
                inverses.append(1.0 / pivots[c, c])
                scale.append(lax.rsqrt(pivots[c, c]))
                for a in range(c + 1, SUB):
                    mult[a, c] = pivots[a, c] * inverses[c]
                    rows[a] = rows[a] - mult[a, c] * rows[c]
                    for b in range(c + 1, a + 1):
                        pivots[a, b] = pivots[a, b] - mult[a, c] * pivots[b, c]
            scaled = [rows[c] * scale[c] for c in range(SUB)]
            panel = scaled[0]
            for c in range(1, SUB):
                panel = jnp.where(sub == c, scaled[c], panel)
            done[s].append(panel)
            for g in range(p + 1, min(p + 3, groups)):
                cols = [spread[g, c] for c in range(SUB)]
                for c in range(SUB):
                    for a in range(c + 1, SUB):
                        cols[a] = cols[a] - mult[a, c] * cols[c]
                    if g == p + 1:
                        part = cols[c] * inverses[c]
                        coming = [x - part * spread_row(cols[c], b) for b, x in enumerate(coming)]
                    v[g] = v[g] - (cols[c] * scale[c]) * scaled[c]
                if g == p + 1:
                    ready[s] = coming
            if p + 3 < groups:
                solved = [scaled[c] * scale[c] for c in range(SUB)]
                for c in reversed(range(SUB)):
                    for a in range(c):
                        solved[a] = solved[a] - mult[c, a] * solved[c]
                for g in range(p + 3, groups):
                    for c in range(SUB):
                        v[g] = v[g] - spread[g, c] * solved[c]
    out = []
    for panels in done:
        whole = jnp.concatenate(panels, axis=0)
        out.append((whole[:, :SIDE], whole[:, SIDE:]))
    return out

def local_kernel(n, gram, panel, *after):
    blocks = {(i, j): gram[i*SIDE:(i+1)*SIDE, j*SIDE:(j+1)*SIDE] for i, j in block_pairs(n)}
    row, col = square_masks()
    ((factor, inverse),) = factor_blocks([blocks[0, 0]])
    panel[:, :SIDE] = jnp.where(row <= col, factor, 0.0)
    if n > 1:
        row = dot_nn(inverse, jnp.concatenate([blocks[0, j] for j in range(1, n)], axis=1))
        panel[:, SIDE:] = row
        less = dot_tn(row, row)
        for i, j in block_pairs(n - 1):
            at = (slice(i*SIDE, (i+1)*SIDE), slice(j*SIDE, (j+1)*SIDE))
            after[0][at] = blocks[i + 1, j + 1] - less[at]


def local_factor(gram, n):
    panels, left = [], gram
    for k in range(n):
        m = n - k
        shapes = [(SIDE, m*SIDE)] + ([((m-1)*SIDE, (m-1)*SIDE)] if m > 1 else [])
        panel, *left = local_call(functools.partial(local_kernel, m), "local_factor", shapes, [], left, cost=LOCAL_COST)
        left = left[0] if left else None
        panels.append(panel)
    return panels


def factor_kernel(n, weight, own_ref, other_ref, *refs):
    local, (out_ref, growth_ref) = refs[:n], refs[n:]
    high_half = parity()
    own, other = own_ref[...], other_ref[...]
    total = unpack_blocks(jnp.concatenate([jnp.where(high_half, other, own), jnp.where(high_half, own, other)], axis=0), n)
    row, col = square_masks()
    diag = row == col
    rest = {j: [local[i][:, (j-i)*SIDE:(j-i+1)*SIDE] for i in range(j + 1)] for j in range(n)}
    for k in range(n):
        ((factor, inverse),) = factor_blocks([total[k, k]])
        growth_ref[0, k*SIDE:(k+1)*SIDE] = jnp.log(jnp.sum(jnp.where(diag, factor, 0.0), axis=0))
        if k + 1 < n:
            row = dot_nn(inverse, jnp.concatenate([total[k, j] for j in range(k + 1, n)], axis=1))
            for i in range(k + 1, n):
                less = dot_tn(row[:, (i-k-1)*SIDE:(i-k)*SIDE], row[:, (i-k-1)*SIDE:])
                for j in range(i, n):
                    total[i, j] = total[i, j] - less[:, (j-i)*SIDE:(j-i+1)*SIDE]
        answer = dot_nt(jnp.concatenate(rest[k], axis=0), inverse)
        out_ref[:(k+1)*SIDE, k*SIDE:(k+1)*SIDE] = weight * answer
        if k + 1 < n:
            out_ref[(k+1)*SIDE:, k*SIDE:(k+1)*SIDE] = jnp.zeros(((n-k-1)*SIDE, SIDE), jnp.float32)
            less = dot_nn(answer, row)
            for j in range(k + 1, n):
                at = (j-k-1)*SIDE
                rest[j] = [
                    part - less[i*SIDE:(i+1)*SIDE, at:at+SIDE] if i <= k else part for i, part in enumerate(rest[j])
                ]


def factor_call(own, other, local, k, weight):
    out, growth = local_call(
        functools.partial(factor_kernel, k // SIDE, weight), "factor", [(k, k), (1, k)], [], own, other, *local
    )
    return out, growth[0]


def pick(flag, first, second):
    return jnp.where(flag, first, second)


def roll(x, shift):
    return pltpu.roll(x, shift % LANES, 1)


def lane_index(like):
    return lax.broadcasted_iota(jnp.int32, like.shape, like.ndim - 1)


def chunk(g, height):
    return pl.ds(pl.multiple_of(g * height, height), height)


def own_rows(tangents, g, height):
    return [[tangents[f, pl.ds(g * height * SUB + r, height, stride=SUB), :] for r in range(SUB)] for f in range(2)]


def own_coeffs(coeffs):
    return [[spread_row(coeffs[f], r) for r in range(SUB)] for f in range(2)]


def tall(x, height):
    return jnp.concatenate([x] * (height // SUB), axis=0)


def edge_kernel(fields, height, tangents_hbm, coeffs_hbm, last_out, first_out, near, far, far_late, tangents, coeffs, sems):
    chunks = fields // height
    span = height * SUB
    loads = [
        pltpu.make_async_copy(tangents_hbm.at[:, pl.ds(g * span, span), :], tangents.at[:, pl.ds(g * span, span), :], sems.at[g])
        for g in range(chunks)
    ]
    small = pltpu.make_async_copy(coeffs_hbm, coeffs, sems.at[chunks])
    for load in loads + [small]:
        load.start()
    odd = lax.axis_index("tile") % 2 == 1

    def send(at, rows):
        cell = lane_index(rows[0][0]) // SUB
        cells = LANES // SUB
        last, first = None, None
        for f in range(2):
            for r in range(SUB):
                s = f * SUB + r
                turned = roll(rows[f][r], (s + 1) * SUB)
                last = turned if last is None else jnp.where(cell == s, turned, last)
                first = turned if first is None else jnp.where(cell == (s + 1) % cells, turned, first)
        first = roll(first, -SUB)
        last_out[at, :] = last
        first_out[at, :] = first
        half = cell % SUB < STEPS
        to_above = jnp.where(half, last, roll(first, STEPS * SUB))
        to_below = jnp.where(half, roll(last, -STEPS * SUB), first)
        near[0, at, :] = pick(odd, to_above, to_below)
        far[0, at, :] = pick(odd, to_below, to_above)
        for f in range(2):
            count = STEPS - f
            for j in range(count):
                top, bottom = rows[f][j], rows[f][SUB - count + j]
                row = f * STEPS + j
                near[1 + row, at, :] = pick(odd, top, bottom)
                if row < EARLY_ROWS:
                    far[1 + row, at, :] = pick(odd, bottom, top)
                else:
                    far_late[row - EARLY_ROWS, at, :] = pick(odd, bottom, top)

    for g, load in enumerate(loads):
        load.wait()
        send(pl.ds(g * height, height), own_rows(tangents, g, height))
    small.wait()
    send(pl.ds(fields, SUB), own_coeffs(coeffs))


def row_mirror_kernel(last, first, mirrored):
    tile, tiles = lax.axis_index("tile"), lax.axis_size("tile")

    @pl.when((tile == 0) | (tile == tiles - 1))
    def _():
        for i, ref in enumerate((last, first)):
            own = ref[...]
            cell = lane_index(own) // SUB % SUB
            turned = roll(own, -7 * SUB)
            for s in range(1, SUB):
                turned = jnp.where(cell == s, roll(own, (2 * s - 7) * SUB), turned)
            mirrored[i] = turned

    @pl.when((tile != 0) & (tile != tiles - 1))
    def _():
        mirrored[...] = jnp.zeros(mirrored.shape, jnp.float32)


def column_kernel(last, first, mirrored, near, far, strips, near_out, far_out):
    tile, tiles = lax.axis_index("tile"), lax.axis_size("tile")
    odd, at_top, at_bottom = tile % 2 == 1, tile == 0, tile == tiles - 1
    grp_odd = lax.axis_index("grp") % 2 == 1
    one, two = near[0], far[0]
    lane = lane_index(one)
    cell, low, inner = lane // SUB % SUB, lane < LANES // 2, lane % SUB < STEPS
    half = cell < STEPS
    above, below = pick(odd, one, two), pick(odd, two, one)
    outside = (half & at_bottom) | (~half & at_top)
    received = (jnp.where(half, below, roll(above, STEPS * SUB)), jnp.where(half, roll(below, -STEPS * SUB), above))
    sides = []
    for i, ref in enumerate((last, first)):
        own, more = ref[...], jnp.where(outside, mirrored[i], received[i])
        fast = jnp.where(low, own, roll(more, LANES // 2))
        slow = jnp.where(low, roll(own, LANES // 2), more)
        strips[2 * i] = fast
        strips[2 * i + 1] = slow
        sides.append((fast, slow))
    to_left = jnp.where(inner, sides[1][0], roll(sides[1][1], STEPS))
    to_right = jnp.where(inner, roll(sides[0][0], -STEPS), sides[0][1])
    near_out[...] = pick(grp_odd, to_left, to_right)
    far_out[...] = pick(grp_odd, to_right, to_left)


def strip_neighbours(last, first, halo, wanted):
    c = lane_index(last) % SUB
    end, begin = c == SUB - 1, c == 0
    out = []
    sides = (lambda: (last, roll(halo, 7), None), lambda: (first, None, roll(halo, -7)), lambda: (halo, roll(first, 7), roll(last, -7)))
    for side in sides[:wanted]:
        x, after, before = side()
        right, left = roll(x, -1), roll(x, 1)
        if after is not None:
            right = jnp.where(end, after, right)
        if before is not None:
            left = jnp.where(begin, before, left)
        out.append(roll(x, SUB) + roll(x, -SUB) + right + left)
    return out


def advance(fast, slow, around, gain, cross):
    return gain * fast + diffusion * around + cross * slow


def relax(fast, slow):
    return (1.0 - slow_rate) * slow + slow_rate * fast


def column_mirror_kernel(strips, mirrored):
    grp, grps = lax.axis_index("grp"), lax.axis_size("grp")

    @pl.when((grp == 0) | (grp == grps - 1))
    def _():
        for f in range(2):
            tail, start = strips[f], strips[2 + f]
            c = lane_index(tail) % SUB
            turned = roll(tail, -7)
            for s in range(STEPS):
                turned = jnp.where(c == s, roll(tail, 2 * s - 7), turned)
                turned = jnp.where(c == 7 - s, roll(start, 7 - 2 * s), turned)
            mirrored[f] = turned

    @pl.when((grp != 0) & (grp != grps - 1))
    def _():
        mirrored[...] = jnp.zeros(mirrored.shape, jnp.float32)


def gram_kernel(fields, height, middle_gram, strips, mirrored, near, far, packed, gram, halo, ends):
    grp, grps = lax.axis_index("grp"), lax.axis_size("grp")
    grp_odd = grp % 2 == 1
    one, two = near[...], far[...]
    lane = lane_index(one)
    c = lane % SUB
    inner = c < STEPS
    left, right = pick(grp_odd, one, two), pick(grp_odd, two, one)
    outside = (inner & (grp == grps - 1)) | (~inner & (grp == 0))
    halo[0] = jnp.where(outside, mirrored[0], jnp.where(inner, right, roll(left, STEPS)))
    halo[1] = jnp.where(outside, mirrored[1], jnp.where(inner, roll(right, -STEPS), left))

    def parts(f, at):
        return [strips[f, at, :], strips[2 + f, at, :], halo[f, at, :]]

    gains = [tall(x + (1.0 - 4.0 * diffusion), height) for x in parts(0, pl.ds(fields, SUB))]
    crosses = [tall(x, height) for x in parts(1, pl.ds(fields, SUB))]
    places = [pl.ds(at, height) for at in range(0, fields, height)]
    held = [(parts(0, at), parts(1, at)) for at in places]
    for step in range(STEPS):
        wanted = 3 if step + 1 < STEPS else 2
        for i, (fast, slow) in enumerate(held):
            around = strip_neighbours(*fast, wanted)
            moved = [advance(fast[p], slow[p], around[p], gains[p], crosses[p]) for p in range(wanted)]
            held[i] = (moved, [relax(fast[p], slow[p]) for p in range(wanted)])
    for at, pair in zip(places, held):
        l = lane_index(pair[0][0])
        joined = [jnp.where(l % SUB < STEPS, side[1], side[0]) for side in pair]
        ends[at, :] = jnp.where(l < LANES // 2, joined[0], roll(joined[1], LANES // 2))

    whole = middle_gram[...] + gram_of(ends[...])
    gram[...] = whole
    packed[...] = pack_blocks(whole, fields // SIDE)


def extended_rows(own, near, far, far_late, at):
    tile, tiles = lax.axis_index("tile"), lax.axis_size("tile")
    odd, at_top, at_bottom = tile % 2 == 1, tile == 0, tile == tiles - 1
    out = []
    for f in range(2):
        count = STEPS - f
        rows = dict(enumerate(own[f]))
        for j in range(count):
            row = f * STEPS + j
            one = near[1 + row, at, :]
            two = far[1 + row, at, :] if row < EARLY_ROWS else far_late[row - EARLY_ROWS, at, :]
            rows[j - count] = pick(at_top, own[f][count - 1 - j], pick(odd, one, two))
            rows[SUB + j] = pick(at_bottom, own[f][SUB - 1 - j], pick(odd, two, one))
        out.append(rows)
    return out


def evolve_kernel(fields, height, tangents, coeffs, near, far, far_late, middle_gram, row_coeffs, cells):
    coeff_rows = extended_rows(own_coeffs(coeffs), near, far, far_late, pl.ds(fields, SUB))
    for f in range(2):
        for r in range(1 - STEPS, SUB + STEPS - 1):
            row_coeffs[f, r + STEPS - 1, :, :] = coeff_rows[f][r] + (1.0 - 4.0 * diffusion) * (1 - f)

    for g in range(fields // height):
        at = chunk(g, height)
        fast, slow = extended_rows(own_rows(tangents, g, height), near, far, far_late, at)
        for step in range(1, STEPS + 1):
            margin = STEPS - step
            new_fast = {}
            for r in range(-margin, SUB + margin):
                around = fast[r - 1] + fast[r + 1] + roll(fast[r], 1) + roll(fast[r], -1)
                gain, cross = (tall(row_coeffs[f, r + STEPS - 1], height) for f in range(2))
                new_fast[r] = advance(fast[r], slow[r], around, gain, cross)
            keep = max(margin - 1, 0)
            slow = {r: relax(fast[r], slow[r]) for r in range(-keep, SUB + keep)}
            fast = new_fast
        lane = lane_index(fast[0])
        middle = (lane >= STEPS) & (lane < LANES - STEPS)
        for f, rows in enumerate((fast, slow)):
            for r in range(SUB):
                cells[at, (f * SUB + r) * LANES:(f * SUB + r + 1) * LANES] = jnp.where(middle, rows[r], 0.0)

    middle_gram[...] = gram_of(cells[...])


def local_call(body, name, out_shapes, scratch, *args, hbm=False, vmem=VMEM_BYTES, cost=None):
    spec = pl.BlockSpec(memory_space=pltpu.VMEM)
    return pl.pallas_call(
        body,
        out_shape=[jax.ShapeDtypeStruct(s, jnp.float32) for s in out_shapes],
        in_specs=[pl.BlockSpec(memory_space=pltpu.HBM) if hbm else spec] * len(args),
        out_specs=[spec] * len(out_shapes),
        scratch_shapes=[pltpu.VMEM(s, jnp.float32) if isinstance(s, tuple) else s for s in scratch],
        compiler_params=pltpu.CompilerParams(vmem_limit_bytes=vmem),
        name=name,
        cost_estimate=cost,
    )(*args)


def swap(cells, axis, first, close=False):
    count = lax.axis_size(axis)
    pairs = [(i, i + 1) for i in range(first, count - 1, 2)]
    if close and first:
        pairs.append((0, count - 1))
    return lax.ppermute(cells, axis, pairs + [(b, a) for a, b in pairs])


def exchange(cells, grp_bit, tile_bit):
    grps, tiles = lax.axis_size("grp"), lax.axis_size("tile")
    moves = [(g * tiles + t, (g ^ grp_bit) * tiles + (t ^ tile_bit)) for g in range(grps) for t in range(tiles)]
    return lax.ppermute(cells, ("grp", "tile"), moves)


def parity():
    bits = lax.axis_index("grp") ^ lax.axis_index("tile")
    shift = 1
    while shift < max(lax.axis_size("grp"), lax.axis_size("tile")):
        bits = bits ^ (bits >> shift)
        shift *= 2
    return (bits & 1) == 1


def sum_blocks(packed, beside):
    half = packed.shape[0] // 2
    high_half = parity()
    low, high = packed[:half], packed[half:]
    part = jnp.where(high_half, high, low) + exchange(jnp.where(high_half, low, high), 0, 1)
    for axis in ("grp", "tile"):
        bit = 1 if axis == "grp" else 2
        while bit < lax.axis_size(axis):
            if axis == "tile" and 2 * bit >= lax.axis_size(axis):
                part, beside = lax.optimization_barrier((part, beside))
            part = part + (exchange(part, bit, 1) if axis == "grp" else exchange(part, 0, bit + 1))
            bit *= 2
    return part, exchange(part, 0, 1), beside


def per_device(tangents, reaction_self, reaction_cross):
    fields = tangents.shape[1]
    padded = fields + SUB
    rows = tangents.reshape(2, fields * tangents.shape[2], tangents.shape[3])
    strip = (padded, LANES)
    early, late = (1 + EARLY_ROWS,) + strip, (2 * STEPS - 1 - EARLY_ROWS,) + strip
    inputs = (rows, jnp.stack([reaction_self, reaction_cross]))
    last, first, near, far, far_late = local_call(
        functools.partial(edge_kernel, fields, HEIGHT_EDGE), "edges", [strip] * 2 + [(2 * STEPS, padded, LANES), early, late],
        [a.shape for a in inputs] + [pltpu.SemaphoreType.DMA((fields // HEIGHT_EDGE + 1,))], *inputs,
        hbm=True, vmem=EDGE_VMEM_BYTES,
    )
    near, far, far_late = swap(near, "tile", 0), swap(far, "tile", 1), swap(far_late, "tile", 1)
    (row_mirror,) = local_call(row_mirror_kernel, "row_mirror", [(2,) + strip], [], last, first)
    strips, near_cols, far_cols = local_call(
        column_kernel, "columns", [(4,) + strip, strip, strip], [], last, first, row_mirror, near, far
    )
    (column_mirror,) = local_call(column_mirror_kernel, "column_mirror", [(2,) + strip], [], strips)
    far_cols = swap(far_cols, "grp", 1, close=True)
    near_cols = swap(near_cols, "grp", 0)
    (middle_gram,) = local_call(
        functools.partial(evolve_kernel, fields, HEIGHT_EVOLVE), "evolve", [(fields, fields)],
        [(2, SUB + 2 * STEPS - 2, SUB, LANES), (fields, 2 * SUB * LANES)], *inputs, near, far, far_late,
    )
    side_blocks = fields // SIDE
    packed, gram = local_call(
        functools.partial(gram_kernel, fields, HEIGHT_STRIP), "gram", [(packed_rows(side_blocks), 2 * SIDE), (fields, fields)],
        [(2,) + strip, (fields, LANES)], middle_gram, strips, column_mirror, near_cols, far_cols,
    )
    block_total = lax.axis_size("grp") * lax.axis_size("tile")
    corrections, growth = factor_call(*sum_blocks(packed, local_factor(gram, side_blocks)), fields, math.sqrt(block_total))
    return (corrections, growth)


def solution(mesh):
    in_specs = (P(None, None, "tile", "grp"), P("tile", "grp"), P("tile", "grp"))
    out_specs = (P(("grp", "tile"), None), P())
    return jax.shard_map(
        per_device, mesh=mesh, in_specs=in_specs, out_specs=out_specs, check_vma=False
    )
```

```python
import functools
import math

import jax
import jax.numpy as jnp
from jax import lax
from jax.experimental import pallas as pl
from jax.experimental.pallas import tpu as pltpu
from jax.sharding import PartitionSpec as P


STEPS = 4
diffusion = 0.2
slow_rate = 0.05
HEIGHT_EDGE = 96
HEIGHT_STRIP = 8
HEIGHT_EVOLVE = 24
SIDE = 64
VMEM_BYTES = 24 * 1024 * 1024
EARLY_ROWS = 3
LOCAL_COST = pl.CostEstimate(flops=10**9, bytes_accessed=10**6, transcendentals=0)
EDGE_VMEM_BYTES = 52 * 1024 * 1024
LANES = 128
SUB = 8
HI = lax.Precision.HIGHEST

def dot_nn(a, b):
    return lax.dot_general(a, b, (((1,), (0,)), ((), ())), precision=HI, preferred_element_type=jnp.float32)
def dot_tn(a, b):
    return lax.dot_general(a, b, (((0,), (0,)), ((), ())), precision=HI, preferred_element_type=jnp.float32)
def dot_nt(a, b):
    return lax.dot_general(a, b, (((1,), (1,)), ((), ())), precision=HI, preferred_element_type=jnp.float32)

def gram_of(cells):
    high = cells.astype(jnp.bfloat16)
    left = cells - high.astype(jnp.float32)
    middle = left.astype(jnp.bfloat16)
    low = (left - middle.astype(jnp.float32)).astype(jnp.bfloat16)

    def product(a, b):
        return lax.dot_general(a, b, (((1,), (1,)), ((), ())), preferred_element_type=jnp.float32)

    mixed = product(middle, high) + product(low, high)
    return product(high, high) + product(middle, middle) + (mixed + mixed.T)


def block_pairs(n):
    return [(i, j) for i in range(n) for j in range(i, n)]

def square_masks():
    row = lax.broadcasted_iota(jnp.int32, (SIDE, SIDE), 0)
    col = lax.broadcasted_iota(jnp.int32, (SIDE, SIDE), 1)
    return row, col


def packed_rows(n):
    count = n // 2 + n * (n - 1) // 2 + 1
    return count * SIDE // 2


def pack_blocks(whole, n):
    row, col = square_masks()

    def block(i, j):
        return whole[i*SIDE:(i+1)*SIDE, j*SIDE:(j+1)*SIDE]

    squares, below = [], jnp.zeros((SIDE, SIDE), jnp.float32)
    for m in range(n // 2):
        second = block(2*m + 1, 2*m + 1)
        line = jnp.sum(jnp.where(row == col, second, 0.0), axis=0, keepdims=True)
        at = SIDE - 1 - 2*m
        turned = jnp.concatenate([line[:, at:], line[:, :at]], axis=1)
        below = jnp.where(row == at, line, jnp.where(row == at - 1, turned, below))
        squares.append(jnp.where(row <= col, block(2*m, 2*m), second))
    squares += [block(i, j) for i, j in block_pairs(n) if i < j]
    squares.append(jnp.where(row <= col, block(n - 1, n - 1), below) if n % 2 else below)
    lines = [jnp.concatenate(squares[i:i+2], axis=1) for i in range(0, len(squares) - 1, 2)]
    if len(squares) % 2:
        lines.append(jnp.concatenate([squares[-1][:SIDE // 2], squares[-1][SIDE // 2:]], axis=1))
    return jnp.concatenate(lines, axis=0)


def unpack_blocks(packed, n):
    row, col = square_masks()
    count = packed.shape[0] * 2 // SIDE
    squares = []
    for i in range(count // 2):
        squares += [packed[i*SIDE:(i+1)*SIDE, :SIDE], packed[i*SIDE:(i+1)*SIDE, SIDE:]]
    if count % 2:
        rest = packed[count // 2 * SIDE:]
        squares.append(jnp.concatenate([rest[:, :SIDE], rest[:, SIDE:]], axis=0))
    last = squares[-1]
    blocks = dict(zip([(i, j) for i, j in block_pairs(n) if i < j], squares[n // 2:-1]))
    for m in range(n // 2):
        both, other = squares[m], squares[m].T
        at = SIDE - 1 - 2*m
        line, turned = last[at:at + 1], last[at - 1:at]
        turned = jnp.concatenate([turned[:, SIDE - at:], turned[:, :SIDE - at]], axis=1)
        line = jnp.where(col[:1] < at, line, turned)
        blocks[2*m, 2*m] = jnp.where(row <= col, both, other)
        blocks[2*m + 1, 2*m + 1] = jnp.where(row > col, both, jnp.where(row < col, other, line))
    if n % 2:
        blocks[n - 1, n - 1] = jnp.where(row <= col, last, last.T)
    return blocks


def spread_lane(x, lane):
    return jnp.broadcast_to(x[:, lane:lane+1], (x.shape[0], LANES))
def spread_row(x, row):
    return jnp.broadcast_to(x[row:row+1, :], (SUB, x.shape[1]))

def factor_blocks(blocks):
    groups = SIDE // SUB
    eye = (lax.broadcasted_iota(jnp.int32, (SIDE, SIDE), 0) == lax.broadcasted_iota(jnp.int32, (SIDE, SIDE), 1)).astype(jnp.float32)
    sub = lax.broadcasted_iota(jnp.int32, (SUB, LANES), 0)
    states = []
    for d in blocks:
        whole = jnp.concatenate([d, eye], axis=1)
        states.append([whole[g*SUB:(g+1)*SUB] for g in range(groups)])
    done = [[] for _ in blocks]
    ready = [None for _ in blocks]
    for p in range(groups):
        for s, v in enumerate(states):
            spread = {(g, c): spread_lane(v[g], p*SUB + c) for g in range(p + 1, groups) for c in range(SUB)}
            if p + 1 < groups:
                coming = [spread_lane(v[p + 1], (p + 1)*SUB + c) for c in range(SUB)]
            columns = ready[s] or [spread_lane(v[p], p*SUB + c) for c in range(SUB)]
            rows = [spread_row(v[p], c) for c in range(SUB)]
            pivots = {(a, c): spread_row(columns[c], a) for c in range(SUB) for a in range(c, SUB)}
            mult, inverses, scale = {}, [], []
            for c in range(SUB):
                inverses.append(1.0 / pivots[c, c])
                scale.append(lax.rsqrt(pivots[c, c]))
                for a in range(c + 1, SUB):
                    mult[a, c] = pivots[a, c] * inverses[c]
                    rows[a] = rows[a] - mult[a, c] * rows[c]
                    for b in range(c + 1, a + 1):
                        pivots[a, b] = pivots[a, b] - mult[a, c] * pivots[b, c]
            scaled = [rows[c] * scale[c] for c in range(SUB)]
            panel = scaled[0]
            for c in range(1, SUB):
                panel = jnp.where(sub == c, scaled[c], panel)
            done[s].append(panel)
            for g in range(p + 1, min(p + 3, groups)):
                cols = [spread[g, c] for c in range(SUB)]
                for c in range(SUB):
                    for a in range(c + 1, SUB):
                        cols[a] = cols[a] - mult[a, c] * cols[c]
                    if g == p + 1:
                        part = cols[c] * inverses[c]
                        coming = [x - part * spread_row(cols[c], b) for b, x in enumerate(coming)]
                    v[g] = v[g] - (cols[c] * scale[c]) * scaled[c]
                if g == p + 1:
                    ready[s] = coming
            if p + 3 < groups:
                solved = [scaled[c] * scale[c] for c in range(SUB)]
                for c in reversed(range(SUB)):
                    for a in range(c):
                        solved[a] = solved[a] - mult[c, a] * solved[c]
                for g in range(p + 3, groups):
                    for c in range(SUB):
                        v[g] = v[g] - spread[g, c] * solved[c]
    out = []
    for panels in done:
        whole = jnp.concatenate(panels, axis=0)
        out.append((whole[:, :SIDE], whole[:, SIDE:]))
    return out

def local_kernel(n, gram, panel, *after):
    blocks = {(i, j): gram[i*SIDE:(i+1)*SIDE, j*SIDE:(j+1)*SIDE] for i, j in block_pairs(n)}
    row, col = square_masks()
    ((factor, inverse),) = factor_blocks([blocks[0, 0]])
    panel[:, :SIDE] = jnp.where(row <= col, factor, 0.0)
    if n > 1:
        row = dot_nn(inverse, jnp.concatenate([blocks[0, j] for j in range(1, n)], axis=1))
        panel[:, SIDE:] = row
        less = dot_tn(row, row)
        for i, j in block_pairs(n - 1):
            at = (slice(i*SIDE, (i+1)*SIDE), slice(j*SIDE, (j+1)*SIDE))
            after[0][at] = blocks[i + 1, j + 1] - less[at]


def local_factor(gram, n):
    panels, left = [], gram
    for k in range(n):
        m = n - k
        shapes = [(SIDE, m*SIDE)] + ([((m-1)*SIDE, (m-1)*SIDE)] if m > 1 else [])
        panel, *left = local_call(functools.partial(local_kernel, m), "local_factor", shapes, [], left, cost=LOCAL_COST)
        left = left[0] if left else None
        panels.append(panel)
    return panels


def factor_kernel(n, weight, own_ref, other_ref, *refs):
    local, (out_ref, growth_ref) = refs[:n], refs[n:]
    high_half = parity()
    own, other = own_ref[...], other_ref[...]
    total = unpack_blocks(jnp.concatenate([jnp.where(high_half, other, own), jnp.where(high_half, own, other)], axis=0), n)
    row, col = square_masks()
    diag = row == col
    rest = {j: [local[i][:, (j-i)*SIDE:(j-i+1)*SIDE] for i in range(j + 1)] for j in range(n)}
    for k in range(n):
        ((factor, inverse),) = factor_blocks([total[k, k]])
        growth_ref[0, k*SIDE:(k+1)*SIDE] = jnp.log(jnp.sum(jnp.where(diag, factor, 0.0), axis=0))
        if k + 1 < n:
            row = dot_nn(inverse, jnp.concatenate([total[k, j] for j in range(k + 1, n)], axis=1))
            for i in range(k + 1, n):
                less = dot_tn(row[:, (i-k-1)*SIDE:(i-k)*SIDE], row[:, (i-k-1)*SIDE:])
                for j in range(i, n):
                    total[i, j] = total[i, j] - less[:, (j-i)*SIDE:(j-i+1)*SIDE]
        answer = dot_nt(jnp.concatenate(rest[k], axis=0), inverse)
        out_ref[:(k+1)*SIDE, k*SIDE:(k+1)*SIDE] = weight * answer
        if k + 1 < n:
            out_ref[(k+1)*SIDE:, k*SIDE:(k+1)*SIDE] = jnp.zeros(((n-k-1)*SIDE, SIDE), jnp.float32)
            less = dot_nn(answer, row)
            for j in range(k + 1, n):
                at = (j-k-1)*SIDE
                rest[j] = [
                    part - less[i*SIDE:(i+1)*SIDE, at:at+SIDE] if i <= k else part for i, part in enumerate(rest[j])
                ]


def factor_call(own, other, local, k, weight):
    out, growth = local_call(
        functools.partial(factor_kernel, k // SIDE, weight), "factor", [(k, k), (1, k)], [], own, other, *local
    )
    return out, growth[0]


def pick(flag, first, second):
    return jnp.where(flag, first, second)


def roll(x, shift):
    return pltpu.roll(x, shift % LANES, 1)


def lane_index(like):
    return lax.broadcasted_iota(jnp.int32, like.shape, like.ndim - 1)


def chunk(g, height):
    return pl.ds(pl.multiple_of(g * height, height), height)


def own_rows(tangents, g, height):
    return [[tangents[f, pl.ds(g * height * SUB + r, height, stride=SUB), :] for r in range(SUB)] for f in range(2)]


def own_coeffs(coeffs):
    return [[spread_row(coeffs[f], r) for r in range(SUB)] for f in range(2)]


def tall(x, height):
    return jnp.concatenate([x] * (height // SUB), axis=0)


def edge_kernel(fields, height, tangents_hbm, coeffs_hbm, last_out, first_out, near, far, far_late, tangents, coeffs, sems):
    chunks = fields // height
    span = height * SUB
    loads = [
        pltpu.make_async_copy(tangents_hbm.at[:, pl.ds(g * span, span), :], tangents.at[:, pl.ds(g * span, span), :], sems.at[g])
        for g in range(chunks)
    ]
    small = pltpu.make_async_copy(coeffs_hbm, coeffs, sems.at[chunks])
    for load in loads + [small]:
        load.start()
    odd = lax.axis_index("tile") % 2 == 1

    def send(at, rows):
        cell = lane_index(rows[0][0]) // SUB
        cells = LANES // SUB
        last, first = None, None
        for f in range(2):
            for r in range(SUB):
                s = f * SUB + r
                turned = roll(rows[f][r], (s + 1) * SUB)
                last = turned if last is None else jnp.where(cell == s, turned, last)
                first = turned if first is None else jnp.where(cell == (s + 1) % cells, turned, first)
        first = roll(first, -SUB)
        last_out[at, :] = last
        first_out[at, :] = first
        half = cell % SUB < STEPS
        to_above = jnp.where(half, last, roll(first, STEPS * SUB))
        to_below = jnp.where(half, roll(last, -STEPS * SUB), first)
        near[0, at, :] = pick(odd, to_above, to_below)
        far[0, at, :] = pick(odd, to_below, to_above)
        for f in range(2):
            count = STEPS - f
            for j in range(count):
                top, bottom = rows[f][j], rows[f][SUB - count + j]
                row = f * STEPS + j
                near[1 + row, at, :] = pick(odd, top, bottom)
                if row < EARLY_ROWS:
                    far[1 + row, at, :] = pick(odd, bottom, top)
                else:
                    far_late[row - EARLY_ROWS, at, :] = pick(odd, bottom, top)

    for g, load in enumerate(loads):
        load.wait()
        send(pl.ds(g * height, height), own_rows(tangents, g, height))
    small.wait()
    send(pl.ds(fields, SUB), own_coeffs(coeffs))


def row_mirror_kernel(last, first, mirrored):
    tile, tiles = lax.axis_index("tile"), lax.axis_size("tile")

    @pl.when((tile == 0) | (tile == tiles - 1))
    def _():
        for i, ref in enumerate((last, first)):
            own = ref[...]
            cell = lane_index(own) // SUB % SUB
            turned = roll(own, -7 * SUB)
            for s in range(1, SUB):
                turned = jnp.where(cell == s, roll(own, (2 * s - 7) * SUB), turned)
            mirrored[i] = turned

    @pl.when((tile != 0) & (tile != tiles - 1))
    def _():
        mirrored[...] = jnp.zeros(mirrored.shape, jnp.float32)


def column_kernel(last, first, mirrored, near, far, strips, near_out, far_out):
    tile, tiles = lax.axis_index("tile"), lax.axis_size("tile")
    odd, at_top, at_bottom = tile % 2 == 1, tile == 0, tile == tiles - 1
    grp_odd = lax.axis_index("grp") % 2 == 1
    one, two = near[0], far[0]
    lane = lane_index(one)
    cell, low, inner = lane // SUB % SUB, lane < LANES // 2, lane % SUB < STEPS
    half = cell < STEPS
    above, below = pick(odd, one, two), pick(odd, two, one)
    outside = (half & at_bottom) | (~half & at_top)
    received = (jnp.where(half, below, roll(above, STEPS * SUB)), jnp.where(half, roll(below, -STEPS * SUB), above))
    sides = []
    for i, ref in enumerate((last, first)):
        own, more = ref[...], jnp.where(outside, mirrored[i], received[i])
        fast = jnp.where(low, own, roll(more, LANES // 2))
        slow = jnp.where(low, roll(own, LANES // 2), more)
        strips[2 * i] = fast
        strips[2 * i + 1] = slow
        sides.append((fast, slow))
    to_left = jnp.where(inner, sides[1][0], roll(sides[1][1], STEPS))
    to_right = jnp.where(inner, roll(sides[0][0], -STEPS), sides[0][1])
    near_out[...] = pick(grp_odd, to_left, to_right)
    far_out[...] = pick(grp_odd, to_right, to_left)


def strip_neighbours(last, first, halo, wanted):
    c = lane_index(last) % SUB
    end, begin = c == SUB - 1, c == 0
    out = []
    sides = (lambda: (last, roll(halo, 7), None), lambda: (first, None, roll(halo, -7)), lambda: (halo, roll(first, 7), roll(last, -7)))
    for side in sides[:wanted]:
        x, after, before = side()
        right, left = roll(x, -1), roll(x, 1)
        if after is not None:
            right = jnp.where(end, after, right)
        if before is not None:
            left = jnp.where(begin, before, left)
        out.append(roll(x, SUB) + roll(x, -SUB) + right + left)
    return out


def advance(fast, slow, around, gain, cross):
    return gain * fast + diffusion * around + cross * slow


def relax(fast, slow):
    return (1.0 - slow_rate) * slow + slow_rate * fast


def column_mirror_kernel(strips, mirrored):
    grp, grps = lax.axis_index("grp"), lax.axis_size("grp")

    @pl.when((grp == 0) | (grp == grps - 1))
    def _():
        for f in range(2):
            tail, start = strips[f], strips[2 + f]
            c = lane_index(tail) % SUB
            turned = roll(tail, -7)
            for s in range(STEPS):
                turned = jnp.where(c == s, roll(tail, 2 * s - 7), turned)
                turned = jnp.where(c == 7 - s, roll(start, 7 - 2 * s), turned)
            mirrored[f] = turned

    @pl.when((grp != 0) & (grp != grps - 1))
    def _():
        mirrored[...] = jnp.zeros(mirrored.shape, jnp.float32)


def gram_kernel(fields, height, middle_gram, strips, mirrored, near, far, packed, gram, halo, ends):
    grp, grps = lax.axis_index("grp"), lax.axis_size("grp")
    grp_odd = grp % 2 == 1
    one, two = near[...], far[...]
    lane = lane_index(one)
    c = lane % SUB
    inner = c < STEPS
    left, right = pick(grp_odd, one, two), pick(grp_odd, two, one)
    outside = (inner & (grp == grps - 1)) | (~inner & (grp == 0))
    halo[0] = jnp.where(outside, mirrored[0], jnp.where(inner, right, roll(left, STEPS)))
    halo[1] = jnp.where(outside, mirrored[1], jnp.where(inner, roll(right, -STEPS), left))

    def parts(f, at):
        return [strips[f, at, :], strips[2 + f, at, :], halo[f, at, :]]

    gains = [tall(x + (1.0 - 4.0 * diffusion), height) for x in parts(0, pl.ds(fields, SUB))]
    crosses = [tall(x, height) for x in parts(1, pl.ds(fields, SUB))]
    places = [pl.ds(at, height) for at in range(0, fields, height)]
    held = [(parts(0, at), parts(1, at)) for at in places]
    for step in range(STEPS):
        wanted = 3 if step + 1 < STEPS else 2
        for i, (fast, slow) in enumerate(held):
            around = strip_neighbours(*fast, wanted)
            moved = [advance(fast[p], slow[p], around[p], gains[p], crosses[p]) for p in range(wanted)]
            held[i] = (moved, [relax(fast[p], slow[p]) for p in range(wanted)])
    for at, pair in zip(places, held):
        l = lane_index(pair[0][0])
        joined = [jnp.where(l % SUB < STEPS, side[1], side[0]) for side in pair]
        ends[at, :] = jnp.where(l < LANES // 2, joined[0], roll(joined[1], LANES // 2))

    whole = middle_gram[...] + dot_nt(ends[...], ends[...])
    gram[...] = whole
    packed[...] = pack_blocks(whole, fields // SIDE)


def extended_rows(own, near, far, far_late, at):
    tile, tiles = lax.axis_index("tile"), lax.axis_size("tile")
    odd, at_top, at_bottom = tile % 2 == 1, tile == 0, tile == tiles - 1
    out = []
    for f in range(2):
        count = STEPS - f
        rows = dict(enumerate(own[f]))
        for j in range(count):
            row = f * STEPS + j
            one = near[1 + row, at, :]
            two = far[1 + row, at, :] if row < EARLY_ROWS else far_late[row - EARLY_ROWS, at, :]
            rows[j - count] = pick(at_top, own[f][count - 1 - j], pick(odd, one, two))
            rows[SUB + j] = pick(at_bottom, own[f][SUB - 1 - j], pick(odd, two, one))
        out.append(rows)
    return out


def evolve_kernel(fields, height, tangents, coeffs, near, far, far_late, middle_gram, row_coeffs, cells):
    coeff_rows = extended_rows(own_coeffs(coeffs), near, far, far_late, pl.ds(fields, SUB))
    for f in range(2):
        for r in range(1 - STEPS, SUB + STEPS - 1):
            row_coeffs[f, r + STEPS - 1, :, :] = coeff_rows[f][r] + (1.0 - 4.0 * diffusion) * (1 - f)

    for g in range(fields // height):
        at = chunk(g, height)
        fast, slow = extended_rows(own_rows(tangents, g, height), near, far, far_late, at)
        for step in range(1, STEPS + 1):
            margin = STEPS - step
            new_fast = {}
            for r in range(-margin, SUB + margin):
                around = fast[r - 1] + fast[r + 1] + roll(fast[r], 1) + roll(fast[r], -1)
                gain, cross = (tall(row_coeffs[f, r + STEPS - 1], height) for f in range(2))
                new_fast[r] = advance(fast[r], slow[r], around, gain, cross)
            keep = max(margin - 1, 0)
            slow = {r: relax(fast[r], slow[r]) for r in range(-keep, SUB + keep)}
            fast = new_fast
        lane = lane_index(fast[0])
        middle = (lane >= STEPS) & (lane < LANES - STEPS)
        for f, rows in enumerate((fast, slow)):
            for r in range(SUB):
                cells[at, (f * SUB + r) * LANES:(f * SUB + r + 1) * LANES] = jnp.where(middle, rows[r], 0.0)

    middle_gram[...] = gram_of(cells[...])


def local_call(body, name, out_shapes, scratch, *args, hbm=False, vmem=VMEM_BYTES, cost=None):
    spec = pl.BlockSpec(memory_space=pltpu.VMEM)
    return pl.pallas_call(
        body,
        out_shape=[jax.ShapeDtypeStruct(s, jnp.float32) for s in out_shapes],
        in_specs=[pl.BlockSpec(memory_space=pltpu.HBM) if hbm else spec] * len(args),
        out_specs=[spec] * len(out_shapes),
        scratch_shapes=[pltpu.VMEM(s, jnp.float32) if isinstance(s, tuple) else s for s in scratch],
        compiler_params=pltpu.CompilerParams(vmem_limit_bytes=vmem),
        name=name,
        cost_estimate=cost,
    )(*args)


def swap(cells, axis, first, close=False):
    count = lax.axis_size(axis)
    pairs = [(i, i + 1) for i in range(first, count - 1, 2)]
    if close and first:
        pairs.append((0, count - 1))
    return lax.ppermute(cells, axis, pairs + [(b, a) for a, b in pairs])


def exchange(cells, grp_bit, tile_bit):
    grps, tiles = lax.axis_size("grp"), lax.axis_size("tile")
    moves = [(g * tiles + t, (g ^ grp_bit) * tiles + (t ^ tile_bit)) for g in range(grps) for t in range(tiles)]
    return lax.ppermute(cells, ("grp", "tile"), moves)


def parity():
    bits = lax.axis_index("grp") ^ lax.axis_index("tile")
    shift = 1
    while shift < max(lax.axis_size("grp"), lax.axis_size("tile")):
        bits = bits ^ (bits >> shift)
        shift *= 2
    return (bits & 1) == 1


def sum_blocks(packed, beside):
    half = packed.shape[0] // 2
    high_half = parity()
    low, high = packed[:half], packed[half:]
    part = jnp.where(high_half, high, low) + exchange(jnp.where(high_half, low, high), 0, 1)
    for axis in ("grp", "tile"):
        bit = 1 if axis == "grp" else 2
        while bit < lax.axis_size(axis):
            if axis == "tile" and 2 * bit >= lax.axis_size(axis):
                part, beside = lax.optimization_barrier((part, beside))
            part = part + (exchange(part, bit, 1) if axis == "grp" else exchange(part, 0, bit + 1))
            bit *= 2
    return part, exchange(part, 0, 1), beside


def per_device(tangents, reaction_self, reaction_cross):
    fields = tangents.shape[1]
    padded = fields + SUB
    rows = tangents.reshape(2, fields * tangents.shape[2], tangents.shape[3])
    strip = (padded, LANES)
    early, late = (1 + EARLY_ROWS,) + strip, (2 * STEPS - 1 - EARLY_ROWS,) + strip
    inputs = (rows, jnp.stack([reaction_self, reaction_cross]))
    last, first, near, far, far_late = local_call(
        functools.partial(edge_kernel, fields, HEIGHT_EDGE), "edges", [strip] * 2 + [(2 * STEPS, padded, LANES), early, late],
        [a.shape for a in inputs] + [pltpu.SemaphoreType.DMA((fields // HEIGHT_EDGE + 1,))], *inputs,
        hbm=True, vmem=EDGE_VMEM_BYTES,
    )
    near, far, far_late = swap(near, "tile", 0), swap(far, "tile", 1), swap(far_late, "tile", 1)
    (row_mirror,) = local_call(row_mirror_kernel, "row_mirror", [(2,) + strip], [], last, first)
    strips, near_cols, far_cols = local_call(
        column_kernel, "columns", [(4,) + strip, strip, strip], [], last, first, row_mirror, near, far
    )
    (column_mirror,) = local_call(column_mirror_kernel, "column_mirror", [(2,) + strip], [], strips)
    far_cols = swap(far_cols, "grp", 1, close=True)
    near_cols = swap(near_cols, "grp", 0)
    (middle_gram,) = local_call(
        functools.partial(evolve_kernel, fields, HEIGHT_EVOLVE), "evolve", [(fields, fields)],
        [(2, SUB + 2 * STEPS - 2, SUB, LANES), (fields, 2 * SUB * LANES)], *inputs, near, far, far_late,
    )
    side_blocks = fields // SIDE
    packed, gram = local_call(
        functools.partial(gram_kernel, fields, HEIGHT_STRIP), "gram", [(packed_rows(side_blocks), 2 * SIDE), (fields, fields)],
        [(2,) + strip, (fields, LANES)], middle_gram, strips, column_mirror, near_cols, far_cols,
    )
    block_total = lax.axis_size("grp") * lax.axis_size("tile")
    corrections, growth = factor_call(*sum_blocks(packed, local_factor(gram, side_blocks)), fields, math.sqrt(block_total))
    return (corrections, growth)


def solution(mesh):
    in_specs = (P(None, None, "tile", "grp"), P("tile", "grp"), P("tile", "grp"))
    out_specs = (P(("grp", "tile"), None), P())
    return jax.shard_map(
        per_device, mesh=mesh, in_specs=in_specs, out_specs=out_specs, check_vma=False
    )
```

```python
import functools
import math

import jax
import jax.numpy as jnp
from jax import lax
from jax.experimental import pallas as pl
from jax.experimental.pallas import tpu as pltpu
from jax.sharding import PartitionSpec as P


STEPS = 4
diffusion = 0.2
slow_rate = 0.05
HEIGHT_EDGE = 96
HEIGHT_STRIP = 8
HEIGHT_EVOLVE = 24
SIDE = 64
VMEM_BYTES = 24 * 1024 * 1024
EARLY_ROWS = 3
LOCAL_COST = pl.CostEstimate(flops=10**9, bytes_accessed=10**6, transcendentals=0)
EDGE_VMEM_BYTES = 52 * 1024 * 1024
LANES = 128
SUB = 8
HI = lax.Precision.HIGHEST

def dot_nn(a, b):
    return lax.dot_general(a, b, (((1,), (0,)), ((), ())), precision=HI, preferred_element_type=jnp.float32)
def dot_tn(a, b):
    return lax.dot_general(a, b, (((0,), (0,)), ((), ())), precision=HI, preferred_element_type=jnp.float32)
def dot_nt(a, b):
    return lax.dot_general(a, b, (((1,), (1,)), ((), ())), precision=HI, preferred_element_type=jnp.float32)

def gram_of(cells):
    high = cells.astype(jnp.bfloat16)
    left = cells - high.astype(jnp.float32)
    middle = left.astype(jnp.bfloat16)
    low = (left - middle.astype(jnp.float32)).astype(jnp.bfloat16)

    def product(a, b):
        return lax.dot_general(a, b, (((1,), (1,)), ((), ())), preferred_element_type=jnp.float32)

    mixed = product(middle, high) + product(low, high)
    return product(high, high) + product(middle, middle) + (mixed + mixed.T)


def block_pairs(n):
    return [(i, j) for i in range(n) for j in range(i, n)]

def square_masks():
    row = lax.broadcasted_iota(jnp.int32, (SIDE, SIDE), 0)
    col = lax.broadcasted_iota(jnp.int32, (SIDE, SIDE), 1)
    return row, col


def packed_rows(n):
    count = n // 2 + n * (n - 1) // 2 + 1
    return count * SIDE // 2


def pack_blocks(whole, n):
    row, col = square_masks()

    def block(i, j):
        return whole[i*SIDE:(i+1)*SIDE, j*SIDE:(j+1)*SIDE]

    squares, below = [], jnp.zeros((SIDE, SIDE), jnp.float32)
    for m in range(n // 2):
        second = block(2*m + 1, 2*m + 1)
        line = jnp.sum(jnp.where(row == col, second, 0.0), axis=0, keepdims=True)
        at = SIDE - 1 - 2*m
        turned = jnp.concatenate([line[:, at:], line[:, :at]], axis=1)
        below = jnp.where(row == at, line, jnp.where(row == at - 1, turned, below))
        squares.append(jnp.where(row <= col, block(2*m, 2*m), second))
    squares += [block(i, j) for i, j in block_pairs(n) if i < j]
    squares.append(jnp.where(row <= col, block(n - 1, n - 1), below) if n % 2 else below)
    lines = [jnp.concatenate(squares[i:i+2], axis=1) for i in range(0, len(squares) - 1, 2)]
    if len(squares) % 2:
        lines.append(jnp.concatenate([squares[-1][:SIDE // 2], squares[-1][SIDE // 2:]], axis=1))
    return jnp.concatenate(lines, axis=0)


def unpack_blocks(packed, n):
    row, col = square_masks()
    count = packed.shape[0] * 2 // SIDE
    squares = []
    for i in range(count // 2):
        squares += [packed[i*SIDE:(i+1)*SIDE, :SIDE], packed[i*SIDE:(i+1)*SIDE, SIDE:]]
    if count % 2:
        rest = packed[count // 2 * SIDE:]
        squares.append(jnp.concatenate([rest[:, :SIDE], rest[:, SIDE:]], axis=0))
    last = squares[-1]
    blocks = dict(zip([(i, j) for i, j in block_pairs(n) if i < j], squares[n // 2:-1]))
    for m in range(n // 2):
        both, other = squares[m], squares[m].T
        at = SIDE - 1 - 2*m
        line, turned = last[at:at + 1], last[at - 1:at]
        turned = jnp.concatenate([turned[:, SIDE - at:], turned[:, :SIDE - at]], axis=1)
        line = jnp.where(col[:1] < at, line, turned)
        blocks[2*m, 2*m] = jnp.where(row <= col, both, other)
        blocks[2*m + 1, 2*m + 1] = jnp.where(row > col, both, jnp.where(row < col, other, line))
    if n % 2:
        blocks[n - 1, n - 1] = jnp.where(row <= col, last, last.T)
    return blocks


def spread_lane(x, lane):
    return jnp.broadcast_to(x[:, lane:lane+1], (x.shape[0], LANES))
def spread_row(x, row):
    return jnp.broadcast_to(x[row:row+1, :], (SUB, x.shape[1]))

def factor_blocks(blocks):
    groups = SIDE // SUB
    eye = (lax.broadcasted_iota(jnp.int32, (SIDE, SIDE), 0) == lax.broadcasted_iota(jnp.int32, (SIDE, SIDE), 1)).astype(jnp.float32)
    sub = lax.broadcasted_iota(jnp.int32, (SUB, LANES), 0)
    states = []
    for d in blocks:
        whole = jnp.concatenate([d, eye], axis=1)
        states.append([whole[g*SUB:(g+1)*SUB] for g in range(groups)])
    done = [[] for _ in blocks]
    ready = [None for _ in blocks]
    for p in range(groups):
        for s, v in enumerate(states):
            spread = {(g, c): spread_lane(v[g], p*SUB + c) for g in range(p + 1, groups) for c in range(SUB)}
            if p + 1 < groups:
                coming = [spread_lane(v[p + 1], (p + 1)*SUB + c) for c in range(SUB)]
            columns = ready[s] or [spread_lane(v[p], p*SUB + c) for c in range(SUB)]
            rows = [spread_row(v[p], c) for c in range(SUB)]
            pivots = {(a, c): spread_row(columns[c], a) for c in range(SUB) for a in range(c, SUB)}
            mult, inverses, scale = {}, [], []
            for c in range(SUB):
                inverses.append(1.0 / pivots[c, c])
                scale.append(lax.rsqrt(pivots[c, c]))
                for a in range(c + 1, SUB):
                    mult[a, c] = pivots[a, c] * inverses[c]
                    rows[a] = rows[a] - mult[a, c] * rows[c]
                    for b in range(c + 1, a + 1):
                        pivots[a, b] = pivots[a, b] - mult[a, c] * pivots[b, c]
            scaled = [rows[c] * scale[c] for c in range(SUB)]
            panel = scaled[0]
            for c in range(1, SUB):
                panel = jnp.where(sub == c, scaled[c], panel)
            done[s].append(panel)
            for g in range(p + 1, min(p + 3, groups)):
                cols = [spread[g, c] for c in range(SUB)]
                for c in range(SUB):
                    for a in range(c + 1, SUB):
                        cols[a] = cols[a] - mult[a, c] * cols[c]
                    if g == p + 1:
                        part = cols[c] * inverses[c]
                        coming = [x - part * spread_row(cols[c], b) for b, x in enumerate(coming)]
                    v[g] = v[g] - (cols[c] * scale[c]) * scaled[c]
                if g == p + 1:
                    ready[s] = coming
            if p + 3 < groups:
                solved = [scaled[c] * scale[c] for c in range(SUB)]
                for c in reversed(range(SUB)):
                    for a in range(c):
                        solved[a] = solved[a] - mult[c, a] * solved[c]
                for g in range(p + 3, groups):
                    for c in range(SUB):
                        v[g] = v[g] - spread[g, c] * solved[c]
    out = []
    for panels in done:
        whole = jnp.concatenate(panels, axis=0)
        out.append((whole[:, :SIDE], whole[:, SIDE:]))
    return out

def local_kernel(n, gram, panel, *after):
    blocks = {(i, j): gram[i*SIDE:(i+1)*SIDE, j*SIDE:(j+1)*SIDE] for i, j in block_pairs(n)}
    row, col = square_masks()
    ((factor, inverse),) = factor_blocks([blocks[0, 0]])
    panel[:, :SIDE] = jnp.where(row <= col, factor, 0.0)
    if n > 1:
        row = dot_nn(inverse, jnp.concatenate([blocks[0, j] for j in range(1, n)], axis=1))
        panel[:, SIDE:] = row
        less = dot_tn(row, row)
        for i, j in block_pairs(n - 1):
            at = (slice(i*SIDE, (i+1)*SIDE), slice(j*SIDE, (j+1)*SIDE))
            after[0][at] = blocks[i + 1, j + 1] - less[at]


def local_factor(gram, n):
    panels, left = [], gram
    for k in range(n):
        m = n - k
        shapes = [(SIDE, m*SIDE)] + ([((m-1)*SIDE, (m-1)*SIDE)] if m > 1 else [])
        panel, *left = local_call(functools.partial(local_kernel, m), "local_factor", shapes, [], left, cost=LOCAL_COST)
        left = left[0] if left else None
        panels.append(panel)
    return panels


def factor_kernel(n, weight, own_ref, other_ref, *refs):
    local, (out_ref, growth_ref) = refs[:n], refs[n:]
    high_half = parity()
    own, other = own_ref[...], other_ref[...]
    total = unpack_blocks(jnp.concatenate([jnp.where(high_half, other, own), jnp.where(high_half, own, other)], axis=0), n)
    row, col = square_masks()
    diag = row == col
    rest = {j: [local[i][:, (j-i)*SIDE:(j-i+1)*SIDE] for i in range(j + 1)] for j in range(n)}
    for k in range(n):
        ((factor, inverse),) = factor_blocks([total[k, k]])
        growth_ref[0, k*SIDE:(k+1)*SIDE] = jnp.log(jnp.sum(jnp.where(diag, factor, 0.0), axis=0))
        if k + 1 < n:
            row = dot_nn(inverse, jnp.concatenate([total[k, j] for j in range(k + 1, n)], axis=1))
            for i in range(k + 1, n):
                less = dot_tn(row[:, (i-k-1)*SIDE:(i-k)*SIDE], row[:, (i-k-1)*SIDE:])
                for j in range(i, n):
                    total[i, j] = total[i, j] - less[:, (j-i)*SIDE:(j-i+1)*SIDE]
        answer = dot_nt(jnp.concatenate(rest[k], axis=0), inverse)
        out_ref[:(k+1)*SIDE, k*SIDE:(k+1)*SIDE] = weight * answer
        if k + 1 < n:
            out_ref[(k+1)*SIDE:, k*SIDE:(k+1)*SIDE] = jnp.zeros(((n-k-1)*SIDE, SIDE), jnp.float32)
            less = dot_nn(answer, row)
            for j in range(k + 1, n):
                at = (j-k-1)*SIDE
                rest[j] = [
                    part - less[i*SIDE:(i+1)*SIDE, at:at+SIDE] if i <= k else part for i, part in enumerate(rest[j])
                ]


def factor_call(own, other, local, k, weight):
    out, growth = local_call(
        functools.partial(factor_kernel, k // SIDE, weight), "factor", [(k, k), (1, k)], [], own, other, *local
    )
    return out, growth[0]


def pick(flag, first, second):
    return jnp.where(flag, first, second)


def roll(x, shift):
    return pltpu.roll(x, shift % LANES, 1)


def lane_index(like):
    return lax.broadcasted_iota(jnp.int32, like.shape, like.ndim - 1)


def chunk(g, height):
    return pl.ds(pl.multiple_of(g * height, height), height)


def own_rows(tangents, g, height):
    return [[tangents[f, pl.ds(g * height * SUB + r, height, stride=SUB), :] for r in range(SUB)] for f in range(2)]


def own_coeffs(coeffs):
    return [[spread_row(coeffs[f], r) for r in range(SUB)] for f in range(2)]


def tall(x, height):
    return jnp.concatenate([x] * (height // SUB), axis=0)


def edge_kernel(fields, height, tangents_hbm, coeffs_hbm, last_out, first_out, near, far, far_late, tangents, coeffs, sems):
    chunks = fields // height
    span = height * SUB
    loads = [
        pltpu.make_async_copy(tangents_hbm.at[:, pl.ds(g * span, span), :], tangents.at[:, pl.ds(g * span, span), :], sems.at[g])
        for g in range(chunks)
    ]
    small = pltpu.make_async_copy(coeffs_hbm, coeffs, sems.at[chunks])
    for load in loads + [small]:
        load.start()
    odd = lax.axis_index("tile") % 2 == 1

    def send(at, rows):
        cell = lane_index(rows[0][0]) // SUB
        cells = LANES // SUB
        last, first = None, None
        for f in range(2):
            for r in range(SUB):
                s = f * SUB + r
                turned = roll(rows[f][r], (s + 1) * SUB)
                last = turned if last is None else jnp.where(cell == s, turned, last)
                first = turned if first is None else jnp.where(cell == (s + 1) % cells, turned, first)
        first = roll(first, -SUB)
        last_out[at, :] = last
        first_out[at, :] = first
        half = cell % SUB < STEPS
        to_above = jnp.where(half, last, roll(first, STEPS * SUB))
        to_below = jnp.where(half, roll(last, -STEPS * SUB), first)
        near[0, at, :] = pick(odd, to_above, to_below)
        far[0, at, :] = pick(odd, to_below, to_above)
        for f in range(2):
            count = STEPS - f
            for j in range(count):
                top, bottom = rows[f][j], rows[f][SUB - count + j]
                row = f * STEPS + j
                near[1 + row, at, :] = pick(odd, top, bottom)
                if row < EARLY_ROWS:
                    far[1 + row, at, :] = pick(odd, bottom, top)
                else:
                    far_late[row - EARLY_ROWS, at, :] = pick(odd, bottom, top)

    for g, load in enumerate(loads):
        load.wait()
        send(pl.ds(g * height, height), own_rows(tangents, g, height))
    small.wait()
    send(pl.ds(fields, SUB), own_coeffs(coeffs))


def row_mirror_kernel(last, first, mirrored):
    tile, tiles = lax.axis_index("tile"), lax.axis_size("tile")

    @pl.when((tile == 0) | (tile == tiles - 1))
    def _():
        for i, ref in enumerate((last, first)):
            own = ref[...]
            cell = lane_index(own) // SUB % SUB
            turned = roll(own, -7 * SUB)
            for s in range(1, SUB):
                turned = jnp.where(cell == s, roll(own, (2 * s - 7) * SUB), turned)
            mirrored[i] = turned

    @pl.when((tile != 0) & (tile != tiles - 1))
    def _():
        mirrored[...] = jnp.zeros(mirrored.shape, jnp.float32)


def column_kernel(last, first, mirrored, near, far, strips, near_out, far_out):
    tile, tiles = lax.axis_index("tile"), lax.axis_size("tile")
    odd, at_top, at_bottom = tile % 2 == 1, tile == 0, tile == tiles - 1
    grp_odd = lax.axis_index("grp") % 2 == 1
    one, two = near[0], far[0]
    lane = lane_index(one)
    cell, low, inner = lane // SUB % SUB, lane < LANES // 2, lane % SUB < STEPS
    half = cell < STEPS
    above, below = pick(odd, one, two), pick(odd, two, one)
    outside = (half & at_bottom) | (~half & at_top)
    received = (jnp.where(half, below, roll(above, STEPS * SUB)), jnp.where(half, roll(below, -STEPS * SUB), above))
    sides = []
    for i, ref in enumerate((last, first)):
        own, more = ref[...], jnp.where(outside, mirrored[i], received[i])
        fast = jnp.where(low, own, roll(more, LANES // 2))
        slow = jnp.where(low, roll(own, LANES // 2), more)
        strips[2 * i] = fast
        strips[2 * i + 1] = slow
        sides.append((fast, slow))
    to_left = jnp.where(inner, sides[1][0], roll(sides[1][1], STEPS))
    to_right = jnp.where(inner, roll(sides[0][0], -STEPS), sides[0][1])
    near_out[...] = pick(grp_odd, to_left, to_right)
    far_out[...] = pick(grp_odd, to_right, to_left)


def strip_neighbours(last, first, halo, wanted):
    c = lane_index(last) % SUB
    end, begin = c == SUB - 1, c == 0
    out = []
    sides = (lambda: (last, roll(halo, 7), None), lambda: (first, None, roll(halo, -7)), lambda: (halo, roll(first, 7), roll(last, -7)))
    for side in sides[:wanted]:
        x, after, before = side()
        right, left = roll(x, -1), roll(x, 1)
        if after is not None:
            right = jnp.where(end, after, right)
        if before is not None:
            left = jnp.where(begin, before, left)
        out.append(roll(x, SUB) + roll(x, -SUB) + right + left)
    return out


def advance(fast, slow, around, gain, cross):
    return gain * fast + diffusion * around + cross * slow


def relax(fast, slow):
    return (1.0 - slow_rate) * slow + slow_rate * fast


def column_mirror_kernel(strips, mirrored):
    grp, grps = lax.axis_index("grp"), lax.axis_size("grp")

    @pl.when((grp == 0) | (grp == grps - 1))
    def _():
        for f in range(2):
            tail, start = strips[f], strips[2 + f]
            c = lane_index(tail) % SUB
            turned = roll(tail, -7)
            for s in range(STEPS):
                turned = jnp.where(c == s, roll(tail, 2 * s - 7), turned)
                turned = jnp.where(c == 7 - s, roll(start, 7 - 2 * s), turned)
            mirrored[f] = turned

    @pl.when((grp != 0) & (grp != grps - 1))
    def _():
        mirrored[...] = jnp.zeros(mirrored.shape, jnp.float32)


def gram_kernel(fields, height, middle_gram, strips, mirrored, near, far, packed, gram, halo, ends):
    grp, grps = lax.axis_index("grp"), lax.axis_size("grp")
    grp_odd = grp % 2 == 1
    one, two = near[...], far[...]
    lane = lane_index(one)
    c = lane % SUB
    inner = c < STEPS
    left, right = pick(grp_odd, one, two), pick(grp_odd, two, one)
    outside = (inner & (grp == grps - 1)) | (~inner & (grp == 0))
    halo[0] = jnp.where(outside, mirrored[0], jnp.where(inner, right, roll(left, STEPS)))
    halo[1] = jnp.where(outside, mirrored[1], jnp.where(inner, roll(right, -STEPS), left))

    def parts(f, at):
        return [strips[f, at, :], strips[2 + f, at, :], halo[f, at, :]]

    gains = [tall(x + (1.0 - 4.0 * diffusion), height) for x in parts(0, pl.ds(fields, SUB))]
    crosses = [tall(x, height) for x in parts(1, pl.ds(fields, SUB))]
    places = [pl.ds(at, height) for at in range(0, fields, height)]
    held = [(parts(0, at), parts(1, at)) for at in places]
    for step in range(STEPS):
        wanted = 3 if step + 1 < STEPS else 2
        for i, (fast, slow) in enumerate(held):
            around = strip_neighbours(*fast, wanted)
            moved = [advance(fast[p], slow[p], around[p], gains[p], crosses[p]) for p in range(wanted)]
            held[i] = (moved, [relax(fast[p], slow[p]) for p in range(wanted)])
    for at, pair in zip(places, held):
        l = lane_index(pair[0][0])
        joined = [jnp.where(l % SUB < STEPS, side[1], side[0]) for side in pair]
        ends[at, :] = jnp.where(l < LANES // 2, joined[0], roll(joined[1], LANES // 2))

    whole = middle_gram[...] + dot_nt(ends[...], ends[...])
    gram[...] = whole
    packed[...] = pack_blocks(whole, fields // SIDE)


def extended_rows(own, near, far, far_late, at):
    tile, tiles = lax.axis_index("tile"), lax.axis_size("tile")
    odd, at_top, at_bottom = tile % 2 == 1, tile == 0, tile == tiles - 1
    out = []
    for f in range(2):
        count = STEPS - f
        rows = dict(enumerate(own[f]))
        for j in range(count):
            row = f * STEPS + j
            one = near[1 + row, at, :]
            two = far[1 + row, at, :] if row < EARLY_ROWS else far_late[row - EARLY_ROWS, at, :]
            rows[j - count] = pick(at_top, own[f][count - 1 - j], pick(odd, one, two))
            rows[SUB + j] = pick(at_bottom, own[f][SUB - 1 - j], pick(odd, two, one))
        out.append(rows)
    return out


def evolve_kernel(fields, height, tangents, coeffs, near, far, far_late, middle_gram, row_coeffs, cells):
    coeff_rows = extended_rows(own_coeffs(coeffs), near, far, far_late, pl.ds(fields, SUB))
    for f in range(2):
        for r in range(1 - STEPS, SUB + STEPS - 1):
            row_coeffs[f, r + STEPS - 1, :, :] = coeff_rows[f][r] + (1.0 - 4.0 * diffusion) * (1 - f)

    for g in range(fields // height):
        at = chunk(g, height)
        fast, slow = extended_rows(own_rows(tangents, g, height), near, far, far_late, at)
        for step in range(1, STEPS + 1):
            margin = STEPS - step
            new_fast = {}
            for r in range(-margin, SUB + margin):
                around = fast[r - 1] + fast[r + 1] + roll(fast[r], 1) + roll(fast[r], -1)
                gain, cross = (tall(row_coeffs[f, r + STEPS - 1], height) for f in range(2))
                new_fast[r] = advance(fast[r], slow[r], around, gain, cross)
            keep = max(margin - 1, 0)
            slow = {r: relax(fast[r], slow[r]) for r in range(-keep, SUB + keep)}
            fast = new_fast
        lane = lane_index(fast[0])
        middle = (lane >= STEPS) & (lane < LANES - STEPS)
        for f, rows in enumerate((fast, slow)):
            for r in range(SUB):
                cells[at, (f * SUB + r) * LANES:(f * SUB + r + 1) * LANES] = jnp.where(middle, rows[r], 0.0)

    middle_gram[...] = gram_of(cells[...])


def local_call(body, name, out_shapes, scratch, *args, hbm=False, vmem=VMEM_BYTES, cost=None):
    spec = pl.BlockSpec(memory_space=pltpu.VMEM)
    return pl.pallas_call(
        body,
        out_shape=[jax.ShapeDtypeStruct(s, jnp.float32) for s in out_shapes],
        in_specs=[pl.BlockSpec(memory_space=pltpu.HBM) if hbm else spec] * len(args),
        out_specs=[spec] * len(out_shapes),
        scratch_shapes=[pltpu.VMEM(s, jnp.float32) if isinstance(s, tuple) else s for s in scratch],
        compiler_params=pltpu.CompilerParams(vmem_limit_bytes=vmem),
        name=name,
        cost_estimate=cost,
    )(*args)


def swap(cells, axis, first, close=False):
    count = lax.axis_size(axis)
    pairs = [(i, i + 1) for i in range(first, count - 1, 2)]
    if close and first:
        pairs.append((0, count - 1))
    return lax.ppermute(cells, axis, pairs + [(b, a) for a, b in pairs])


def exchange(cells, grp_bit, tile_bit):
    grps, tiles = lax.axis_size("grp"), lax.axis_size("tile")
    moves = [(g * tiles + t, (g ^ grp_bit) * tiles + (t ^ tile_bit)) for g in range(grps) for t in range(tiles)]
    return lax.ppermute(cells, ("grp", "tile"), moves)


def parity():
    bits = lax.axis_index("grp") ^ lax.axis_index("tile")
    shift = 1
    while shift < max(lax.axis_size("grp"), lax.axis_size("tile")):
        bits = bits ^ (bits >> shift)
        shift *= 2
    return (bits & 1) == 1


def sum_blocks(packed, beside):
    half = packed.shape[0] // 2
    high_half = parity()
    low, high = packed[:half], packed[half:]
    part = jnp.where(high_half, high, low) + exchange(jnp.where(high_half, low, high), 0, 1)
    for axis in ("tile", "grp"):
        bit = 1 if axis == "grp" else 2
        while bit < lax.axis_size(axis):
            if axis == "grp" and 2 * bit >= lax.axis_size(axis):
                part, beside = lax.optimization_barrier((part, beside))
            part = part + (exchange(part, bit, 1) if axis == "grp" else exchange(part, 0, bit + 1))
            bit *= 2
    return part, exchange(part, 0, 1), beside


def per_device(tangents, reaction_self, reaction_cross):
    fields = tangents.shape[1]
    padded = fields + SUB
    rows = tangents.reshape(2, fields * tangents.shape[2], tangents.shape[3])
    strip = (padded, LANES)
    early, late = (1 + EARLY_ROWS,) + strip, (2 * STEPS - 1 - EARLY_ROWS,) + strip
    inputs = (rows, jnp.stack([reaction_self, reaction_cross]))
    last, first, near, far, far_late = local_call(
        functools.partial(edge_kernel, fields, HEIGHT_EDGE), "edges", [strip] * 2 + [(2 * STEPS, padded, LANES), early, late],
        [a.shape for a in inputs] + [pltpu.SemaphoreType.DMA((fields // HEIGHT_EDGE + 1,))], *inputs,
        hbm=True, vmem=EDGE_VMEM_BYTES,
    )
    near, far, far_late = swap(near, "tile", 0), swap(far, "tile", 1), swap(far_late, "tile", 1)
    (row_mirror,) = local_call(row_mirror_kernel, "row_mirror", [(2,) + strip], [], last, first)
    strips, near_cols, far_cols = local_call(
        column_kernel, "columns", [(4,) + strip, strip, strip], [], last, first, row_mirror, near, far
    )
    (column_mirror,) = local_call(column_mirror_kernel, "column_mirror", [(2,) + strip], [], strips)
    far_cols = swap(far_cols, "grp", 1, close=True)
    near_cols = swap(near_cols, "grp", 0)
    (middle_gram,) = local_call(
        functools.partial(evolve_kernel, fields, HEIGHT_EVOLVE), "evolve", [(fields, fields)],
        [(2, SUB + 2 * STEPS - 2, SUB, LANES), (fields, 2 * SUB * LANES)], *inputs, near, far, far_late,
    )
    side_blocks = fields // SIDE
    packed, gram = local_call(
        functools.partial(gram_kernel, fields, HEIGHT_STRIP), "gram", [(packed_rows(side_blocks), 2 * SIDE), (fields, fields)],
        [(2,) + strip, (fields, LANES)], middle_gram, strips, column_mirror, near_cols, far_cols,
    )
    block_total = lax.axis_size("grp") * lax.axis_size("tile")
    corrections, growth = factor_call(*sum_blocks(packed, local_factor(gram, side_blocks)), fields, math.sqrt(block_total))
    return (corrections, growth)


def solution(mesh):
    in_specs = (P(None, None, "tile", "grp"), P("tile", "grp"), P("tile", "grp"))
    out_specs = (P(("grp", "tile"), None), P())
    return jax.shard_map(
        per_device, mesh=mesh, in_specs=in_specs, out_specs=out_specs, check_vma=False
    )
```
